32 devices in a mesh: fsdp: 32 (over z, y, x, core).
Axes of the slice: x: 2, y: 2, z: 4, core: 2. Of those that a mesh axis runs over, the one named last changes fastest.
Arguments:
- tokens: bfloat16 [64, 128, 1024], P('fsdp'), may hold values from -6 to 6
- segment_ids: int32 [64, 128], P('fsdp'), may hold values from 0 to 3, never falling along the last dimension, each value on 1 to 64 neighbouring positions
- variate_ids: int32 [64, 128], P('fsdp'), may hold values from 0 to 3
- time_ids: int32 [64, 128], P('fsdp'), may hold values from 0 to 127
- w_query: bfloat16 [1024, 1024], P('fsdp'), may hold values from -0.1875 to 0.1875
- w_key: bfloat16 [1024, 1024], P('fsdp'), may hold values from -0.1875 to 0.1875
- w_value: bfloat16 [1024, 1024], P('fsdp'), may hold values from -0.1875 to 0.1875
- w_out: bfloat16 [1024, 1024], P('fsdp'), may hold values from -0.5 to 0.5
- w_gate: bfloat16 [1024, 4096], P('fsdp'), may hold values from -0.1875 to 0.1875
- w_up: bfloat16 [1024, 4096], P('fsdp'), may hold values from -0.1875 to 0.1875
- w_down: bfloat16 [4096, 1024], P('fsdp'), may hold values from -0.09375 to 0.09375
- gain_attn: bfloat16 [1024], P('fsdp'), may hold values from 0.5 to 1.5
- gain_ffn: bfloat16 [1024], P('fsdp'), may hold values from 0.5 to 1.5
- gain_query: bfloat16 [64], replicated, may hold values from 0.099609375 to 1.8984375
- gain_key: bfloat16 [64], replicated, may hold values from 0.099609375 to 1.8984375
- variate_bias: bfloat16 [2, 16], replicated, may hold values from -3 to 3
- cotangent: bfloat16 [64, 128, 1024], P('fsdp'), may hold values from -6 to 6
Outputs:
- activations: bfloat16 [64, 128, 1024], P('fsdp')
- input_grad: bfloat16 [64, 128, 1024], P('fsdp')
- grad_query: float32 [1024, 1024], P('fsdp')
- grad_key: float32 [1024, 1024], P('fsdp')
- grad_value: float32 [1024, 1024], P('fsdp')
- grad_out: float32 [1024, 1024], P('fsdp')
- grad_gate: float32 [1024, 4096], P('fsdp')
- grad_up: float32 [1024, 4096], P('fsdp')
- grad_down: float32 [4096, 1024], P('fsdp')
- grad_gain_attn: float32 [1024], P('fsdp')
- grad_gain_ffn: float32 [1024], P('fsdp')
- grad_gain_query: float32 [64], replicated
- grad_gain_key: float32 [64], replicated
- grad_variate_bias: float32 [2, 16], replicated
The draws below stay inside these ranges and needn't reach their ends.
Inputs may be any that keep to these rules, and one draw needn't show every extreme that they name: `segment_ids`: 0 marks padding; each other value is one document; values never fall along a sequence.
All inputs are finite; a program needn't handle non-finite values.
Results may differ from the reference program's by a relative error of at most 0.014.
The reference program's roundings to bfloat16 on the way count: a program that leaves them out, or rounds other values in their place, can miss the bound.
Values may be sent and summed in bfloat16 or wider, within the bound.
A program may use at most 384 MiB of HBM per device.

```python
import math
import jax
import jax.numpy as jnp
import numpy as np
from jax import lax

D = 1024
HEADS = 16
HEAD_SIZE = 64
FF = 4096
SEQ = 128
SEQS = 64


def place_ends(entries, rng, least, top_value):
    spot = [jax.random.randint(jax.random.fold_in(rng, axis), (), 0, length) for axis, length in enumerate(entries.shape)]
    widest = entries.shape.index(max(entries.shape))
    neighbour = spot[:widest] + [(spot[widest] + 1) % entries.shape[widest]] + spot[widest + 1:]
    return entries.at[tuple(spot)].set(least).at[tuple(neighbour)].set(top_value)


def with_spikes(entries, own_key, source, target, shards_of, factor):
    def block_of(axis_at):
        return (jnp.arange(entries.shape[axis_at]) // (entries.shape[axis_at] // shards_of)).reshape((-1,) + (1,) * (entries.ndim - 1 - axis_at))

    first = jax.random.permutation(own_key, shards_of)[block_of(target)]
    second = (block_of(target) + shards_of // 2) % shards_of
    return jnp.where((block_of(source) == first) | (block_of(source) == second), factor * entries, entries)


def levels(key, dims, shards, low, top_value):
    level, own = 1.0, jax.random.fold_in(key, 6)
    for dim, shards_of in shards:
        steps = jnp.exp(jax.random.uniform(jax.random.fold_in(own, dim), (shards_of,), jnp.float32, low / len(shards), top_value / len(shards)))
        level = level * jnp.repeat(steps, dims[dim] // shards_of).reshape([-1 if axis == dim else 1 for axis in range(len(dims))])
    return level


def length_profile(number_of, total, most, skew):
    loads = [(1 << 20) // math.isqrt(rank ** skew) + 1 for rank in range(2, number_of + 1)]
    rest, counts = total - most - (number_of - 1), [1] * (number_of - 1)
    while rest > 0:
        candidates = [i for i in range(number_of - 1) if counts[i] < most]
        mass, budget = sum([loads[i] for i in candidates]), rest
        for i in candidates:
            addition = min(most - counts[i], max(1, budget * loads[i] // mass), rest)
            counts[i] = counts[i] + addition
            rest = rest - addition
    return np.array([most] + counts)


def uneven(stream_key, number_of, total, reach, lean):
    if number_of == 2:
        one = jax.random.randint(stream_key, (), max(1, total - reach), min(reach, total - 1) + 1)
        return jnp.stack([one, total - one])
    tallies = jnp.asarray(length_profile(number_of, total, reach, lean), jnp.int32)
    pairs = (number_of - 1) // 2
    source_of, receiver = tallies[1:1 + 2 * pairs:2], tallies[2:2 + 2 * pairs:2]
    slack = jnp.minimum(source_of - 1, reach - receiver)
    passed = jax.random.randint(jax.random.fold_in(stream_key, 1), (pairs,), 0, 1 << 20) % (slack + 1)
    tallies = tallies.at[1:1 + 2 * pairs:2].set(source_of - passed).at[2:2 + 2 * pairs:2].set(receiver + passed)
    return tallies[jax.random.permutation(jax.random.fold_in(stream_key, 2), number_of)]


def normal_values(rng, extent, deviation, bound, shards=(), kind=jnp.bfloat16):
    drawn = deviation * jax.random.normal(rng, extent, jnp.float32)
    if shards:
        drawn = drawn * levels(rng, extent, shards, -0.22, 0.18)
    return jnp.clip(drawn, -bound, bound).astype(kind)


def noise_with(key, extent, deviation, reach, pieces, heavy, kind=jnp.bfloat16):
    values = deviation * jax.random.normal(key, extent, jnp.float32)
    if pieces:
        values = values * levels(key, extent, pieces, -0.22, 0.18)
    return jnp.clip(with_spikes(values, jax.random.fold_in(key, 3), *heavy), -reach, reach).astype(kind)


def setup_inputs(seed: int = 0) -> dict:
    key_of = jax.random.split(jax.random.key(seed), 18)
    tokens = normal_values(key_of[0], (SEQS, SEQ, D), 1.0, 6.0, ((0, 32),))
    segment_ids = jax.vmap(lambda own: jnp.searchsorted(jnp.cumsum(uneven(own, max(4, SEQ // 32), SEQ, SEQ // 2, 2)), jnp.arange(SEQ), side="right"))(jax.random.split(key_of[1], SEQS)).reshape((SEQS, SEQ)).astype(jnp.int32)
    variate_ids = place_ends(jax.random.randint(key_of[2], (SEQS, SEQ), 0, 4), jax.random.fold_in(key_of[2], 1), 0, 3).astype(jnp.int32)
    time_ids = place_ends(jax.random.randint(key_of[3], (SEQS, SEQ), 0, SEQ), jax.random.fold_in(key_of[3], 1), 0, SEQ - 1).astype(jnp.int32)
    w_query = normal_values(key_of[4], (D, D), D ** -0.5, 0.1875, ((0, 32),))
    w_key = normal_values(key_of[5], (D, D), D ** -0.5, 0.1875, ((0, 32),))
    w_value = normal_values(key_of[6], (D, D), D ** -0.5, 0.1875, ((0, 32),))
    w_out = normal_values(key_of[7], (D, D), (D // 8) ** -0.5, 0.5, ((0, 32),))
    w_gate = normal_values(key_of[8], (D, FF), D ** -0.5, 0.1875, ((0, 32),))
    w_up = normal_values(key_of[9], (D, FF), D ** -0.5, 0.1875, ((0, 32),))
    w_down = normal_values(key_of[10], (FF, D), FF ** -0.5, 0.09375, ((0, 32),))
    gain_attn = jnp.clip(1.0 + 0.1 * jax.random.normal(key_of[11], (D,), jnp.float32), 0.5, 1.5).astype(jnp.bfloat16)
    gain_ffn = jnp.clip(1.0 + 0.1 * jax.random.normal(key_of[12], (D,), jnp.float32), 0.5, 1.5).astype(jnp.bfloat16)
    gain_query = jnp.clip(1.0 + 0.18 * jax.random.normal(key_of[13], (HEAD_SIZE,), jnp.float32), 0.099609375, 1.8984375).astype(jnp.bfloat16)
    gain_key = jnp.clip(1.0 + 0.18 * jax.random.normal(key_of[14], (HEAD_SIZE,), jnp.float32), 0.099609375, 1.8984375).astype(jnp.bfloat16)
    variate_bias = normal_values(key_of[15], (2, HEADS), 1.0, 3.0)
    cotangent = noise_with(key_of[16], (SEQS, SEQ, D), 1.0, 6.0, ((0, 32),), (0, 2, 32, 2.75))
    return dict(tokens=tokens, segment_ids=segment_ids, variate_ids=variate_ids, time_ids=time_ids, w_query=w_query, w_key=w_key, w_value=w_value, w_out=w_out, w_gate=w_gate, w_up=w_up, w_down=w_down, gain_attn=gain_attn, gain_ffn=gain_ffn, gain_query=gain_query, gain_key=gain_key, variate_bias=variate_bias, cotangent=cotangent)


EPSILON = 1e-05
highest = lax.Precision.HIGHEST

@jax.custom_vjp
def low(v):
    return lax.optimization_barrier(v.astype(jnp.bfloat16)).astype(jnp.float32)

@jax.custom_vjp
def low_back(v):
    return v

def low_keep(v):
    return (low(v), None)

def low_pass(kept, grad):
    return (grad,)

def back_keep(v):
    return (v, None)

def back_low(kept, grad):
    return (low(grad),)
low.defvjp(low_keep, low_pass)
low_back.defvjp(back_keep, back_low)

def normalize(values, scale_gain):
    return values * lax.rsqrt(lax.optimization_barrier(jnp.mean(values * values, axis=-1, keepdims=True)) + EPSILON) * scale_gain

def rotate(values, moments):
    halfway = values.shape[-1] // 2
    frequency = jnp.exp(-math.log(10000.0) * jnp.arange(halfway).astype(jnp.float32) / halfway)
    angles = moments.astype(jnp.float32)[:, None] * frequency[None, :]
    cosine = jnp.cos(angles)[:, None, :]
    sine_part = jnp.sin(angles)[:, None, :]
    former = values[..., :halfway]
    latter = values[..., halfway:]
    return jnp.concatenate([former * cosine - latter * sine_part, former * sine_part + latter * cosine], axis=-1)

def prepare(raw_heads, head_gain, moments, factor):
    return rotate(normalize(raw_heads, head_gain), moments) * factor

def attention_masks(segments, variates):
    length = segments.shape[0]
    diagonal = jnp.arange(length)[:, None] == jnp.arange(length)[None, :]
    allowed = (segments[:, None] == segments[None, :]) & ((segments[None, :] != 0) | diagonal)
    same_var = variates[:, None] == variates[None, :]
    return (allowed, same_var)

def pair_bias(bias_table, same_var):
    return jnp.where(same_var[None], bias_table[1][:, None, None], bias_table[0][:, None, None])

def matmul(left, right):
    return jnp.dot(left, right, precision=highest)

def block_layer(inputs, params, segments, variates, moments):
    w_query, w_key, w_value, w_out, w_gate, w_up, w_down, gain_attn, gain_ffn, gain_query, gain_key, bias_table = params
    length, model_width = inputs.shape
    head_count = bias_table.shape[1]
    head_dim = gain_query.shape[0]
    factor = head_dim ** (-0.5)
    normed = low(normalize(inputs, gain_attn))
    queries = low_back(matmul(normed, w_query)).reshape(length, head_count, head_dim)
    key_raw = low_back(matmul(normed, w_key)).reshape(length, head_count, head_dim)
    values = low_back(matmul(normed, w_value)).reshape(length, head_count, head_dim)
    q_rot = low(prepare(queries, gain_query, moments, factor))
    k_rot = low(prepare(key_raw, gain_key, moments, 1.0))
    v_low = low(values)
    allowed, same_var = attention_masks(segments, variates)
    scores = jnp.einsum('qhe,khe->hqk', q_rot, k_rot, precision=highest) + pair_bias(bias_table, same_var)
    scores = jnp.where(allowed[None], low_back(scores), -1000000000.0)
    maximum = lax.optimization_barrier(jnp.max(scores, axis=-1, keepdims=True))
    exponent = jnp.exp(scores - maximum)
    softmax_probs = exponent / lax.optimization_barrier(jnp.sum(exponent, axis=-1, keepdims=True))
    attended = jnp.einsum('hqk,khe->qhe', low(softmax_probs), v_low, precision=highest).reshape(length, model_width)
    mixed_state = inputs + low_back(matmul(low(low_back(attended)), w_out))
    normed_ffn = low(normalize(mixed_state, gain_ffn))
    gate_act = low_back(matmul(normed_ffn, w_gate))
    up_act = low_back(matmul(normed_ffn, w_up))
    hidden = low(jax.nn.silu(gate_act) * up_act)
    return mixed_state + low_back(matmul(hidden, w_down))

def reference(tokens, segment_ids, variate_ids, time_ids, w_query, w_key, w_value, w_out, w_gate, w_up, w_down, gain_attn, gain_ffn, gain_query, gain_key, variate_bias, cotangent):
    params = tuple((weight.astype(jnp.float32) for weight in (w_query, w_key, w_value, w_out, w_gate, w_up, w_down, gain_attn, gain_ffn, gain_query, gain_key, variate_bias)))

    def one_sequence(totals, sequence_item):
        inputs, segments, variates, moments, upstream = sequence_item

        def apply_layer(inputs_float, *weights):
            return block_layer(inputs_float, weights, segments, variates, moments)
        result, pullback = jax.vjp(apply_layer, inputs.astype(jnp.float32), *params)
        gradients = pullback(upstream.astype(jnp.float32))
        totals = tuple((running + fresh for running, fresh in zip(totals, gradients[1:])))
        return (totals, (result.astype(jnp.bfloat16), gradients[0].astype(jnp.bfloat16)))
    initial = tuple((jnp.zeros(weight.shape, jnp.float32) for weight in params))
    totals, (outputs, input_grad) = lax.scan(one_sequence, initial, (tokens, segment_ids, variate_ids, time_ids, cotangent))
    return (outputs, input_grad, totals[0], totals[1], totals[2], totals[3], totals[4], totals[5], totals[6], totals[7], totals[8], totals[9], totals[10], totals[11])
```

```python
import functools
import math

import jax
import jax.numpy as jnp
from jax import lax
from jax.experimental import pallas as pl
from jax.experimental.pallas import tpu as pltpu
from jax.sharding import PartitionSpec as P

EPSILON = 1e-05


def normalize(values, scale_gain):
    return (
        values * lax.rsqrt(jnp.mean(values * values, axis=-1, keepdims=True) + EPSILON) * scale_gain
    )


def rotate(values, moments):
    halfway = values.shape[-1] // 2
    frequency = jnp.exp(-math.log(10000.0) * jnp.arange(halfway).astype(jnp.float32) / halfway)
    angles = moments.astype(jnp.float32)[:, None] * frequency[None, :]
    cosine = jnp.cos(angles)[:, None, :]
    sine_part = jnp.sin(angles)[:, None, :]
    former = values[..., :halfway]
    latter = values[..., halfway:]
    return jnp.concatenate(
        [former * cosine - latter * sine_part, former * sine_part + latter * cosine], axis=-1
    )


def prepare(raw_heads, head_gain, moments, factor):
    return rotate(normalize(raw_heads, head_gain), moments) * factor


def swiglu(gate_act, up_act):
    return jax.nn.silu(gate_act) * up_act


def attention_masks(segments, variates):
    length = segments.shape[0]
    diagonal = jnp.arange(length)[:, None] == jnp.arange(length)[None, :]
    allowed = (segments[:, None] == segments[None, :]) & ((segments[None, :] != 0) | diagonal)
    same_var = variates[:, None] == variates[None, :]
    return (allowed, same_var)


def scoring(q_rot, k_rot, bias_table, allowed, same_var):
    scores = jnp.einsum("qhe,khe->hqk", q_rot, k_rot, preferred_element_type=jnp.float32)
    scores = scores + jnp.where(
        same_var[None], bias_table[1][:, None, None], bias_table[0][:, None, None]
    )
    return jnp.where(allowed[None], scores, -1000000000.0)


def project(left, right):
    return jnp.dot(left, right, preferred_element_type=jnp.float32)


def across(left, right):
    return lax.dot_general(
        left, right, (((0,), (0,)), ((), ())), preferred_element_type=jnp.float32
    )


def against(left, weight):
    return lax.dot_general(
        left, weight, (((1,), (1,)), ((), ())), preferred_element_type=jnp.float32
    )


def forward(inputs_low, weights, side_params, segments, variates, moments):
    w_query, w_key, w_value, w_out, w_gate, w_up, w_down, gain_attn, gain_ffn = weights
    gain_query, gain_key, bias_table = side_params
    length, model_width = inputs_low.shape
    head_count = bias_table.shape[1]
    head_dim = gain_query.shape[0]
    inputs = inputs_low.astype(jnp.float32)
    normed = normalize(inputs, gain_attn.astype(jnp.float32)).astype(jnp.bfloat16)
    queries = project(normed, w_query).reshape(length, head_count, head_dim)
    key_raw = project(normed, w_key).reshape(length, head_count, head_dim)
    v_low = project(normed, w_value).reshape(length, head_count, head_dim).astype(jnp.bfloat16)
    q_rot = prepare(queries, gain_query, moments, head_dim ** (-0.5)).astype(jnp.bfloat16)
    k_rot = prepare(key_raw, gain_key, moments, 1.0).astype(jnp.bfloat16)
    allowed, same_var = attention_masks(segments, variates)
    scores = scoring(q_rot, k_rot, bias_table, allowed, same_var)
    maximum = jnp.max(scores, axis=-1, keepdims=True)
    exponent = jnp.exp(scores - maximum)
    row_total = jnp.sum(exponent, axis=-1, keepdims=True)
    log_total = maximum + jnp.log(row_total)
    softmax_probs = (exponent / row_total).astype(jnp.bfloat16)
    attended = jnp.einsum("hqk,khe->qhe", softmax_probs, v_low, preferred_element_type=jnp.float32)
    attended = attended.reshape(length, model_width).astype(jnp.bfloat16)
    mixed_state = inputs + project(attended, w_out)
    normed_ffn = normalize(mixed_state, gain_ffn.astype(jnp.float32)).astype(jnp.bfloat16)
    gate_act = project(normed_ffn, w_gate)
    up_act = project(normed_ffn, w_up)
    hidden = swiglu(gate_act, up_act).astype(jnp.bfloat16)
    result = mixed_state + project(hidden, w_down)
    kept_state = (
        inputs,
        normed,
        queries,
        key_raw,
        q_rot,
        k_rot,
        v_low,
        log_total,
        attended,
        mixed_state,
        normed_ffn,
        gate_act,
        up_act,
        hidden,
    )
    return (result, kept_state)


def backward(upstream, kept_state, weights, side_params, segments, variates, moments):
    (
        inputs,
        normed,
        queries,
        key_raw,
        q_rot,
        k_rot,
        v_low,
        log_total,
        attended,
        mixed_state,
        normed_ffn,
        gate_act,
        up_act,
        hidden,
    ) = kept_state
    w_query, w_key, w_value, w_out, w_gate, w_up, w_down, gain_attn, gain_ffn = weights
    gain_query, gain_key, bias_table = side_params
    length, head_count, head_dim = queries.shape
    grad_down = across(hidden, upstream)
    d_hidden = against(upstream, w_down)
    _, pullback = jax.vjp(swiglu, gate_act, up_act)
    d_gate, d_up = pullback(d_hidden)
    d_gate = d_gate.astype(jnp.bfloat16)
    d_up = d_up.astype(jnp.bfloat16)
    grad_gate = across(normed_ffn, d_gate)
    grad_up = across(normed_ffn, d_up)
    d_normed_ffn = against(d_gate, w_gate) + against(d_up, w_up)
    _, pullback = jax.vjp(normalize, mixed_state, gain_ffn.astype(jnp.float32))
    d_mixed, grad_gain_ffn = pullback(d_normed_ffn)
    d_mixed = d_mixed + upstream.astype(jnp.float32)
    d_branch = d_mixed.astype(jnp.bfloat16)
    grad_out = across(attended, d_branch)
    d_attended = against(d_branch, w_out).astype(jnp.bfloat16).reshape(length, head_count, head_dim)
    allowed, same_var = attention_masks(segments, variates)
    scores = scoring(q_rot, k_rot, bias_table, allowed, same_var)
    softmax_probs = jnp.exp(scores - log_total)
    d_probs = jnp.einsum("qhe,khe->hqk", d_attended, v_low, preferred_element_type=jnp.float32)
    d_values = jnp.einsum(
        "hqk,qhe->khe",
        softmax_probs.astype(jnp.bfloat16),
        d_attended,
        preferred_element_type=jnp.float32,
    )
    d_values = d_values.reshape(length, head_count * head_dim).astype(jnp.bfloat16)
    weighted = jnp.sum(softmax_probs * d_probs, axis=-1, keepdims=True)
    d_scores = (softmax_probs * (d_probs - weighted)).astype(jnp.bfloat16)
    d_float = d_scores.astype(jnp.float32)
    same_sum = jnp.sum(jnp.where(same_var[None], d_float, 0.0), axis=(1, 2))
    other_sum = jnp.sum(jnp.where(same_var[None], 0.0, d_float), axis=(1, 2))
    grad_bias = jnp.stack([other_sum, same_sum])
    d_qrot = jnp.einsum("hqk,khe->qhe", d_scores, k_rot, preferred_element_type=jnp.float32)
    d_krot = jnp.einsum("hqk,qhe->khe", d_scores, q_rot, preferred_element_type=jnp.float32)
    factor = head_dim ** (-0.5)
    _, pullback = jax.vjp(
        lambda raw_heads, head_gain: prepare(raw_heads, head_gain, moments, factor),
        queries,
        gain_query,
    )
    d_queries, grad_gain_query = pullback(d_qrot)
    _, pullback = jax.vjp(
        lambda raw_heads, head_gain: prepare(raw_heads, head_gain, moments, 1.0), key_raw, gain_key
    )
    d_keys, grad_gain_key = pullback(d_krot)
    d_queries = d_queries.reshape(length, head_count * head_dim).astype(jnp.bfloat16)
    d_keys = d_keys.reshape(length, head_count * head_dim).astype(jnp.bfloat16)
    grad_query = across(normed, d_queries)
    grad_key = across(normed, d_keys)
    grad_value = across(normed, d_values)
    d_normed = against(d_queries, w_query) + against(d_keys, w_key) + against(d_values, w_value)
    _, pullback = jax.vjp(normalize, inputs, gain_attn.astype(jnp.float32))
    d_inputs, grad_gain_attn = pullback(d_normed)
    row_grads = jnp.concatenate(
        [grad_query, grad_key, grad_value, grad_out, grad_gate, grad_up], axis=1
    )
    small = (grad_gain_query, grad_gain_key, grad_bias, grad_gain_attn, grad_gain_ffn)
    return (d_inputs + d_mixed, row_grads, grad_down, small)


def plain(
    tokens,
    segment_ids,
    variate_ids,
    time_ids,
    w_query,
    w_key,
    w_value,
    w_out,
    w_gate,
    w_up,
    w_down,
    gain_attn,
    gain_ffn,
    gain_query,
    gain_key,
    variate_bias,
    cotangent,
):
    devices = lax.axis_size("fsdp")
    owner = lax.axis_index("fsdp")
    width = w_query.shape[1]
    hidden_width = w_gate.shape[1]
    own_rows = w_query.shape[0]
    own_down = w_down.shape[0]
    side_params = (
        gain_query.astype(jnp.float32),
        gain_key.astype(jnp.float32),
        variate_bias.astype(jnp.float32),
    )
    rows_total = jnp.zeros((own_rows * devices, 4 * width + 2 * hidden_width), jnp.float32)
    down_total = jnp.zeros((own_down * devices, width), jnp.float32)
    side_totals = (
        jnp.zeros(gain_query.shape, jnp.float32),
        jnp.zeros(gain_key.shape, jnp.float32),
        jnp.zeros(variate_bias.shape, jnp.float32),
        jnp.zeros((own_rows * devices,), jnp.float32),
        jnp.zeros((own_rows * devices,), jnp.float32),
    )
    results = []
    input_grads = []
    for micro_index in range(tokens.shape[0]):
        segments = segment_ids[micro_index]
        variates = variate_ids[micro_index]
        moments = time_ids[micro_index]
        forward_weights = (
            lax.all_gather(w_query, "fsdp", axis=0, tiled=True),
            lax.all_gather(w_key, "fsdp", axis=0, tiled=True),
            lax.all_gather(w_value, "fsdp", axis=0, tiled=True),
            lax.all_gather(w_out, "fsdp", axis=0, tiled=True),
            lax.all_gather(w_gate, "fsdp", axis=0, tiled=True),
            lax.all_gather(w_up, "fsdp", axis=0, tiled=True),
            lax.all_gather(w_down, "fsdp", axis=0, tiled=True),
            lax.all_gather(gain_attn, "fsdp", axis=0, tiled=True),
            lax.all_gather(gain_ffn, "fsdp", axis=0, tiled=True),
        )
        result, kept_state = forward(
            tokens[micro_index], forward_weights, side_params, segments, variates, moments
        )
        results.append(result.astype(jnp.bfloat16))
        backward_weights = (
            lax.all_gather(w_query, "fsdp", axis=0, tiled=True),
            lax.all_gather(w_key, "fsdp", axis=0, tiled=True),
            lax.all_gather(w_value, "fsdp", axis=0, tiled=True),
            lax.all_gather(w_out, "fsdp", axis=0, tiled=True),
            lax.all_gather(w_gate, "fsdp", axis=0, tiled=True),
            lax.all_gather(w_up, "fsdp", axis=0, tiled=True),
            lax.all_gather(w_down, "fsdp", axis=0, tiled=True),
            lax.all_gather(gain_attn, "fsdp", axis=0, tiled=True),
            lax.all_gather(gain_ffn, "fsdp", axis=0, tiled=True),
        )
        d_inputs, row_grads, down_grads, small = backward(
            cotangent[micro_index],
            kept_state,
            backward_weights,
            side_params,
            segments,
            variates,
            moments,
        )
        input_grads.append(d_inputs.astype(jnp.bfloat16))
        rows_total = rows_total + row_grads
        down_total = down_total + down_grads
        side_totals = tuple((running + fresh for running, fresh in zip(side_totals, small)))
    owned_rows = lax.psum_scatter(rows_total, "fsdp", scatter_dimension=0, tiled=True)
    owned_down = lax.psum_scatter(down_total, "fsdp", scatter_dimension=0, tiled=True)
    shared = lax.psum(
        (side_totals[0], side_totals[1], side_totals[2], side_totals[3], side_totals[4]), "fsdp"
    )
    gain_attn_own = lax.dynamic_slice_in_dim(shared[3], owner * own_rows, own_rows, 0)
    gain_ffn_own = lax.dynamic_slice_in_dim(shared[4], owner * own_rows, own_rows, 0)
    grad_query = owned_rows[:, 0:width]
    grad_key = owned_rows[:, width : 2 * width]
    grad_value = owned_rows[:, 2 * width : 3 * width]
    grad_out = owned_rows[:, 3 * width : 4 * width]
    grad_gate = owned_rows[:, 4 * width : 4 * width + hidden_width]
    grad_up = owned_rows[:, 4 * width + hidden_width :]
    return (
        jnp.stack(results),
        jnp.stack(input_grads),
        grad_query,
        grad_key,
        grad_value,
        grad_out,
        grad_gate,
        grad_up,
        owned_down,
        gain_attn_own,
        gain_ffn_own,
        shared[0],
        shared[1],
        shared[2],
    )


F32 = jnp.float32
BF16 = jnp.bfloat16
MESH = pl.DeviceIdType.MESH
NT = (((1,), (1,)), ((), ()))
TN = (((0,), (0,)), ((), ()))


def mm(left, right, dims=(((1,), (0,)), ((), ()))):
    return lax.dot_general(left, right, dims, preferred_element_type=F32)


def at(start, size):
    return pl.ds(pl.multiple_of(start, size), size)


def lanes(start, size):
    return pl.ds(pl.multiple_of(start, 128), size)


def loop(count, body):
    lax.fori_loop(0, count, lambda i, carry: (body(i), carry)[1], 0)


def sizes_of(devices, tokens, w_query, w_gate, gain_query, bias):
    seqs, length, width = tokens.shape
    own_rows, hidden = w_query.shape[0], w_gate.shape[1]
    return dict(
        n=devices, S=seqs, L=length, D=width, FF=hidden, rows=own_rows, T=seqs * length,
        G=devices // 4, Z=devices // 8, QC=width // 4, FC=hidden // 4, B=4 * own_rows,
        HD=gain_query.shape[0], H=bias.shape[1],
    )


def fits(s):
    return (
        s["n"] % 8 == 0 and s["rows"] % 16 == 0 and s["L"] == 128 and s["HD"] == 64
        and s["H"] * s["HD"] == s["D"] and s["QC"] % 128 == 0 and s["FF"] == 4 * s["D"]
        and s["B"] % 128 == 0 and s["FC"] // 2 % s["B"] == 0 and s["FC"] == s["D"]
    )


def scratch_of(s):
    n, S, L, D, rows, T, G, Z, QC, FC, B = (
        s[k] for k in ("n", "S", "L", "D", "rows", "T", "G", "Z", "QC", "FC", "B")
    )
    Q = 4 * T
    vm = pltpu.VMEM
    return dict(
        WA=vm((D, 4 * QC), BF16), WB=vm((D, 2 * FC), BF16), WC=vm((FC, D), BF16), WO=vm((D, D), BF16),
        SA=vm((4, rows, 4 * QC), BF16), SB=vm((4, rows, 2 * FC), BF16),
        h1Q=vm((Q, D), BF16), dyQ=vm((Q, D), BF16), attQ=vm((Q, D), BF16), h2Q=vm((Q, D), BF16),
        qraw=vm((Q, QC), F32), kraw=vm((Q, QC), F32),
        qr=vm((Q, QC), BF16), kr=vm((Q, QC), BF16), vb=vm((Q, QC), BF16),
        PR=vm((4 * S, QC // 64, L, L), F32), CT=vm((Q, 128), F32), ST=vm((Q, 128), F32),
        x1=vm((T, D), F32), dx1=vm((T, D), F32), acc=vm((T, D), F32),
        hid=vm((Q, FC), BF16), dgdu=vm((Q, 2 * FC), BF16),
        rsS=vm((3, T, D), BF16), rsR=vm((3, 3, T, D), BF16),
        daS=vm((T, D), BF16), daR=vm((Q, QC), BF16), dattS=vm((T, D), BF16), dattR=vm((Q, QC), BF16),
        YS=vm((2, Z, B, FC), BF16), YR=vm((4, Z, B, FC), BF16), ZR=vm((4, Z - 1, B, FC), BF16),
        QS=vm((3, B, FC), BF16), QR=vm((3, 4, rows, FC), BF16),
        idq=vm((4 * S, 8, L), F32),
        GT=vm((3, 8, D), F32), GR=vm((4 + Z, 8, D), F32),
        TT=vm((3, 8, D), F32), TR=vm((4 + Z, 8, D), F32),
        HG=vm((4, QC // 128, 8, 128), F32), BG=vm((2, QC // 64, 8, 128), F32),
        send=pltpu.SemaphoreType.DMA((192,)), recv=pltpu.SemaphoreType.DMA((192,)),
    )


INPUTS = (
    "tok", "cot", "seg", "var", "tim", "wq", "wk", "wv", "wo", "wg", "wu", "wd", "gains", "hgain", "bias",
)
OUTPUTS = ("act", "ig", "gq", "gk", "gv", "go", "gg", "gu", "gd", "tot")


def fused(s, names, *refs):
    R = dict(zip(names, refs, strict=True))
    n, S, L, D, rows, T, G, Z, QC, FC, B = (
        s[k] for k in ("n", "S", "L", "D", "rows", "T", "G", "Z", "QC", "FC", "B")
    )
    HF = FC // 2
    Q = 4 * T
    me = lax.axis_index("fsdp")
    r, c, xx, g = lax.rem(me, 4), lax.rem(me, 2), lax.rem(lax.div(me, 2), 2), lax.div(me, 4)
    y, z = lax.rem(g, 2), lax.div(g, 2)
    r_sib, r_par = r + 1 - 2 * c, r + 2 - 4 * xx
    r_dia = r_sib + 2 - 4 * xx
    sib, par, dia = me - r + r_sib, me - r + r_par, me - r + r_dia
    peer = me + 4 - 8 * y
    quad = ((sib, r_sib), (par, r_par), (dia, r_dia))

    def at_z(step):
        return lax.rem(z + step, Z)

    def z_dev(step):
        return at_z(step) * 8 + y * 4 + r

    def z_src(step):
        return lax.rem(z + Z - step, Z)

    used = [0]
    sent = []

    def take(count=1):
        used[0] += count
        return used[0] - count

    def remote(src, dst, device, sem=None):
        sem = take() if sem is None else sem
        return pltpu.make_async_remote_copy(
            src_ref=src, dst_ref=dst, send_sem=R["send"].at[sem], recv_sem=R["recv"].at[sem],
            device_id=(device,), device_id_type=MESH,
        )

    def go(copy):
        copy.start()
        sent.append(copy)
        return copy

    SA, SB, WA, WB, WC, WO = (R[k] for k in ("SA", "SB", "WA", "WB", "WC", "WO"))
    for q in range(4):
        for m, name in enumerate(("wq", "wk", "wv", "wo")):
            SA[q, :, QC * m : QC * (m + 1)] = R[name][:, QC * q : QC * (q + 1)]
        for j in range(G):
            half, within = divmod(B * j, HF)
            source = slice(B * (4 * j + q), B * (4 * j + q) + B)
            SB[q, :, half * FC + within : half * FC + within + B] = R["wg"][:, source]
            SB[q, :, half * FC + HF + within : half * FC + HF + within + B] = R["wu"][:, source]
    own = at(B * g + rows * r, rows)
    WA[own, :] = SA[r]
    WB[own, :] = SB[r]
    WC[at(B * g, B), :] = R["wd"][...]
    idq = R["idq"]
    for q in range(S):
        idq[S * r + q, 0:1, :] = R["seg"][q : q + 1, :].astype(F32)
        idq[S * r + q, 1:2, :] = R["var"][q : q + 1, :].astype(F32)
        idq[S * r + q, 2:3, :] = R["tim"][q : q + 1, :].astype(F32)
        idq[S * r + q, 3:8, :] = jnp.zeros((5, L), F32)
    GT, GR = R["GT"], R["GR"]
    GT[0] = R["gains"][...]
    dyQ, h1Q, h2Q, attQ = R["dyQ"], R["h1Q"], R["h2Q"], R["attQ"]
    dyQ[at(T * r, T), :] = R["cot"][...]

    barrier = pltpu.get_barrier_semaphore()
    others = [sib, par, dia, peer] + [z_dev(d) for d in range(1, Z)]
    for device in others:
        pl.semaphore_signal(barrier, inc=1, device_id=(device,), device_id_type=MESH)
    pl.semaphore_wait(barrier, len(others))

    def tile_sum(tile, got):
        first = [remote(tile.at[0], got.at[i], dev) for i, (dev, _) in enumerate(quad)]
        second = remote(tile.at[1], got.at[3], peer)
        third = [remote(tile.at[2], got.at[4 + z], z_dev(d)) for d in range(1, Z)]

        def round1():
            for copy in first:
                go(copy)

        def round2():
            for copy in first:
                copy.wait_recv()
            tile[1] = (tile[0] + got[0]) + (got[1] + got[2])
            go(second)

        def round3():
            second.wait_recv()
            value = tile[1] + got[3]
            tile[2] = value
            got[4 + z] = value
            for copy in third:
                go(copy)

        def finish():
            for copy in third:
                copy.wait_recv()
            value = got[4]
            for i in range(1, Z):
                value = value + got[4 + i]
            return value

        return round1, round2, round3, finish

    def quad_gather(block):
        to_sib, to_par = remote(block(r), block(r), sib), remote(block(r), block(r), par)
        passed = remote(block(r_par), block(r_par), sib)

        def start():
            go(to_par)
            go(to_sib)

        def forward():
            to_par.wait_recv()
            go(passed)

        def finish():
            to_sib.wait_recv()
            passed.wait_recv()

        return start, forward, finish

    chunks = [(WA, 0, 2 * QC), (WA, 2 * QC, 2 * QC)]
    chunks += [(WB, HF * k, HF) for k in range(4)]
    chunks += [(WC, 0, D // 2), (WC, D // 2, D // 2)]

    def piece(k, group):
        ref, start, size = chunks[k]
        return ref.at[at(B * group, B), pl.ds(start, size)]

    along = [[remote(piece(k, g), piece(k, g), z_dev(d)) for d in range(1, Z)] for k in range(8)]
    over = [
        [remote(piece(k, 2 * z_src(d) + y), piece(k, 2 * z_src(d) + y), peer) for d in range(Z)]
        for k in range(8)
    ]

    def ag_start(k):
        for copy in along[k]:
            go(copy)
        go(over[k][0])

    def ag_forward(k):
        for d in range(1, Z):
            along[k][d - 1].wait_recv()
            go(over[k][d])

    def ag_finish(k):
        for copy in over[k]:
            copy.wait_recv()

    g1, g2, g3, g_finish = tile_sum(GT, GR)
    g1()
    sendA = [remote(SA.at[q], WA.at[own], dev) for dev, q in quad]
    sendB = [remote(SB.at[q], WB.at[own], dev) for dev, q in quad]
    for copy in sendA:
        go(copy)
    mine = idq.at[pl.ds(S * r, S)]
    sendI = [remote(mine, mine, dev) for dev, q in quad]
    for copy in sendI:
        go(copy)
    for copy in sendB:
        go(copy)
    g2()
    for copy in sendA:
        copy.wait_recv()
    ag_start(0)
    ag_start(1)
    g3()
    for copy in sendB:
        copy.wait_recv()
    for k in range(2, 8):
        ag_start(k)
    for copy in sendI:
        copy.wait_recv()

    lane = lax.broadcasted_iota(jnp.int32, (L, 128), 1)
    sub = lax.broadcasted_iota(jnp.int32, (L, 128), 0)
    front = lax.rem(lane, 64) < 32
    low = lane < 64
    freq = jnp.exp(-math.log(10000.0) * lax.rem(lane, 32).astype(F32) / 32)
    CT, ST = R["CT"], R["ST"]

    def tables(q):
        times = jnp.broadcast_to(idq[q, 2:3, :], (L, L)).T
        angles = times * freq
        CT[at(L * q, L), :] = jnp.cos(angles)
        sine = jnp.sin(angles)
        ST[at(L * q, L), :] = jnp.where(front, -sine, sine)

    loop(4 * S, tables)

    for copy in sent[:3]:
        copy.wait_send()
    del sent[:3]
    GT[0] = g_finish()
    tok = R["tok"]
    step = 64

    def norm_in(i):
        x = tok[at(step * i, step), :].astype(F32)
        inv = lax.rsqrt(jnp.mean(x * x, axis=-1, keepdims=True) + EPSILON)
        h1Q[at(T * r + step * i, step), :] = (x * inv * GT[0, 0:1, :]).astype(BF16)

    loop(T // step, norm_in)

    def token_block(ref):
        return lambda role: ref.at[at(T * role, T)]

    h1_start, h1_forward, h1_finish = quad_gather(token_block(h1Q))
    dy_start, dy_forward, dy_finish = quad_gather(token_block(dyQ))
    att_start, att_forward, att_finish = quad_gather(lambda role: attQ.at[:, lanes(QC * role, QC)])
    wo_start, wo_forward, wo_finish = quad_gather(lambda role: WO.at[:, lanes(QC * role, QC)])
    h2_start, h2_forward, h2_finish = quad_gather(token_block(h2Q))
    h1_start()
    ag_forward(0)
    h1_forward()
    dy_start()
    ag_forward(1)
    h1_finish()
    ag_finish(0)
    ag_finish(1)

    qraw, kraw, qr, kr, vb, PR = (R[k] for k in ("qraw", "kraw", "qr", "kr", "vb", "PR"))
    hgain, bias = R["hgain"], R["bias"]

    def swap(v):
        return jnp.where(front, pltpu.roll(v, 96, 1), pltpu.roll(v, 32, 1))

    def per_head(v):
        first = jnp.sum(jnp.where(low, v, 0.0), axis=-1, keepdims=True)
        second = jnp.sum(jnp.where(low, 0.0, v), axis=-1, keepdims=True)
        return jnp.where(low, first, second)

    def project_heads(q):
        at_q = at(L * q, L)
        value = mm(h1Q[at_q, :], WA[:, 0 : 3 * QC])
        cosine, sine = CT[at_q, :], ST[at_q, :]
        for m, (raw, ready) in enumerate(((qraw, qr), (kraw, kr))):
            raw[at_q, :] = value[:, QC * m : QC * (m + 1)]
            for j in range(QC // 128):
                v = value[:, QC * m + 128 * j : QC * m + 128 * (j + 1)]
                inv = lax.rsqrt(per_head(v * v) / 64 + EPSILON)
                v = v * inv * hgain[m : m + 1, :]
                v = v * cosine + swap(v) * sine
                if m == 0:
                    v = v * 0.125
                ready[at_q, 128 * j : 128 * (j + 1)] = v.astype(BF16)
        vb[at_q, :] = value[:, 2 * QC : 3 * QC].astype(BF16)

    loop(4 * S, project_heads)
    WO[:, lanes(QC * r, QC)] = WA[:, 3 * QC : 4 * QC]
    wo_start()
    ag_forward(2)
    dy_forward()

    def masks(q):
        segment = jnp.broadcast_to(idq[q, 0:1, :], (L, L))
        variate = jnp.broadcast_to(idq[q, 1:2, :], (L, L))
        allowed = (segment == segment.T) & ((segment != 0.0) | (lane == sub))
        return allowed, variate == variate.T

    heads = [jnp.where(low, 1.0, 0.0).astype(BF16), jnp.where(low, 0.0, 1.0).astype(BF16)]

    def attend(q):
        at_q = at(L * q, L)
        allowed, same = masks(q)
        for j in range(QC // 128):
            tile = slice(128 * j, 128 * (j + 1))
            q2, k2, v2 = qr[at_q, tile], kr[at_q, tile], vb[at_q, tile]
            outs = []
            for h in range(2):
                head = 2 * j + h
                index = QC // 64 * r + head
                score = mm(q2 * heads[h], k2, NT) + jnp.where(same, bias[1, index], bias[0, index])
                score = jnp.where(allowed, score, -1000000000.0)
                e = jnp.exp(score - jnp.max(score, axis=-1, keepdims=True))
                p = e / jnp.sum(e, axis=-1, keepdims=True)
                PR[q, head] = p
                outs.append(mm(p.astype(BF16), v2))
            attQ[at_q, lanes(QC * r + 128 * j, 128)] = jnp.where(low, outs[0], outs[1]).astype(BF16)

    loop(4 * S, attend)
    att_start()
    wo_forward()
    ag_forward(3)
    att_forward()
    wo_finish()
    att_finish()

    x1, dx1, acc = R["x1"], R["dx1"], R["acc"]

    def mix(i):
        x = tok[at(step * i, step), :].astype(F32) + mm(attQ[at(T * r + step * i, step), :], WO[...])
        x1[at(step * i, step), :] = x
        inv = lax.rsqrt(jnp.mean(x * x, axis=-1, keepdims=True) + EPSILON)
        h2Q[at(T * r + step * i, step), :] = (x * inv * GT[0, 1:2, :]).astype(BF16)

    loop(T // step, mix)
    h2_start()
    ag_forward(4)
    h2_forward()
    dy_finish()
    ag_forward(5)
    h2_finish()
    for k in range(2, 6):
        ag_finish(k)

    hid, dgdu = R["hid"], R["dgdu"]

    def hidden(i):
        at_i = at(L * i, L)
        for half in range(2):
            both = mm(h2Q[at_i, :], WB[:, half * FC : (half + 1) * FC])
            gate, up = both[:, 0:HF], both[:, HF:FC]
            hid[at_i, half * HF : (half + 1) * HF] = (gate / (1.0 + jnp.exp(-gate)) * up).astype(BF16)

    loop(4 * S, hidden)
    ag_forward(6)

    YS, YR, ZR, QS, QR = (R[k] for k in ("YS", "YR", "ZR", "QS", "QR"))
    y_sem, z_sem = [take(Z) for _ in range(4)], [take(Z - 1) for _ in range(4)]

    def gradient(unit, group, store):
        at_g = lanes(B * group, B)
        if unit == 0:
            store(slice(0, FC), mm(hid[:, at_g], dyQ[...], TN))
        elif unit < 3:
            store(slice(0, FC), mm(h2Q[:, at_g], dgdu[:, (unit - 1) * FC : unit * FC], TN))
        else:
            store(slice(0, 3 * QC), mm(h1Q[:, at_g], hid[:, 0 : 3 * QC], TN))
            store(slice(3 * QC, 4 * QC), mm(attQ[:, at_g], R["daR"][...], TN))

    def y_copy(unit, i):
        return remote(YS.at[unit % 2, i], YR.at[unit, i], peer, y_sem[unit] + i)

    def z_copy(unit, i):
        return remote(YR.at[unit, i], ZR.at[unit, i - 1], z_dev(i), z_sem[unit] + i - 1)

    def order(i):
        return lax.rem(i + 1, Z)

    def rs_first(unit):
        if unit >= 2:
            for i in range(Z):
                y_copy(unit - 2, i).wait_send()

        def body(i):
            d = order(i)

            def store(cols, value):
                YS[unit % 2, d, :, cols] = value.astype(BF16)

            gradient(unit, 2 * at_z(d) + 1 - y, store)
            y_copy(unit, d).start()

        loop(Z, body)

    def rs_second(unit):
        def body(i):
            d = order(i)
            y_copy(unit, d).wait_recv()

            def store(cols, value):
                YR[unit, d, :, cols] = (value + YR[unit, d, :, cols].astype(F32)).astype(BF16)

            gradient(unit, 2 * at_z(d) + y, store)

            @pl.when(d != 0)
            def _():
                z_copy(unit, d).start()

        loop(Z, body)

    quad_copies = {}

    def rs_third(unit):
        for i in range(1, Z):
            z_copy(unit, i).wait_recv()
        width = 256
        for j in range(FC // width):
            cols = slice(width * j, width * (j + 1))
            value = YR[unit, 0, :, cols].astype(F32)
            for i in range(1, Z):
                value = value + ZR[unit, i - 1, :, cols].astype(F32)
            if unit == 0:
                R["gd"][:, cols] = value
            else:
                QS[unit - 1, :, cols] = value.astype(BF16)
        if unit:
            QR[unit - 1, r] = QS[unit - 1, at(rows * r, rows), :]
            quad_copies[unit] = [
                go(remote(QS.at[unit - 1, at(rows * q, rows)], QR.at[unit - 1, r], dev)) for dev, q in quad
            ]

    def rs_last(unit):
        for copy in quad_copies[unit]:
            copy.wait_recv()
        for q in range(4):
            if unit == 3:
                for m, name in enumerate(("gq", "gk", "gv", "go")):
                    R[name][:, QC * q : QC * (q + 1)] = QR[unit - 1, q, :, QC * m : QC * (m + 1)].astype(F32)
            else:
                for j in range(G):
                    half, within = divmod(B * j, HF)
                    if half == unit - 1:
                        target = slice(B * (4 * j + q), B * (4 * j + q) + B)
                        R["gg"][:, target] = QR[unit - 1, q, :, within : within + B].astype(F32)
                        R["gu"][:, target] = QR[unit - 1, q, :, HF + within : HF + within + B].astype(F32)

    rsS, rsR = R["rsS"], R["rsR"]

    def quad_sum(kind, prepare_block, partial):
        width = 512
        tiles = [slice(width * j, width * (j + 1)) for j in range(D // width)]
        copies = [
            remote(rsS.at[0], rsR.at[kind, 0], sib),
            remote(rsS.at[1], rsR.at[kind, 1], sib),
            remote(rsS.at[2], rsR.at[kind, 2], par),
        ]

        def blocks(role, store):
            def body(i):
                for cols in tiles:
                    store(at(L * i, L), cols, partial(at(T * role + L * i, L), cols))

            loop(T // L, body)

        def to_dia(at_i, cols, value):
            rsS[1, at_i, cols] = value.astype(BF16)

        def to_par(at_i, cols, value):
            rsS[2, at_i, cols] = (value + rsR[kind, 1, at_i, cols].astype(F32)).astype(BF16)

        def to_sib(at_i, cols, value):
            rsS[0, at_i, cols] = value.astype(BF16)

        def keep(at_i, cols, value):
            acc[at_i, cols] = value

        prepare_block(r_dia)
        blocks(r_dia, to_dia)
        copies[1].start()
        prepare_block(r_par)
        copies[1].wait_recv()
        blocks(r_par, to_par)
        copies[2].start()
        prepare_block(r_sib)
        blocks(r_sib, to_sib)
        copies[0].start()
        prepare_block(r)
        blocks(r, keep)

        def finish():
            copies[0].wait_recv()
            copies[2].wait_recv()
            for copy in copies:
                copy.wait_send()

        return finish

    def summed(kind, at_i):
        return acc[at_i, :] + (rsR[kind, 0, at_i, :].astype(F32) + rsR[kind, 2, at_i, :].astype(F32))

    rs_first(0)
    ag_forward(7)
    rs_second(0)
    ag_finish(6)
    ag_finish(7)

    def ffn_back(role):
        def body(i):
            at_i = at(T * role + L * i, L)
            for half in range(2):
                both = mm(h2Q[at_i, :], WB[:, half * FC : (half + 1) * FC])
                gate, up = both[:, 0:HF], both[:, HF:FC]
                d_hidden = mm(dyQ[at_i, :], WC[half * HF : (half + 1) * HF, :], NT)
                sigma = 1.0 / (1.0 + jnp.exp(-gate))
                d_up = d_hidden * (gate * sigma)
                d_gate = d_hidden * up * (sigma * (1.0 + gate * (1.0 - sigma)))
                dgdu[at_i, half * FC : half * FC + HF] = d_gate.astype(BF16)
                dgdu[at_i, half * FC + HF : (half + 1) * FC] = d_up.astype(BF16)

        loop(T // L, body)

    def nothing(role):
        return None

    h2_sum = quad_sum(0, ffn_back, lambda at_i, cols: mm(dgdu[at_i, :], WB[cols, :], NT))
    rs_first(1)
    h2_sum()

    TT, TR = R["TT"], R["TR"]
    daS, daR, dattS, dattR = (R[k] for k in ("daS", "daR", "dattS", "dattR"))
    TT[0] = jnp.zeros((8, D), F32)

    def norm_back(v, d_out, gain, row):
        inv = lax.rsqrt(jnp.mean(v * v, axis=-1, keepdims=True) + EPSILON)
        TT[0, row : row + 1, :] += jnp.sum(d_out * (v * inv), axis=0, keepdims=True)
        d = d_out * gain
        return inv * d - v * (inv * inv * inv * jnp.mean(d * v, axis=-1, keepdims=True))

    def mix_back(i):
        at_i = at(step * i, step)
        d = norm_back(x1[at_i, :], summed(0, at_i), GT[0, 1:2, :], 1)
        d = d + R["cot"][at_i, :].astype(F32)
        dx1[at_i, :] = d
        daS[at_i, :] = d.astype(BF16)

    loop(T // step, mix_back)
    sendD = [remote(daS.at[:, lanes(QC * q, QC)], daR.at[at(T * r, T)], dev) for dev, q in quad]
    sendT = [remote(dattS.at[:, lanes(QC * q, QC)], dattR.at[at(T * r, T)], dev) for dev, q in quad]

    def out_back(i):
        at_i = at(step * i, step)
        dattS[at_i, :] = mm(daS[at_i, :], WO[...], NT).astype(BF16)

    loop(T // step, out_back)
    for copy in sendT:
        go(copy)
    for copy in sendD:
        go(copy)
    dattR[at(T * r, T), :] = dattS[:, lanes(QC * r, QC)]
    daR[at(T * r, T), :] = daS[:, lanes(QC * r, QC)]
    rs_second(1)
    rs_first(2)

    out_sum = quad_sum(1, nothing, lambda at_i, cols: mm(hid[at_i, :], WC[:, cols]))
    out_sum()

    def write_out(i):
        at_i = at(step * i, step)
        R["act"][at_i, :] = (x1[at_i, :] + summed(1, at_i)).astype(BF16)

    loop(T // step, write_out)
    for copy in sendT:
        copy.wait_recv()

    HG, BG = R["HG"], R["BG"]
    HG[...] = jnp.zeros(HG.shape, F32)
    BG[...] = jnp.zeros(BG.shape, F32)

    def fold(v):
        return jnp.sum(v.reshape(L // 8, 8, 128), axis=0)

    def prepare_back(raw, d, m, j, cosine, sine, factor):
        if factor != 1.0:
            d = d * factor
        d = d * cosine - swap(d) * sine
        inv = lax.rsqrt(per_head(raw * raw) / 64 + EPSILON)
        HG[m, j] += fold(d * (raw * inv))
        d = d * hgain[m : m + 1, :]
        return inv * d - raw * (inv * inv * inv * (per_head(d * raw) / 64))

    def attend_back(q):
        at_q = at(L * q, L)
        _, same = masks(q)
        cosine, sine = CT[at_q, :], ST[at_q, :]
        for j in range(QC // 128):
            tile = slice(128 * j, 128 * (j + 1))
            q2, k2, v2, d2 = qr[at_q, tile], kr[at_q, tile], vb[at_q, tile], dattR[at_q, tile]
            dq, dk, dv = [], [], []
            for h in range(2):
                p = PR[q, 2 * j + h]
                dp = mm(d2 * heads[h], v2, NT)
                ds = (p * (dp - jnp.sum(p * dp, axis=-1, keepdims=True))).astype(BF16)
                wide = ds.astype(F32)
                BG[0, 2 * j + h] += fold(jnp.where(same, 0.0, wide))
                BG[1, 2 * j + h] += fold(jnp.where(same, wide, 0.0))
                dv.append(mm(p.astype(BF16), d2, TN))
                dq.append(mm(ds, k2))
                dk.append(mm(ds, q2, TN))
            d_query = jnp.where(low, dq[0], dq[1])
            d_key = jnp.where(low, dk[0], dk[1])
            d_query = prepare_back(qraw[at_q, tile], d_query, 0, j, cosine, sine, 0.125)
            d_key = prepare_back(kraw[at_q, tile], d_key, 1, j, cosine, sine, 1.0)
            hid[at_q, tile] = d_query.astype(BF16)
            hid[at_q, QC + 128 * j : QC + 128 * (j + 1)] = d_key.astype(BF16)
            hid[at_q, 2 * QC + 128 * j : 2 * QC + 128 * (j + 1)] = jnp.where(low, dv[0], dv[1]).astype(BF16)

    loop(4 * S, attend_back)
    rs_second(2)
    for copy in sendD:
        copy.wait_recv()
    rs_first(3)
    rs_third(0)
    in_sum = quad_sum(2, nothing, lambda at_i, cols: mm(hid[at_i, 0 : 3 * QC], WA[cols, 0 : 3 * QC], NT))
    rs_third(1)
    rs_second(3)
    in_sum()

    def input_back(i):
        at_i = at(step * i, step)
        d = norm_back(tok[at_i, :].astype(F32), summed(2, at_i), GT[0, 0:1, :], 0)
        R["ig"][at_i, :] = (dx1[at_i, :] + d).astype(BF16)

    loop(T // step, input_back)

    for m in range(2):
        value = HG[m, 0]
        for j in range(1, QC // 128):
            value = value + HG[m, j]
        TT[0, 2:3, 128 * m : 128 * (m + 1)] = jnp.sum(value, axis=0, keepdims=True)
    spot = lax.broadcasted_iota(jnp.int32, (1, 128), 1)
    for m in range(2):
        line = jnp.zeros((1, 128), F32)
        for h in range(QC // 64):
            line = line + jnp.where(spot == QC // 64 * r + h, jnp.sum(BG[m, h]), 0.0)
        TT[0, 3 + m : 4 + m, 0:128] = line
    t1, t2, t3, t_finish = tile_sum(TT, TR)
    t1()
    rs_third(2)
    t2()
    rs_last(1)
    t3()
    rs_last(2)
    R["tot"][...] = t_finish()
    rs_third(3)
    rs_last(3)
    for copy in sent:
        copy.wait_send()
    for unit in range(4):
        for i in range(Z):
            if unit >= 2:
                y_copy(unit, i).wait_send()
            if i:
                z_copy(unit, i).wait_send()


def layer(s, tokens, segment_ids, variate_ids, time_ids, w_query, w_key, w_value, w_out, w_gate, w_up, w_down,
          gain_attn, gain_ffn, gain_query, gain_key, variate_bias, cotangent):
    D, T, rows, B, FF = s["D"], s["T"], s["rows"], s["B"], s["FF"]
    owner = lax.axis_index("fsdp")
    pair = jnp.stack([gain_attn, gain_ffn]).astype(F32)
    gains = lax.dynamic_update_slice(jnp.zeros((8, D), F32), pair, (0, owner * rows))
    hgain = jnp.tile(jnp.stack([gain_query, gain_key]).astype(F32), (4, 2))
    scratch = scratch_of(s)
    names = INPUTS + OUTPUTS + tuple(scratch)
    vmem = pl.BlockSpec(memory_space=pltpu.VMEM)
    small = [(rows, D)] * 4 + [(rows, FF)] * 2 + [(B, D), (8, D)]
    outs = pl.pallas_call(
        functools.partial(fused, s, names),
        out_shape=[jax.ShapeDtypeStruct((T, D), BF16)] * 2 + [jax.ShapeDtypeStruct(d, F32) for d in small],
        in_specs=[vmem] * (len(INPUTS) - 1) + [pl.BlockSpec(memory_space=pltpu.SMEM)],
        out_specs=[vmem] * len(OUTPUTS),
        scratch_shapes=list(scratch.values()),
        compiler_params=pltpu.CompilerParams(
            collective_id=0, has_side_effects=True, vmem_limit_bytes=64 << 20
        ),
        name="fused_layer",
    )(
        tokens.reshape(T, D), cotangent.reshape(T, D), segment_ids, variate_ids, time_ids,
        w_query, w_key, w_value, w_out, w_gate, w_up, w_down, gains, hgain, variate_bias.astype(F32),
    )
    act, ig, gq, gk, gv, go, gg, gu, gd, tot = outs
    attn_own = lax.dynamic_slice(tot, (0, owner * rows), (1, rows)).reshape(rows)
    ffn_own = lax.dynamic_slice(tot, (1, owner * rows), (1, rows)).reshape(rows)
    HD, H = s["HD"], s["H"]
    return (
        act.reshape(tokens.shape), ig.reshape(tokens.shape), gq, gk, gv, go, gg, gu, gd, attn_own, ffn_own,
        tot[2, 0:HD] + tot[2, HD : 2 * HD], tot[2, 128 : 128 + HD] + tot[2, 128 + HD : 128 + 2 * HD],
        tot[3:5, 0:H],
    )


def local(tokens, segment_ids, variate_ids, time_ids, *rest):
    s = sizes_of(lax.axis_size("fsdp"), tokens, rest[0], rest[4], rest[9], rest[11])
    chosen = functools.partial(layer, s) if fits(s) else plain
    return chosen(tokens, segment_ids, variate_ids, time_ids, *rest)


def solution(mesh):
    placed = (
        P("fsdp", None, None),
        P("fsdp", None),
        P("fsdp", None),
        P("fsdp", None),
        P("fsdp", None),
        P("fsdp", None),
        P("fsdp", None),
        P("fsdp", None),
        P("fsdp", None),
        P("fsdp", None),
        P("fsdp", None),
        P("fsdp"),
        P("fsdp"),
        P(),
        P(),
        P(),
        P("fsdp", None, None),
    )
    return jax.shard_map(
        local,
        mesh=mesh,
        in_specs=placed,
        out_specs=(
            P("fsdp", None, None),
            P("fsdp", None, None),
            P("fsdp", None),
            P("fsdp", None),
            P("fsdp", None),
            P("fsdp", None),
            P("fsdp", None),
            P("fsdp", None),
            P("fsdp", None),
            P("fsdp"),
            P("fsdp"),
            P(),
            P(),
            P(),
        ),
        check_vma=False,
    )
```

```python
import functools
import math

import jax
import jax.numpy as jnp
from jax import lax
from jax.experimental import pallas as pl
from jax.experimental.pallas import tpu as pltpu
from jax.sharding import PartitionSpec as P

EPSILON = 1e-05


def normalize(values, scale_gain):
    return (
        values * lax.rsqrt(jnp.mean(values * values, axis=-1, keepdims=True) + EPSILON) * scale_gain
    )


def rotate(values, moments):
    halfway = values.shape[-1] // 2
    frequency = jnp.exp(-math.log(10000.0) * jnp.arange(halfway).astype(jnp.float32) / halfway)
    angles = moments.astype(jnp.float32)[:, None] * frequency[None, :]
    cosine = jnp.cos(angles)[:, None, :]
    sine_part = jnp.sin(angles)[:, None, :]
    former = values[..., :halfway]
    latter = values[..., halfway:]
    return jnp.concatenate(
        [former * cosine - latter * sine_part, former * sine_part + latter * cosine], axis=-1
    )


def prepare(raw_heads, head_gain, moments, factor):
    return rotate(normalize(raw_heads, head_gain), moments) * factor


def swiglu(gate_act, up_act):
    return jax.nn.silu(gate_act) * up_act


def attention_masks(segments, variates):
    length = segments.shape[0]
    diagonal = jnp.arange(length)[:, None] == jnp.arange(length)[None, :]
    allowed = (segments[:, None] == segments[None, :]) & ((segments[None, :] != 0) | diagonal)
    same_var = variates[:, None] == variates[None, :]
    return (allowed, same_var)


def scoring(q_rot, k_rot, bias_table, allowed, same_var):
    scores = jnp.einsum("qhe,khe->hqk", q_rot, k_rot, preferred_element_type=jnp.float32)
    scores = scores + jnp.where(
        same_var[None], bias_table[1][:, None, None], bias_table[0][:, None, None]
    )
    return jnp.where(allowed[None], scores, -1000000000.0)


def project(left, right):
    return jnp.dot(left, right, preferred_element_type=jnp.float32)


def across(left, right):
    return lax.dot_general(
        left, right, (((0,), (0,)), ((), ())), preferred_element_type=jnp.float32
    )


def against(left, weight):
    return lax.dot_general(
        left, weight, (((1,), (1,)), ((), ())), preferred_element_type=jnp.float32
    )


def forward(inputs_low, weights, side_params, segments, variates, moments):
    w_query, w_key, w_value, w_out, w_gate, w_up, w_down, gain_attn, gain_ffn = weights
    gain_query, gain_key, bias_table = side_params
    length, model_width = inputs_low.shape
    head_count = bias_table.shape[1]
    head_dim = gain_query.shape[0]
    inputs = inputs_low.astype(jnp.float32)
    normed = normalize(inputs, gain_attn.astype(jnp.float32)).astype(jnp.bfloat16)
    queries = project(normed, w_query).reshape(length, head_count, head_dim)
    key_raw = project(normed, w_key).reshape(length, head_count, head_dim)
    v_low = project(normed, w_value).reshape(length, head_count, head_dim).astype(jnp.bfloat16)
    q_rot = prepare(queries, gain_query, moments, head_dim ** (-0.5)).astype(jnp.bfloat16)
    k_rot = prepare(key_raw, gain_key, moments, 1.0).astype(jnp.bfloat16)
    allowed, same_var = attention_masks(segments, variates)
    scores = scoring(q_rot, k_rot, bias_table, allowed, same_var)
    maximum = jnp.max(scores, axis=-1, keepdims=True)
    exponent = jnp.exp(scores - maximum)
    row_total = jnp.sum(exponent, axis=-1, keepdims=True)
    log_total = maximum + jnp.log(row_total)
    softmax_probs = (exponent / row_total).astype(jnp.bfloat16)
    attended = jnp.einsum("hqk,khe->qhe", softmax_probs, v_low, preferred_element_type=jnp.float32)
    attended = attended.reshape(length, model_width).astype(jnp.bfloat16)
    mixed_state = inputs + project(attended, w_out)
    normed_ffn = normalize(mixed_state, gain_ffn.astype(jnp.float32)).astype(jnp.bfloat16)
    gate_act = project(normed_ffn, w_gate)
    up_act = project(normed_ffn, w_up)
    hidden = swiglu(gate_act, up_act).astype(jnp.bfloat16)
    result = mixed_state + project(hidden, w_down)
    kept_state = (
        inputs,
        normed,
        queries,
        key_raw,
        q_rot,
        k_rot,
        v_low,
        log_total,
        attended,
        mixed_state,
        normed_ffn,
        gate_act,
        up_act,
        hidden,
    )
    return (result, kept_state)


def backward(upstream, kept_state, weights, side_params, segments, variates, moments):
    (
        inputs,
        normed,
        queries,
        key_raw,
        q_rot,
        k_rot,
        v_low,
        log_total,
        attended,
        mixed_state,
        normed_ffn,
        gate_act,
        up_act,
        hidden,
    ) = kept_state
    w_query, w_key, w_value, w_out, w_gate, w_up, w_down, gain_attn, gain_ffn = weights
    gain_query, gain_key, bias_table = side_params
    length, head_count, head_dim = queries.shape
    grad_down = across(hidden, upstream)
    d_hidden = against(upstream, w_down)
    _, pullback = jax.vjp(swiglu, gate_act, up_act)
    d_gate, d_up = pullback(d_hidden)
    d_gate = d_gate.astype(jnp.bfloat16)
    d_up = d_up.astype(jnp.bfloat16)
    grad_gate = across(normed_ffn, d_gate)
    grad_up = across(normed_ffn, d_up)
    d_normed_ffn = against(d_gate, w_gate) + against(d_up, w_up)
    _, pullback = jax.vjp(normalize, mixed_state, gain_ffn.astype(jnp.float32))
    d_mixed, grad_gain_ffn = pullback(d_normed_ffn)
    d_mixed = d_mixed + upstream.astype(jnp.float32)
    d_branch = d_mixed.astype(jnp.bfloat16)
    grad_out = across(attended, d_branch)
    d_attended = against(d_branch, w_out).astype(jnp.bfloat16).reshape(length, head_count, head_dim)
    allowed, same_var = attention_masks(segments, variates)
    scores = scoring(q_rot, k_rot, bias_table, allowed, same_var)
    softmax_probs = jnp.exp(scores - log_total)
    d_probs = jnp.einsum("qhe,khe->hqk", d_attended, v_low, preferred_element_type=jnp.float32)
    d_values = jnp.einsum(
        "hqk,qhe->khe",
        softmax_probs.astype(jnp.bfloat16),
        d_attended,
        preferred_element_type=jnp.float32,
    )
    d_values = d_values.reshape(length, head_count * head_dim).astype(jnp.bfloat16)
    weighted = jnp.sum(softmax_probs * d_probs, axis=-1, keepdims=True)
    d_scores = (softmax_probs * (d_probs - weighted)).astype(jnp.bfloat16)
    d_float = d_scores.astype(jnp.float32)
    same_sum = jnp.sum(jnp.where(same_var[None], d_float, 0.0), axis=(1, 2))
    other_sum = jnp.sum(jnp.where(same_var[None], 0.0, d_float), axis=(1, 2))
    grad_bias = jnp.stack([other_sum, same_sum])
    d_qrot = jnp.einsum("hqk,khe->qhe", d_scores, k_rot, preferred_element_type=jnp.float32)
    d_krot = jnp.einsum("hqk,qhe->khe", d_scores, q_rot, preferred_element_type=jnp.float32)
    factor = head_dim ** (-0.5)
    _, pullback = jax.vjp(
        lambda raw_heads, head_gain: prepare(raw_heads, head_gain, moments, factor),
        queries,
        gain_query,
    )
    d_queries, grad_gain_query = pullback(d_qrot)
    _, pullback = jax.vjp(
        lambda raw_heads, head_gain: prepare(raw_heads, head_gain, moments, 1.0), key_raw, gain_key
    )
    d_keys, grad_gain_key = pullback(d_krot)
    d_queries = d_queries.reshape(length, head_count * head_dim).astype(jnp.bfloat16)
    d_keys = d_keys.reshape(length, head_count * head_dim).astype(jnp.bfloat16)
    grad_query = across(normed, d_queries)
    grad_key = across(normed, d_keys)
    grad_value = across(normed, d_values)
    d_normed = against(d_queries, w_query) + against(d_keys, w_key) + against(d_values, w_value)
    _, pullback = jax.vjp(normalize, inputs, gain_attn.astype(jnp.float32))
    d_inputs, grad_gain_attn = pullback(d_normed)
    row_grads = jnp.concatenate(
        [grad_query, grad_key, grad_value, grad_out, grad_gate, grad_up], axis=1
    )
    small = (grad_gain_query, grad_gain_key, grad_bias, grad_gain_attn, grad_gain_ffn)
    return (d_inputs + d_mixed, row_grads, grad_down, small)


def plain(
    tokens,
    segment_ids,
    variate_ids,
    time_ids,
    w_query,
    w_key,
    w_value,
    w_out,
    w_gate,
    w_up,
    w_down,
    gain_attn,
    gain_ffn,
    gain_query,
    gain_key,
    variate_bias,
    cotangent,
):
    devices = lax.axis_size("fsdp")
    owner = lax.axis_index("fsdp")
    width = w_query.shape[1]
    hidden_width = w_gate.shape[1]
    own_rows = w_query.shape[0]
    own_down = w_down.shape[0]
    side_params = (
        gain_query.astype(jnp.float32),
        gain_key.astype(jnp.float32),
        variate_bias.astype(jnp.float32),
    )
    rows_total = jnp.zeros((own_rows * devices, 4 * width + 2 * hidden_width), jnp.float32)
    down_total = jnp.zeros((own_down * devices, width), jnp.float32)
    side_totals = (
        jnp.zeros(gain_query.shape, jnp.float32),
        jnp.zeros(gain_key.shape, jnp.float32),
        jnp.zeros(variate_bias.shape, jnp.float32),
        jnp.zeros((own_rows * devices,), jnp.float32),
        jnp.zeros((own_rows * devices,), jnp.float32),
    )
    results = []
    input_grads = []
    for micro_index in range(tokens.shape[0]):
        segments = segment_ids[micro_index]
        variates = variate_ids[micro_index]
        moments = time_ids[micro_index]
        forward_weights = (
            lax.all_gather(w_query, "fsdp", axis=0, tiled=True),
            lax.all_gather(w_key, "fsdp", axis=0, tiled=True),
            lax.all_gather(w_value, "fsdp", axis=0, tiled=True),
            lax.all_gather(w_out, "fsdp", axis=0, tiled=True),
            lax.all_gather(w_gate, "fsdp", axis=0, tiled=True),
            lax.all_gather(w_up, "fsdp", axis=0, tiled=True),
            lax.all_gather(w_down, "fsdp", axis=0, tiled=True),
            lax.all_gather(gain_attn, "fsdp", axis=0, tiled=True),
            lax.all_gather(gain_ffn, "fsdp", axis=0, tiled=True),
        )
        result, kept_state = forward(
            tokens[micro_index], forward_weights, side_params, segments, variates, moments
        )
        results.append(result.astype(jnp.bfloat16))
        backward_weights = (
            lax.all_gather(w_query, "fsdp", axis=0, tiled=True),
            lax.all_gather(w_key, "fsdp", axis=0, tiled=True),
            lax.all_gather(w_value, "fsdp", axis=0, tiled=True),
            lax.all_gather(w_out, "fsdp", axis=0, tiled=True),
            lax.all_gather(w_gate, "fsdp", axis=0, tiled=True),
            lax.all_gather(w_up, "fsdp", axis=0, tiled=True),
            lax.all_gather(w_down, "fsdp", axis=0, tiled=True),
            lax.all_gather(gain_attn, "fsdp", axis=0, tiled=True),
            lax.all_gather(gain_ffn, "fsdp", axis=0, tiled=True),
        )
        d_inputs, row_grads, down_grads, small = backward(
            cotangent[micro_index],
            kept_state,
            backward_weights,
            side_params,
            segments,
            variates,
            moments,
        )
        input_grads.append(d_inputs.astype(jnp.bfloat16))
        rows_total = rows_total + row_grads
        down_total = down_total + down_grads
        side_totals = tuple((running + fresh for running, fresh in zip(side_totals, small)))
    owned_rows = lax.psum_scatter(rows_total, "fsdp", scatter_dimension=0, tiled=True)
    owned_down = lax.psum_scatter(down_total, "fsdp", scatter_dimension=0, tiled=True)
    shared = lax.psum(
        (side_totals[0], side_totals[1], side_totals[2], side_totals[3], side_totals[4]), "fsdp"
    )
    gain_attn_own = lax.dynamic_slice_in_dim(shared[3], owner * own_rows, own_rows, 0)
    gain_ffn_own = lax.dynamic_slice_in_dim(shared[4], owner * own_rows, own_rows, 0)
    grad_query = owned_rows[:, 0:width]
    grad_key = owned_rows[:, width : 2 * width]
    grad_value = owned_rows[:, 2 * width : 3 * width]
    grad_out = owned_rows[:, 3 * width : 4 * width]
    grad_gate = owned_rows[:, 4 * width : 4 * width + hidden_width]
    grad_up = owned_rows[:, 4 * width + hidden_width :]
    return (
        jnp.stack(results),
        jnp.stack(input_grads),
        grad_query,
        grad_key,
        grad_value,
        grad_out,
        grad_gate,
        grad_up,
        owned_down,
        gain_attn_own,
        gain_ffn_own,
        shared[0],
        shared[1],
        shared[2],
    )


F32 = jnp.float32
BF16 = jnp.bfloat16
MESH = pl.DeviceIdType.MESH
NT = (((1,), (1,)), ((), ()))
TN = (((0,), (0,)), ((), ()))


def mm(left, right, dims=(((1,), (0,)), ((), ()))):
    return lax.dot_general(left, right, dims, preferred_element_type=F32)


def at(start, size):
    return pl.ds(pl.multiple_of(start, size), size)


def lanes(start, size):
    return pl.ds(pl.multiple_of(start, 128), size)


def loop(count, body):
    lax.fori_loop(0, count, lambda i, carry: (body(i), carry)[1], 0)


def sizes_of(devices, tokens, w_query, w_gate, gain_query, bias):
    seqs, length, width = tokens.shape
    own_rows, hidden = w_query.shape[0], w_gate.shape[1]
    return dict(
        n=devices, S=seqs, L=length, D=width, FF=hidden, rows=own_rows, T=seqs * length,
        G=devices // 4, Z=devices // 8, QC=width // 4, FC=hidden // 4, B=4 * own_rows,
        HD=gain_query.shape[0], H=bias.shape[1],
    )


def fits(s):
    return (
        s["n"] % 8 == 0 and s["rows"] % 16 == 0 and s["L"] == 128 and s["HD"] == 64
        and s["H"] * s["HD"] == s["D"] and s["QC"] % 128 == 0 and s["FF"] == 4 * s["D"]
        and s["B"] % 128 == 0 and s["FC"] // 2 % s["B"] == 0 and s["FC"] == s["D"]
    )


def scratch_of(s):
    n, S, L, D, rows, T, G, Z, QC, FC, B = (
        s[k] for k in ("n", "S", "L", "D", "rows", "T", "G", "Z", "QC", "FC", "B")
    )
    Q = 4 * T
    vm = pltpu.VMEM
    return dict(
        WA=vm((D, 4 * QC), BF16), WB=vm((D, 2 * FC), BF16), WC=vm((FC, D), BF16), WO=vm((D, D), BF16),
        SA=vm((4, rows, 4 * QC), BF16), SB=vm((4, rows, 2 * FC), BF16),
        h1Q=vm((Q, D), BF16), dyQ=vm((Q, D), BF16), attQ=vm((Q, D), BF16), h2Q=vm((Q, D), BF16),
        qraw=vm((Q, QC), F32), kraw=vm((Q, QC), F32),
        qr=vm((Q, QC), BF16), kr=vm((Q, QC), BF16), vb=vm((Q, QC), BF16),
        PR=vm((4 * S, QC // 64, L, L), F32), CT=vm((Q, 128), F32), ST=vm((Q, 128), F32),
        x1=vm((T, D), F32), dx1=vm((T, D), F32), acc=vm((T, D), F32),
        hid=vm((Q, FC), BF16), dgdu=vm((Q, 2 * FC), BF16),
        rsS=vm((3, T, D), BF16), rsR=vm((3, 3, T, D), BF16),
        daS=vm((T, D), BF16), daR=vm((Q, QC), BF16), dattS=vm((T, D), BF16), dattR=vm((Q, QC), BF16),
        YS=vm((3, Z, B, FC), BF16), YR=vm((4, Z, B, FC), BF16), ZR=vm((4, Z - 1, B, FC), BF16),
        QS=vm((3, B, FC), BF16), QR=vm((3, 4, rows, FC), BF16),
        idq=vm((4 * S, 8, L), F32),
        GT=vm((3, 8, D), F32), GR=vm((4 + Z, 8, D), F32),
        TT=vm((3, 8, D), F32), TR=vm((4 + Z, 8, D), F32),
        HG=vm((4, QC // 128, 8, 128), F32), BG=vm((2, QC // 64, 8, 128), F32),
        send=pltpu.SemaphoreType.DMA((192,)), recv=pltpu.SemaphoreType.DMA((192,)),
    )


INPUTS = (
    "tok", "cot", "seg", "var", "tim", "wq", "wk", "wv", "wo", "wg", "wu", "wd", "small",
)
OUTPUTS = ("act", "ig", "gd", "parts", "tot")


def fused(s, names, *refs):
    R = dict(zip(names, refs, strict=True))
    n, S, L, D, rows, T, G, Z, QC, FC, B = (
        s[k] for k in ("n", "S", "L", "D", "rows", "T", "G", "Z", "QC", "FC", "B")
    )
    HF = FC // 2
    Q = 4 * T
    me = lax.axis_index("fsdp")
    r, c, xx, g = lax.rem(me, 4), lax.rem(me, 2), lax.rem(lax.div(me, 2), 2), lax.div(me, 4)
    y, z = lax.rem(g, 2), lax.div(g, 2)
    r_sib, r_par = r + 1 - 2 * c, r + 2 - 4 * xx
    r_dia = r_sib + 2 - 4 * xx
    sib, par, dia = me - r + r_sib, me - r + r_par, me - r + r_dia
    peer = me + 4 - 8 * y
    quad = ((sib, r_sib), (par, r_par), (dia, r_dia))

    def at_z(step):
        return lax.rem(z + step, Z)

    def z_dev(step):
        return at_z(step) * 8 + y * 4 + r

    def z_src(step):
        return lax.rem(z + Z - step, Z)

    used = [0]
    sent = []

    def take(count=1):
        used[0] += count
        return used[0] - count

    def remote(src, dst, device, sem=None):
        sem = take() if sem is None else sem
        return pltpu.make_async_remote_copy(
            src_ref=src, dst_ref=dst, send_sem=R["send"].at[sem], recv_sem=R["recv"].at[sem],
            device_id=(device,), device_id_type=MESH,
        )

    def go(copy):
        copy.start()
        sent.append(copy)
        return copy

    SA, SB, WA, WB, WC, WO = (R[k] for k in ("SA", "SB", "WA", "WB", "WC", "WO"))
    for q in range(4):
        for m, name in enumerate(("wq", "wk", "wv", "wo")):
            SA[q, :, QC * m : QC * (m + 1)] = R[name][:, QC * q : QC * (q + 1)]
        for j in range(G):
            half, within = divmod(B * j, HF)
            source = slice(B * (4 * j + q), B * (4 * j + q) + B)
            SB[q, :, half * FC + within : half * FC + within + B] = R["wg"][:, source]
            SB[q, :, half * FC + HF + within : half * FC + HF + within + B] = R["wu"][:, source]
    own = at(B * g + rows * r, rows)
    WA[own, :] = SA[r]
    WB[own, :] = SB[r]
    WC[at(B * g, B), :] = R["wd"][...]
    idq = R["idq"]
    for q in range(S):
        idq[S * r + q, 0:1, :] = R["seg"][q : q + 1, :].astype(F32)
        idq[S * r + q, 1:2, :] = R["var"][q : q + 1, :].astype(F32)
        idq[S * r + q, 2:3, :] = R["tim"][q : q + 1, :].astype(F32)
        idq[S * r + q, 3:8, :] = jnp.zeros((5, L), F32)
    GT, GR = R["GT"], R["GR"]
    small = R["small"]
    GT[0] = jnp.zeros((8, D), F32)
    GT[0, :, lanes(128 * lax.div(rows * me, 128), 128)] = pltpu.roll(small[...], lax.rem(rows * me, 128), 1)
    dyQ, h1Q, h2Q, attQ = R["dyQ"], R["h1Q"], R["h2Q"], R["attQ"]
    dyQ[at(T * r, T), :] = R["cot"][...]

    barrier = pltpu.get_barrier_semaphore()
    others = [sib, par, dia, peer] + [z_dev(d) for d in range(1, Z)]
    for device in others:
        pl.semaphore_signal(barrier, inc=1, device_id=(device,), device_id_type=MESH)
    pl.semaphore_wait(barrier, len(others))

    def tile_sum(tile, got):
        first = [remote(tile.at[0], got.at[i], dev) for i, (dev, _) in enumerate(quad)]
        second = [remote(tile.at[1], got.at[4 + z], z_dev(d)) for d in range(1, Z)]
        third = remote(tile.at[2], got.at[3], peer)

        def round1():
            for copy in first:
                go(copy)

        def round2():
            for copy in first:
                copy.wait_recv()
            value = (tile[0] + got[0]) + (got[1] + got[2])
            tile[1] = value
            got[4 + z] = value
            for copy in second:
                go(copy)

        def round3():
            for copy in second:
                copy.wait_recv()
            value = got[4]
            for i in range(1, Z):
                value = value + got[4 + i]
            tile[2] = value
            go(third)

        def finish():
            third.wait_recv()
            return tile[2] + got[3]

        return round1, round2, round3, finish

    def quad_gather(block):
        to_sib, to_par = remote(block(r), block(r), sib), remote(block(r), block(r), par)
        passed = remote(block(r_par), block(r_par), sib)

        def start():
            go(to_par)
            go(to_sib)

        def forward():
            to_par.wait_recv()
            go(passed)

        def finish():
            to_sib.wait_recv()
            passed.wait_recv()

        return start, forward, finish

    chunks = [(WA, 0, 2 * QC), (WA, 2 * QC, 2 * QC), (WC, 0, D // 2), (WC, D // 2, D // 2)]
    chunks += [(WB, HF * k, HF) for k in range(4)]

    def piece(k, group):
        ref, start, size = chunks[k]
        return ref.at[at(B * group, B), pl.ds(start, size)]

    along = [[remote(piece(k, g), piece(k, g), z_dev(d)) for d in range(1, Z)] for k in range(8)]
    over = [
        [remote(piece(k, 2 * z_src(d) + y), piece(k, 2 * z_src(d) + y), peer) for d in range(Z)]
        for k in range(8)
    ]

    def ag_start(k):
        for copy in along[k]:
            go(copy)

    def ag_own(k):
        go(over[k][0])

    def ag_forward(k):
        for d in range(1, Z):
            along[k][d - 1].wait_recv()
            go(over[k][d])
        if k + 2 < len(chunks):
            ag_own(k + 2)

    def ag_finish(k):
        for copy in over[k]:
            copy.wait_recv()

    g1, g2, g3, g_finish = tile_sum(GT, GR)
    g1()
    sendA = [remote(SA.at[q], WA.at[own], dev) for dev, q in quad]
    sendB = [remote(SB.at[q], WB.at[own], dev) for dev, q in quad]
    for copy in sendA:
        go(copy)
    mine = idq.at[pl.ds(S * r, S)]
    sendI = [remote(mine, mine, dev) for dev, q in quad]
    for copy in sendI:
        go(copy)
    g2()
    for copy in sendA:
        copy.wait_recv()
    for k in range(4):
        ag_start(k)
        if k < 2:
            ag_own(k)
    for copy in sendI:
        copy.wait_recv()

    lane = lax.broadcasted_iota(jnp.int32, (L, 128), 1)
    sub = lax.broadcasted_iota(jnp.int32, (L, 128), 0)
    front = lax.rem(lane, 64) < 32
    low = lane < 64
    freq = jnp.exp(-math.log(10000.0) * lax.rem(lane, 32).astype(F32) / 32)
    CT, ST = R["CT"], R["ST"]

    def tables(q):
        times = jnp.broadcast_to(idq[q, 2:3, :], (L, L)).T
        angles = times * freq
        CT[at(L * q, L), :] = jnp.cos(angles)
        sine = jnp.sin(angles)
        ST[at(L * q, L), :] = jnp.where(front, -sine, sine)

    loop(2 * S, tables)
    g3()
    loop(2 * S, lambda q: tables(2 * S + q))
    for copy in sent[:3]:
        copy.wait_send()
    del sent[:3]
    GT[0] = g_finish()
    tok = R["tok"]
    step = 64

    def norm_in(i):
        x = tok[at(step * i, step), :].astype(F32)
        inv = lax.rsqrt(jnp.mean(x * x, axis=-1, keepdims=True) + EPSILON)
        h1Q[at(T * r + step * i, step), :] = (x * inv * GT[0, 0:1, :]).astype(BF16)

    loop(T // step, norm_in)

    def token_block(ref):
        return lambda role: ref.at[at(T * role, T)]

    h1_start, h1_forward, h1_finish = quad_gather(token_block(h1Q))
    dy_start, dy_forward, dy_finish = quad_gather(token_block(dyQ))
    att_start, att_forward, att_finish = quad_gather(lambda role: attQ.at[:, lanes(QC * role, QC)])
    wo_start, wo_forward, wo_finish = quad_gather(lambda role: WO.at[:, lanes(QC * role, QC)])
    h2_start, h2_forward, h2_finish = quad_gather(token_block(h2Q))
    h1_start()
    for copy in sendB:
        go(copy)
    ag_forward(0)
    h1_forward()
    ag_forward(1)
    for copy in sendB:
        copy.wait_recv()
    for k in range(4, 8):
        ag_start(k)
    dy_start()
    h1_finish()
    ag_finish(0)
    ag_finish(1)

    qraw, kraw, qr, kr, vb, PR = (R[k] for k in ("qraw", "kraw", "qr", "kr", "vb", "PR"))
    spot = lax.broadcasted_iota(jnp.int32, (1, 128), 1)
    bias = [
        [jnp.sum(jnp.where(spot == QC // 64 * r + h, small[4 + m : 5 + m, :], 0.0)) for h in range(QC // 64)]
        for m in range(2)
    ]

    def swap(v):
        return jnp.where(front, pltpu.roll(v, 96, 1), pltpu.roll(v, 32, 1))

    def per_head(v):
        first = jnp.sum(jnp.where(low, v, 0.0), axis=-1, keepdims=True)
        second = jnp.sum(jnp.where(low, 0.0, v), axis=-1, keepdims=True)
        return jnp.where(low, first, second)

    def project_heads(q):
        at_q = at(L * q, L)
        value = mm(h1Q[at_q, :], WA[:, 0 : 3 * QC])
        cosine, sine = CT[at_q, :], ST[at_q, :]
        for m, (raw, ready) in enumerate(((qraw, qr), (kraw, kr))):
            raw[at_q, :] = value[:, QC * m : QC * (m + 1)]
            for j in range(QC // 128):
                v = value[:, QC * m + 128 * j : QC * m + 128 * (j + 1)]
                inv = lax.rsqrt(per_head(v * v) / 64 + EPSILON)
                v = v * inv * small[2 + m : 3 + m, :]
                v = v * cosine + swap(v) * sine
                if m == 0:
                    v = v * 0.125
                ready[at_q, 128 * j : 128 * (j + 1)] = v.astype(BF16)
        vb[at_q, :] = value[:, 2 * QC : 3 * QC].astype(BF16)

    loop(4 * S, project_heads)
    WO[:, lanes(QC * r, QC)] = WA[:, 3 * QC : 4 * QC]
    wo_start()
    dy_forward()
    ag_forward(2)

    def masks(q):
        segment = jnp.broadcast_to(idq[q, 0:1, :], (L, L))
        variate = jnp.broadcast_to(idq[q, 1:2, :], (L, L))
        allowed = (segment == segment.T) & ((segment != 0.0) | (lane == sub))
        return allowed, variate == variate.T

    heads = [jnp.where(low, 1.0, 0.0).astype(BF16), jnp.where(low, 0.0, 1.0).astype(BF16)]

    def attend(q):
        at_q = at(L * q, L)
        allowed, same = masks(q)
        for j in range(QC // 128):
            tile = slice(128 * j, 128 * (j + 1))
            q2, k2, v2 = qr[at_q, tile], kr[at_q, tile], vb[at_q, tile]
            outs = []
            for h in range(2):
                head = 2 * j + h
                score = mm(q2 * heads[h], k2, NT) + jnp.where(same, bias[1][head], bias[0][head])
                score = jnp.where(allowed, score, -1000000000.0)
                e = jnp.exp(score - jnp.max(score, axis=-1, keepdims=True))
                p = e / jnp.sum(e, axis=-1, keepdims=True)
                PR[q, head] = p
                outs.append(mm(p.astype(BF16), v2))
            attQ[at_q, lanes(QC * r + 128 * j, 128)] = jnp.where(low, outs[0], outs[1]).astype(BF16)

    loop(4 * S, attend)
    att_start()
    ag_forward(3)
    wo_forward()
    ag_forward(4)
    att_forward()
    wo_finish()
    dy_finish()
    att_finish()

    x1, dx1, acc = R["x1"], R["dx1"], R["acc"]

    def mix(i):
        x = tok[at(step * i, step), :].astype(F32) + mm(attQ[at(T * r + step * i, step), :], WO[...])
        x1[at(step * i, step), :] = x
        inv = lax.rsqrt(jnp.mean(x * x, axis=-1, keepdims=True) + EPSILON)
        h2Q[at(T * r + step * i, step), :] = (x * inv * GT[0, 1:2, :]).astype(BF16)

    loop(T // step, mix)
    h2_start()
    ag_forward(5)
    ag_finish(2)
    ag_finish(3)
    h2_forward()
    ag_finish(4)
    ag_finish(5)

    hid, dgdu = R["hid"], R["dgdu"]

    def ffn(half, role):
        def body(i):
            at_i = at(T * role + L * i, L)
            both = mm(h2Q[at_i, :], WB[:, half * FC : (half + 1) * FC])
            gate, up = both[:, 0:HF], both[:, HF:FC]
            sigma = 1.0 / (1.0 + jnp.exp(-gate))
            silu = gate * sigma
            hid[at_i, half * HF : (half + 1) * HF] = (silu * up).astype(BF16)
            d_hidden = mm(dyQ[at_i, :], WC[half * HF : (half + 1) * HF, :], NT)
            d_gate = d_hidden * up * (sigma * (1.0 + gate * (1.0 - sigma)))
            dgdu[at_i, half * FC : half * FC + HF] = d_gate.astype(BF16)
            dgdu[at_i, half * FC + HF : (half + 1) * FC] = (d_hidden * silu).astype(BF16)

        loop(T // L, body)

    ffn(0, r)
    h2_finish()
    ffn(0, r_sib)
    ag_forward(6)
    ffn(0, r_par)
    ffn(0, r_dia)

    YS, YR, ZR, QS, QR = (R[k] for k in ("YS", "YR", "ZR", "QS", "QR"))
    y_sem, z_sem = [take(Z) for _ in range(4)], [take(Z - 1) for _ in range(4)]

    def gradient(unit, group, store):
        at_g = lanes(B * group, B)
        if unit == 0:
            store(slice(0, FC), mm(hid[:, at_g], dyQ[...], TN))
        elif unit < 3:
            store(slice(0, FC), mm(h2Q[:, at_g], dgdu[:, (unit - 1) * FC : unit * FC], TN))
        else:
            store(slice(0, 3 * QC), mm(h1Q[:, at_g], WC[:, 0 : 3 * QC], TN))
            store(slice(3 * QC, 4 * QC), mm(attQ[:, at_g], R["daR"][...], TN))

    slots = {1: 0, 2: 1, 0: 2, 3: 0}

    def y_copy(unit, i):
        return remote(YS.at[slots[unit], i], YR.at[unit, i], peer, y_sem[unit] + i)

    def z_copy(unit, i):
        return remote(YR.at[unit, i], ZR.at[unit, i - 1], z_dev(i), z_sem[unit] + i - 1)

    def order(unit, i):
        return lax.rem(i + Z - z, Z) if unit == 0 else (i + 1) % Z if isinstance(i, int) else lax.rem(i + 1, Z)

    def rs_first(unit, begin=0, count=Z, send=True):
        if unit == 3:
            for i in range(Z):
                y_copy(1, i).wait_send()

        def body(i):
            d = order(unit, begin + i)

            def store(cols, value):
                YS[slots[unit], d, :, cols] = value.astype(BF16)

            gradient(unit, 2 * at_z(d) + 1 - y, store)
            if send:
                y_copy(unit, d).start()

        loop(count, body)

    def rs_step(unit, i):
        d = order(unit, i)
        y_copy(unit, d).wait_recv()

        def store(cols, value):
            YR[unit, d, :, cols] = (value + YR[unit, d, :, cols].astype(F32)).astype(BF16)

        gradient(unit, 2 * at_z(d) + y, store)

        @pl.when(d != 0)
        def _():
            z_copy(unit, d).start()

    def rs_second(unit, begin=0, count=Z):
        loop(count, lambda i: rs_step(unit, begin + i))

    quad_copies = {}

    def rs_third(unit):
        for i in range(1, Z):
            z_copy(unit, i).wait_recv()
        width = 256
        for j in range(FC // width):
            cols = slice(width * j, width * (j + 1))
            value = YR[unit, 0, :, cols].astype(F32)
            for i in range(1, Z):
                value = value + ZR[unit, i - 1, :, cols].astype(F32)
            if unit == 0:
                R["gd"][:, cols] = value
            else:
                QS[unit - 1, :, cols] = value.astype(BF16)
        if unit:
            QR[unit - 1, r] = QS[unit - 1, at(rows * r, rows), :]
            quad_copies[unit] = [
                go(remote(QS.at[unit - 1, at(rows * q, rows)], QR.at[unit - 1, r], dev)) for dev, q in quad
            ]

    def rs_last(unit):
        for copy in quad_copies[unit]:
            copy.wait_recv()
        R["parts"][unit - 1] = QR[unit - 1]

    rsS, rsR = R["rsS"], R["rsR"]

    def quad_sum(kind, prepare_block, partial, fill=None):
        width = 512
        tiles = [slice(width * j, width * (j + 1)) for j in range(D // width)]
        copies = [
            remote(rsS.at[0], rsR.at[kind, 0], sib),
            remote(rsS.at[1], rsR.at[kind, 1], sib),
            remote(rsS.at[2], rsR.at[kind, 2], par),
        ]

        def blocks(role, store):
            def body(i):
                for cols in tiles:
                    store(at(L * i, L), cols, partial(at(T * role + L * i, L), cols))

            loop(T // L, body)

        def to_dia(at_i, cols, value):
            rsS[1, at_i, cols] = value.astype(BF16)

        def to_par(at_i, cols, value):
            rsS[2, at_i, cols] = (value + rsR[kind, 1, at_i, cols].astype(F32)).astype(BF16)

        def to_sib(at_i, cols, value):
            rsS[0, at_i, cols] = value.astype(BF16)

        def keep(at_i, cols, value):
            acc[at_i, cols] = value

        prepare_block(r_dia)
        blocks(r_dia, to_dia)
        copies[1].start()
        prepare_block(r_par)
        copies[1].wait_recv()
        blocks(r_par, to_par)
        copies[2].start()
        if fill:
            fill(0)
        prepare_block(r_sib)
        blocks(r_sib, to_sib)
        copies[0].start()
        if fill:
            fill(1)
        prepare_block(r)
        blocks(r, keep)

        def finish():
            copies[0].wait_recv()
            copies[2].wait_recv()
            for copy in copies:
                copy.wait_send()

        return finish

    def summed(kind, at_i):
        return acc[at_i, :] + (rsR[kind, 0, at_i, :].astype(F32) + rsR[kind, 2, at_i, :].astype(F32))

    def nothing(role):
        return None

    rs_first(1, send=False)
    ag_forward(7)
    for i in range(Z):
        y_copy(1, order(1, i)).start()
    rs_first(0, 0, Z // 2)
    ag_finish(6)
    ag_finish(7)
    h2_sum = quad_sum(
        0, functools.partial(ffn, 1), lambda at_i, cols: mm(dgdu[at_i, :], WB[cols, :], NT),
        lambda i: rs_second(1, i, 1),
    )
    rs_second(1, 2, 1)
    rs_first(2)
    h2_sum()

    TT, TR = R["TT"], R["TR"]
    daS, daR, dattS, dattR = (R[k] for k in ("daS", "daR", "dattS", "dattR"))
    TT[0] = jnp.zeros((8, D), F32)

    def norm_back(v, d_out, gain, row):
        inv = lax.rsqrt(jnp.mean(v * v, axis=-1, keepdims=True) + EPSILON)
        TT[0, row : row + 1, :] += jnp.sum(d_out * (v * inv), axis=0, keepdims=True)
        d = d_out * gain
        return inv * d - v * (inv * inv * inv * jnp.mean(d * v, axis=-1, keepdims=True))

    def mix_back(i):
        at_i = at(step * i, step)
        d = norm_back(x1[at_i, :], summed(0, at_i), GT[0, 1:2, :], 1)
        d = d + R["cot"][at_i, :].astype(F32)
        dx1[at_i, :] = d
        daS[at_i, :] = d.astype(BF16)

    loop(T // step, mix_back)
    sendD = [remote(daS.at[:, lanes(QC * q, QC)], daR.at[at(T * r, T)], dev) for dev, q in quad]
    sendT = [remote(dattS.at[:, lanes(QC * q, QC)], dattR.at[at(T * r, T)], dev) for dev, q in quad]

    def out_back(i):
        at_i = at(step * i, step)
        dattS[at_i, :] = mm(daS[at_i, :], WO[...], NT).astype(BF16)

    loop(T // step, out_back)
    for copy in sendT:
        go(copy)
    for copy in sendD:
        go(copy)
    dattR[at(T * r, T), :] = dattS[:, lanes(QC * r, QC)]
    daR[at(T * r, T), :] = daS[:, lanes(QC * r, QC)]
    rs_second(1, 3, 1)
    rs_first(0, Z // 2, Z // 2)
    rs_second(0, 0, Z // 2)
    out_sum = quad_sum(1, nothing, lambda at_i, cols: mm(hid[at_i, :], WC[:, cols]))
    for copy in along[2] + along[3] + over[2] + over[3]:
        copy.wait_send()
        sent[:] = [other for other in sent if other is not copy]
    for copy in sendT:
        copy.wait_recv()

    def write_out(i):
        at_i = at(step * i, step)
        R["act"][at_i, :] = (x1[at_i, :] + summed(1, at_i)).astype(BF16)

    HG, BG = R["HG"], R["BG"]
    HG[...] = jnp.zeros(HG.shape, F32)
    BG[...] = jnp.zeros(BG.shape, F32)

    def fold(v):
        return jnp.sum(v.reshape(L // 8, 8, 128), axis=0)

    def prepare_back(raw, d, m, j, cosine, sine, factor):
        if factor != 1.0:
            d = d * factor
        d = d * cosine - swap(d) * sine
        inv = lax.rsqrt(per_head(raw * raw) / 64 + EPSILON)
        HG[m, j] += fold(d * (raw * inv))
        d = d * small[2 + m : 3 + m, :]
        return inv * d - raw * (inv * inv * inv * (per_head(d * raw) / 64))

    def attend_back(q):
        at_q = at(L * q, L)
        _, same = masks(q)
        cosine, sine = CT[at_q, :], ST[at_q, :]
        for j in range(QC // 128):
            tile = slice(128 * j, 128 * (j + 1))
            q2, k2, v2, d2 = qr[at_q, tile], kr[at_q, tile], vb[at_q, tile], dattR[at_q, tile]
            dq, dk, dv = [], [], []
            for h in range(2):
                p = PR[q, 2 * j + h]
                dp = mm(d2 * heads[h], v2, NT)
                ds = (p * (dp - jnp.sum(p * dp, axis=-1, keepdims=True))).astype(BF16)
                wide = ds.astype(F32)
                BG[0, 2 * j + h] += fold(jnp.where(same, 0.0, wide))
                BG[1, 2 * j + h] += fold(jnp.where(same, wide, 0.0))
                dv.append(mm(p.astype(BF16), d2, TN))
                dq.append(mm(ds, k2))
                dk.append(mm(ds, q2, TN))
            d_query = jnp.where(low, dq[0], dq[1])
            d_key = jnp.where(low, dk[0], dk[1])
            d_query = prepare_back(qraw[at_q, tile], d_query, 0, j, cosine, sine, 0.125)
            d_key = prepare_back(kraw[at_q, tile], d_key, 1, j, cosine, sine, 1.0)
            WC[at_q, tile] = d_query.astype(BF16)
            WC[at_q, QC + 128 * j : QC + 128 * (j + 1)] = d_key.astype(BF16)
            WC[at_q, 2 * QC + 128 * j : 2 * QC + 128 * (j + 1)] = jnp.where(low, dv[0], dv[1]).astype(BF16)

    def attend_and_step(i):
        for q in range(S):
            attend_back(S * i + q)
        rs_step(2, i)

    loop(4, attend_and_step)
    for copy in sendD:
        copy.wait_recv()
    rs_first(3)
    out_sum()
    loop(T // step, write_out)
    in_sum = quad_sum(
        2, nothing, lambda at_i, cols: mm(WC[at_i, 0 : 3 * QC], WA[cols, 0 : 3 * QC], NT),
        lambda i: rs_second(0, Z // 2 + i, 1),
    )
    rs_third(1)
    in_sum()

    def input_back(i):
        at_i = at(step * i, step)
        d = norm_back(tok[at_i, :].astype(F32), summed(2, at_i), GT[0, 0:1, :], 0)
        R["ig"][at_i, :] = (dx1[at_i, :] + d).astype(BF16)

    loop(T // step, input_back)

    for m in range(2):
        value = HG[m, 0]
        for j in range(1, QC // 128):
            value = value + HG[m, j]
        TT[0, 2:3, 128 * m : 128 * (m + 1)] = jnp.sum(value, axis=0, keepdims=True)
    for m in range(2):
        line = jnp.zeros((1, 128), F32)
        for h in range(QC // 64):
            line = line + jnp.where(spot == QC // 64 * r + h, jnp.sum(BG[m, h]), 0.0)
        TT[0, 3 + m : 4 + m, 0:128] = line
    t1, t2, t3, t_finish = tile_sum(TT, TR)
    t1()
    rs_second(3, 0, 3)
    t2()
    rs_second(3, 3, 1)
    rs_third(2)
    rs_last(1)
    t3()
    rs_third(0)
    rs_third(3)
    rs_last(2)
    R["tot"][...] = t_finish()
    rs_last(3)
    for copy in sent:
        copy.wait_send()
    for unit in range(4):
        for i in range(Z):
            if unit != 1:
                y_copy(unit, i).wait_send()
            if i:
                z_copy(unit, i).wait_send()


LAST = ("act", "ig", "gq", "gk", "gv", "go", "gg", "gu", "gd", "ga", "gf", "ghq", "ghk", "gb")


def finishing(s, *refs):
    names = tuple(name + "_in" for name in OUTPUTS) + LAST
    R = dict(zip(names, refs, strict=True))
    D, rows, G, QC, FC, B, HD, H = (s[k] for k in ("D", "rows", "G", "QC", "FC", "B", "HD", "H"))
    HF = FC // 2
    for name in ("act", "ig", "gd"):
        R[name][...] = R[name + "_in"][...]
    parts = R["parts_in"]
    for q in range(4):
        for m, name in enumerate(("gq", "gk", "gv", "go")):
            R[name][:, QC * q : QC * (q + 1)] = parts[2, q, :, QC * m : QC * (m + 1)].astype(F32)
        for j in range(G):
            half, within = divmod(B * j, HF)
            target = slice(B * (4 * j + q), B * (4 * j + q) + B)
            R["gg"][:, target] = parts[half, q, :, within : within + B].astype(F32)
            R["gu"][:, target] = parts[half, q, :, HF + within : HF + within + B].astype(F32)
    tot = R["tot_in"]
    own = lax.axis_index("fsdp") * rows
    mine = pltpu.roll(tot[:, lanes(128 * lax.div(own, 128), 128)], lax.rem(128 - lax.rem(own, 128), 128), 1)
    R["ga"][...] = mine[0:1, 0:rows]
    R["gf"][...] = mine[1:2, 0:rows]
    both = tot[:, 0:256]
    both = both + pltpu.roll(both, 256 - HD, 1)
    R["ghq"][...] = both[2:3, 0:HD]
    R["ghk"][...] = both[2:3, 128 : 128 + HD]
    R["gb"][...] = tot[3:5, 0:H]


def layer(s, tokens, segment_ids, variate_ids, time_ids, w_query, w_key, w_value, w_out, w_gate, w_up, w_down,
          gain_attn, gain_ffn, gain_query, gain_key, variate_bias, cotangent):
    D, T, rows, B, FF, FC, HD, H = (s[k] for k in ("D", "T", "rows", "B", "FF", "FC", "HD", "H"))
    lines = [
        gain_attn[None], gain_ffn[None], jnp.tile(gain_query[None], (1, 2)), jnp.tile(gain_key[None], (1, 2)),
        variate_bias,
    ]
    small, line = jnp.zeros((8, 128), F32), 0
    for piece in lines:
        high, wide = piece.shape
        small = small + jnp.pad(piece.astype(F32), ((line, 8 - line - high), (0, 128 - wide)))
        line += high
    scratch = scratch_of(s)
    names = INPUTS + OUTPUTS + tuple(scratch)
    vmem = pl.BlockSpec(memory_space=pltpu.VMEM)

    def shape(*dims, kind=F32):
        return jax.ShapeDtypeStruct(dims, kind)

    tokens_shape = shape(T, D, kind=BF16)
    outs = pl.pallas_call(
        functools.partial(fused, s, names),
        out_shape=[tokens_shape, tokens_shape, shape(B, D), shape(3, 4, rows, FC, kind=BF16), shape(8, D)],
        in_specs=[vmem] * len(INPUTS),
        out_specs=[vmem] * len(OUTPUTS),
        scratch_shapes=list(scratch.values()),
        compiler_params=pltpu.CompilerParams(
            collective_id=0, has_side_effects=True, vmem_limit_bytes=64 << 20
        ),
        name="fused_layer",
    )(
        tokens.reshape(T, D), cotangent.reshape(T, D), segment_ids, variate_ids, time_ids,
        w_query, w_key, w_value, w_out, w_gate, w_up, w_down, small,
    )
    last = pl.pallas_call(
        functools.partial(finishing, s),
        out_shape=[tokens_shape, tokens_shape] + [shape(rows, D)] * 4 + [shape(rows, FF)] * 2
        + [shape(B, D), shape(1, rows), shape(1, rows), shape(1, HD), shape(1, HD), shape(2, H)],
        in_specs=[vmem] * len(OUTPUTS),
        out_specs=[vmem] * len(LAST),
        name="finishing",
    )(*outs)
    flat = [value.reshape(-1) for value in last[9:13]]
    return (last[0].reshape(tokens.shape), last[1].reshape(tokens.shape), *last[2:9], *flat, last[13])


def local(tokens, segment_ids, variate_ids, time_ids, *rest):
    s = sizes_of(lax.axis_size("fsdp"), tokens, rest[0], rest[4], rest[9], rest[11])
    chosen = functools.partial(layer, s) if fits(s) else plain
    return chosen(tokens, segment_ids, variate_ids, time_ids, *rest)


def solution(mesh):
    placed = (
        P("fsdp", None, None),
        P("fsdp", None),
        P("fsdp", None),
        P("fsdp", None),
        P("fsdp", None),
        P("fsdp", None),
        P("fsdp", None),
        P("fsdp", None),
        P("fsdp", None),
        P("fsdp", None),
        P("fsdp", None),
        P("fsdp"),
        P("fsdp"),
        P(),
        P(),
        P(),
        P("fsdp", None, None),
    )
    return jax.shard_map(
        local,
        mesh=mesh,
        in_specs=placed,
        out_specs=(
            P("fsdp", None, None),
            P("fsdp", None, None),
            P("fsdp", None),
            P("fsdp", None),
            P("fsdp", None),
            P("fsdp", None),
            P("fsdp", None),
            P("fsdp", None),
            P("fsdp", None),
            P("fsdp"),
            P("fsdp"),
            P(),
            P(),
            P(),
        ),
        check_vma=False,
    )
```

```python
import functools
import math

import jax
import jax.numpy as jnp
from jax import lax
from jax.experimental import pallas as pl
from jax.experimental.pallas import tpu as pltpu
from jax.sharding import PartitionSpec as P

EPSILON = 1e-05


def normalize(values, scale_gain):
    return (
        values * lax.rsqrt(jnp.mean(values * values, axis=-1, keepdims=True) + EPSILON) * scale_gain
    )


def rotate(values, moments):
    halfway = values.shape[-1] // 2
    frequency = jnp.exp(-math.log(10000.0) * jnp.arange(halfway).astype(jnp.float32) / halfway)
    angles = moments.astype(jnp.float32)[:, None] * frequency[None, :]
    cosine = jnp.cos(angles)[:, None, :]
    sine_part = jnp.sin(angles)[:, None, :]
    former = values[..., :halfway]
    latter = values[..., halfway:]
    return jnp.concatenate(
        [former * cosine - latter * sine_part, former * sine_part + latter * cosine], axis=-1
    )


def prepare(raw_heads, head_gain, moments, factor):
    return rotate(normalize(raw_heads, head_gain), moments) * factor


def swiglu(gate_act, up_act):
    return jax.nn.silu(gate_act) * up_act


def attention_masks(segments, variates):
    length = segments.shape[0]
    diagonal = jnp.arange(length)[:, None] == jnp.arange(length)[None, :]
    allowed = (segments[:, None] == segments[None, :]) & ((segments[None, :] != 0) | diagonal)
    same_var = variates[:, None] == variates[None, :]
    return (allowed, same_var)


def scoring(q_rot, k_rot, bias_table, allowed, same_var):
    scores = jnp.einsum("qhe,khe->hqk", q_rot, k_rot, preferred_element_type=jnp.float32)
    scores = scores + jnp.where(
        same_var[None], bias_table[1][:, None, None], bias_table[0][:, None, None]
    )
    return jnp.where(allowed[None], scores, -1000000000.0)


def project(left, right):
    return jnp.dot(left, right, preferred_element_type=jnp.float32)


def across(left, right):
    return lax.dot_general(
        left, right, (((0,), (0,)), ((), ())), preferred_element_type=jnp.float32
    )


def against(left, weight):
    return lax.dot_general(
        left, weight, (((1,), (1,)), ((), ())), preferred_element_type=jnp.float32
    )


def forward(inputs_low, weights, side_params, segments, variates, moments):
    w_query, w_key, w_value, w_out, w_gate, w_up, w_down, gain_attn, gain_ffn = weights
    gain_query, gain_key, bias_table = side_params
    length, model_width = inputs_low.shape
    head_count = bias_table.shape[1]
    head_dim = gain_query.shape[0]
    inputs = inputs_low.astype(jnp.float32)
    normed = normalize(inputs, gain_attn.astype(jnp.float32)).astype(jnp.bfloat16)
    queries = project(normed, w_query).reshape(length, head_count, head_dim)
    key_raw = project(normed, w_key).reshape(length, head_count, head_dim)
    v_low = project(normed, w_value).reshape(length, head_count, head_dim).astype(jnp.bfloat16)
    q_rot = prepare(queries, gain_query, moments, head_dim ** (-0.5)).astype(jnp.bfloat16)
    k_rot = prepare(key_raw, gain_key, moments, 1.0).astype(jnp.bfloat16)
    allowed, same_var = attention_masks(segments, variates)
    scores = scoring(q_rot, k_rot, bias_table, allowed, same_var)
    maximum = jnp.max(scores, axis=-1, keepdims=True)
    exponent = jnp.exp(scores - maximum)
    row_total = jnp.sum(exponent, axis=-1, keepdims=True)
    log_total = maximum + jnp.log(row_total)
    softmax_probs = (exponent / row_total).astype(jnp.bfloat16)
    attended = jnp.einsum("hqk,khe->qhe", softmax_probs, v_low, preferred_element_type=jnp.float32)
    attended = attended.reshape(length, model_width).astype(jnp.bfloat16)
    mixed_state = inputs + project(attended, w_out)
    normed_ffn = normalize(mixed_state, gain_ffn.astype(jnp.float32)).astype(jnp.bfloat16)
    gate_act = project(normed_ffn, w_gate)
    up_act = project(normed_ffn, w_up)
    hidden = swiglu(gate_act, up_act).astype(jnp.bfloat16)
    result = mixed_state + project(hidden, w_down)
    kept_state = (
        inputs,
        normed,
        queries,
        key_raw,
        q_rot,
        k_rot,
        v_low,
        log_total,
        attended,
        mixed_state,
        normed_ffn,
        gate_act,
        up_act,
        hidden,
    )
    return (result, kept_state)


def backward(upstream, kept_state, weights, side_params, segments, variates, moments):
    (
        inputs,
        normed,
        queries,
        key_raw,
        q_rot,
        k_rot,
        v_low,
        log_total,
        attended,
        mixed_state,
        normed_ffn,
        gate_act,
        up_act,
        hidden,
    ) = kept_state
    w_query, w_key, w_value, w_out, w_gate, w_up, w_down, gain_attn, gain_ffn = weights
    gain_query, gain_key, bias_table = side_params
    length, head_count, head_dim = queries.shape
    grad_down = across(hidden, upstream)
    d_hidden = against(upstream, w_down)
    _, pullback = jax.vjp(swiglu, gate_act, up_act)
    d_gate, d_up = pullback(d_hidden)
    d_gate = d_gate.astype(jnp.bfloat16)
    d_up = d_up.astype(jnp.bfloat16)
    grad_gate = across(normed_ffn, d_gate)
    grad_up = across(normed_ffn, d_up)
    d_normed_ffn = against(d_gate, w_gate) + against(d_up, w_up)
    _, pullback = jax.vjp(normalize, mixed_state, gain_ffn.astype(jnp.float32))
    d_mixed, grad_gain_ffn = pullback(d_normed_ffn)
    d_mixed = d_mixed + upstream.astype(jnp.float32)
    d_branch = d_mixed.astype(jnp.bfloat16)
    grad_out = across(attended, d_branch)
    d_attended = against(d_branch, w_out).astype(jnp.bfloat16).reshape(length, head_count, head_dim)
    allowed, same_var = attention_masks(segments, variates)
    scores = scoring(q_rot, k_rot, bias_table, allowed, same_var)
    softmax_probs = jnp.exp(scores - log_total)
    d_probs = jnp.einsum("qhe,khe->hqk", d_attended, v_low, preferred_element_type=jnp.float32)
    d_values = jnp.einsum(
        "hqk,qhe->khe",
        softmax_probs.astype(jnp.bfloat16),
        d_attended,
        preferred_element_type=jnp.float32,
    )
    d_values = d_values.reshape(length, head_count * head_dim).astype(jnp.bfloat16)
    weighted = jnp.sum(softmax_probs * d_probs, axis=-1, keepdims=True)
    d_scores = (softmax_probs * (d_probs - weighted)).astype(jnp.bfloat16)
    d_float = d_scores.astype(jnp.float32)
    same_sum = jnp.sum(jnp.where(same_var[None], d_float, 0.0), axis=(1, 2))
    other_sum = jnp.sum(jnp.where(same_var[None], 0.0, d_float), axis=(1, 2))
    grad_bias = jnp.stack([other_sum, same_sum])
    d_qrot = jnp.einsum("hqk,khe->qhe", d_scores, k_rot, preferred_element_type=jnp.float32)
    d_krot = jnp.einsum("hqk,qhe->khe", d_scores, q_rot, preferred_element_type=jnp.float32)
    factor = head_dim ** (-0.5)
    _, pullback = jax.vjp(
        lambda raw_heads, head_gain: prepare(raw_heads, head_gain, moments, factor),
        queries,
        gain_query,
    )
    d_queries, grad_gain_query = pullback(d_qrot)
    _, pullback = jax.vjp(
        lambda raw_heads, head_gain: prepare(raw_heads, head_gain, moments, 1.0), key_raw, gain_key
    )
    d_keys, grad_gain_key = pullback(d_krot)
    d_queries = d_queries.reshape(length, head_count * head_dim).astype(jnp.bfloat16)
    d_keys = d_keys.reshape(length, head_count * head_dim).astype(jnp.bfloat16)
    grad_query = across(normed, d_queries)
    grad_key = across(normed, d_keys)
    grad_value = across(normed, d_values)
    d_normed = against(d_queries, w_query) + against(d_keys, w_key) + against(d_values, w_value)
    _, pullback = jax.vjp(normalize, inputs, gain_attn.astype(jnp.float32))
    d_inputs, grad_gain_attn = pullback(d_normed)
    row_grads = jnp.concatenate(
        [grad_query, grad_key, grad_value, grad_out, grad_gate, grad_up], axis=1
    )
    small = (grad_gain_query, grad_gain_key, grad_bias, grad_gain_attn, grad_gain_ffn)
    return (d_inputs + d_mixed, row_grads, grad_down, small)


def plain(
    tokens,
    segment_ids,
    variate_ids,
    time_ids,
    w_query,
    w_key,
    w_value,
    w_out,
    w_gate,
    w_up,
    w_down,
    gain_attn,
    gain_ffn,
    gain_query,
    gain_key,
    variate_bias,
    cotangent,
):
    devices = lax.axis_size("fsdp")
    owner = lax.axis_index("fsdp")
    width = w_query.shape[1]
    hidden_width = w_gate.shape[1]
    own_rows = w_query.shape[0]
    own_down = w_down.shape[0]
    side_params = (
        gain_query.astype(jnp.float32),
        gain_key.astype(jnp.float32),
        variate_bias.astype(jnp.float32),
    )
    rows_total = jnp.zeros((own_rows * devices, 4 * width + 2 * hidden_width), jnp.float32)
    down_total = jnp.zeros((own_down * devices, width), jnp.float32)
    side_totals = (
        jnp.zeros(gain_query.shape, jnp.float32),
        jnp.zeros(gain_key.shape, jnp.float32),
        jnp.zeros(variate_bias.shape, jnp.float32),
        jnp.zeros((own_rows * devices,), jnp.float32),
        jnp.zeros((own_rows * devices,), jnp.float32),
    )
    results = []
    input_grads = []
    for micro_index in range(tokens.shape[0]):
        segments = segment_ids[micro_index]
        variates = variate_ids[micro_index]
        moments = time_ids[micro_index]
        forward_weights = (
            lax.all_gather(w_query, "fsdp", axis=0, tiled=True),
            lax.all_gather(w_key, "fsdp", axis=0, tiled=True),
            lax.all_gather(w_value, "fsdp", axis=0, tiled=True),
            lax.all_gather(w_out, "fsdp", axis=0, tiled=True),
            lax.all_gather(w_gate, "fsdp", axis=0, tiled=True),
            lax.all_gather(w_up, "fsdp", axis=0, tiled=True),
            lax.all_gather(w_down, "fsdp", axis=0, tiled=True),
            lax.all_gather(gain_attn, "fsdp", axis=0, tiled=True),
            lax.all_gather(gain_ffn, "fsdp", axis=0, tiled=True),
        )
        result, kept_state = forward(
            tokens[micro_index], forward_weights, side_params, segments, variates, moments
        )
        results.append(result.astype(jnp.bfloat16))
        backward_weights = (
            lax.all_gather(w_query, "fsdp", axis=0, tiled=True),
            lax.all_gather(w_key, "fsdp", axis=0, tiled=True),
            lax.all_gather(w_value, "fsdp", axis=0, tiled=True),
            lax.all_gather(w_out, "fsdp", axis=0, tiled=True),
            lax.all_gather(w_gate, "fsdp", axis=0, tiled=True),
            lax.all_gather(w_up, "fsdp", axis=0, tiled=True),
            lax.all_gather(w_down, "fsdp", axis=0, tiled=True),
            lax.all_gather(gain_attn, "fsdp", axis=0, tiled=True),
            lax.all_gather(gain_ffn, "fsdp", axis=0, tiled=True),
        )
        d_inputs, row_grads, down_grads, small = backward(
            cotangent[micro_index],
            kept_state,
            backward_weights,
            side_params,
            segments,
            variates,
            moments,
        )
        input_grads.append(d_inputs.astype(jnp.bfloat16))
        rows_total = rows_total + row_grads
        down_total = down_total + down_grads
        side_totals = tuple((running + fresh for running, fresh in zip(side_totals, small)))
    owned_rows = lax.psum_scatter(rows_total, "fsdp", scatter_dimension=0, tiled=True)
    owned_down = lax.psum_scatter(down_total, "fsdp", scatter_dimension=0, tiled=True)
    shared = lax.psum(
        (side_totals[0], side_totals[1], side_totals[2], side_totals[3], side_totals[4]), "fsdp"
    )
    gain_attn_own = lax.dynamic_slice_in_dim(shared[3], owner * own_rows, own_rows, 0)
    gain_ffn_own = lax.dynamic_slice_in_dim(shared[4], owner * own_rows, own_rows, 0)
    grad_query = owned_rows[:, 0:width]
    grad_key = owned_rows[:, width : 2 * width]
    grad_value = owned_rows[:, 2 * width : 3 * width]
    grad_out = owned_rows[:, 3 * width : 4 * width]
    grad_gate = owned_rows[:, 4 * width : 4 * width + hidden_width]
    grad_up = owned_rows[:, 4 * width + hidden_width :]
    return (
        jnp.stack(results),
        jnp.stack(input_grads),
        grad_query,
        grad_key,
        grad_value,
        grad_out,
        grad_gate,
        grad_up,
        owned_down,
        gain_attn_own,
        gain_ffn_own,
        shared[0],
        shared[1],
        shared[2],
    )


F32 = jnp.float32
BF16 = jnp.bfloat16
MESH = pl.DeviceIdType.MESH
NT = (((1,), (1,)), ((), ()))
TN = (((0,), (0,)), ((), ()))


def mm(left, right, dims=(((1,), (0,)), ((), ()))):
    return lax.dot_general(left, right, dims, preferred_element_type=F32)


def at(start, size):
    return pl.ds(pl.multiple_of(start, size), size)


def lanes(start, size):
    return pl.ds(pl.multiple_of(start, 128), size)


def loop(count, body):
    lax.fori_loop(0, count, lambda i, carry: (body(i), carry)[1], 0)


def sizes_of(devices, tokens, w_query, w_gate, gain_query, bias):
    seqs, length, width = tokens.shape
    own_rows, hidden = w_query.shape[0], w_gate.shape[1]
    return dict(
        n=devices, S=seqs, L=length, D=width, FF=hidden, rows=own_rows, T=seqs * length,
        G=devices // 4, Z=devices // 8, QC=width // 4, FC=hidden // 4, B=4 * own_rows,
        HD=gain_query.shape[0], H=bias.shape[1],
    )


def fits(s):
    return (
        s["n"] % 8 == 0 and s["rows"] % 16 == 0 and s["L"] == 128 and s["HD"] == 64
        and s["H"] * s["HD"] == s["D"] and s["QC"] % 128 == 0 and s["FF"] == 4 * s["D"]
        and s["B"] == 128 and s["FC"] // 2 % s["B"] == 0 and s["FC"] == s["D"]
    )


def scratch_of(s):
    n, S, L, D, rows, T, G, Z, QC, FC, B = (
        s[k] for k in ("n", "S", "L", "D", "rows", "T", "G", "Z", "QC", "FC", "B")
    )
    Q = 4 * T
    vm = pltpu.VMEM
    return dict(
        WA=vm((D, 4 * QC), BF16), WB=vm((D, 2 * FC), BF16), WC=vm((FC, D), BF16), WO=vm((D, D), BF16),
        SA=vm((4, rows, 4 * QC), BF16), SB=vm((4, rows, 2 * FC), BF16),
        h1Q=vm((Q, D), BF16), dyQ=vm((Q, D), BF16), attQ=vm((Q, D), BF16), h2Q=vm((Q, D), BF16),
        qraw=vm((Q, QC), F32), kraw=vm((Q, QC), F32),
        qr=vm((Q, QC), BF16), kr=vm((Q, QC), BF16), vb=vm((Q, QC), BF16),
        PR=vm((4 * S, QC // 64, L, L), F32), CT=vm((Q, 128), F32), ST=vm((Q, 128), F32),
        x1=vm((T, D), F32), dx1=vm((T, D), F32), acc=vm((T, D), F32),
        hid=vm((Q, FC), BF16), dgdu=vm((Q, 2 * FC), BF16),
        rsS=vm((3, T, D), BF16), rsR=vm((3, 3, T, D), BF16),
        daS=vm((T, D), BF16), daR=vm((Q, QC), BF16), dattS=vm((T, D), BF16), dattR=vm((Q, QC), BF16),
        YS=vm((3, Z, B, FC), BF16), YR=vm((4, Z, B, FC), BF16), ZR=vm((4, Z - 1, B, FC), BF16), ZX=vm((4, B, FC), BF16),
        QS=vm((3, B, FC), BF16), QR=vm((3, 4, rows, FC), BF16),
        idq=vm((4 * S, 8, L), F32),
        SW=vm((4, rows, D), BF16), SG=vm((2, rows, s["FF"]), BF16), TK=vm((T, D), BF16),
        GQ=vm((4, 8, B), F32), GA=vm((8, D), F32), load=pltpu.SemaphoreType.DMA((9,)),
        TT=vm((3, 8, D), F32), TR=vm((4 + Z, 8, D), F32),
        HG=vm((4, QC // 128, 8, 128), F32), BG=vm((2, QC // 64, 8, 128), F32),
        send=pltpu.SemaphoreType.DMA((192,)), recv=pltpu.SemaphoreType.DMA((192,)),
    )


INPUTS = (
    "tok", "cot", "seg", "var", "tim", "wq", "wk", "wv", "wo", "wg", "wu", "wd", "small",
)
OUTPUTS = ("act", "ig", "gd", "parts", "tot")


def fused(s, names, *refs):
    R = dict(zip(names, refs, strict=True))
    n, S, L, D, rows, T, G, Z, QC, FC, B = (
        s[k] for k in ("n", "S", "L", "D", "rows", "T", "G", "Z", "QC", "FC", "B")
    )
    HF = FC // 2
    Q = 4 * T
    me = lax.axis_index("fsdp")
    r, c, xx, g = lax.rem(me, 4), lax.rem(me, 2), lax.rem(lax.div(me, 2), 2), lax.div(me, 4)
    y, z = lax.rem(g, 2), lax.div(g, 2)
    r_sib, r_par = r + 1 - 2 * c, r + 2 - 4 * xx
    r_dia = r_sib + 2 - 4 * xx
    sib, par, dia = me - r + r_sib, me - r + r_par, me - r + r_dia
    peer = me + 4 - 8 * y
    quad = ((sib, r_sib), (par, r_par), (dia, r_dia))

    def at_z(step):
        return lax.rem(z + step, Z)

    def z_dev(step):
        return at_z(step) * 8 + y * 4 + r

    def z_src(step):
        return lax.rem(z + Z - step, Z)

    relays = Z == 4
    inner, outer = lax.rem(z + 1, 4) >= 2, lax.rem(z + 1, 4) < 2

    def nearby(step, action):
        if relays and step != 2:
            pl.when(z != (Z - 1 if step == 1 else 0))(action)
        else:
            action()

    used = [0]
    sent = []

    def take(count=1):
        used[0] += count
        return used[0] - count

    def remote(src, dst, device, sem=None, arrival=None):
        sem = take() if sem is None else sem
        arrival = sem if arrival is None else arrival
        return pltpu.make_async_remote_copy(
            src_ref=src, dst_ref=dst, send_sem=R["send"].at[sem], recv_sem=R["recv"].at[arrival],
            device_id=(device,), device_id_type=MESH,
        )

    def go(copy):
        copy.start()
        sent.append(copy)
        return copy

    barrier = pltpu.get_barrier_semaphore()
    others = [sib, par, dia, peer] + [z_dev(d) for d in range(1, Z)]
    for device in others:
        pl.semaphore_signal(barrier, inc=1, device_id=(device,), device_id_type=MESH)

    SA, SB, SW, SG, WA, WB, WC, WO = (R[k] for k in ("SA", "SB", "SW", "SG", "WA", "WB", "WC", "WO"))
    dyQ, h1Q, h2Q, attQ, tok = R["dyQ"], R["h1Q"], R["h2Q"], R["attQ"], R["TK"]
    places = [("wq", SW.at[0]), ("wk", SW.at[1]), ("wv", SW.at[2]), ("wo", SW.at[3]), ("wd", WC.at[at(B * g, B)])]
    places += [("tok", tok), ("wg", SG.at[0]), ("wu", SG.at[1]), ("cot", dyQ.at[at(T * r, T)])]
    loads = {}
    for i, (name, place) in enumerate(places):
        loads[name] = pltpu.make_async_copy(R[name], place, R["load"].at[i])
        loads[name].start()
    own = at(B * g + rows * r, rows)
    idq, small, GQ, GA = R["idq"], R["small"], R["GQ"], R["GA"]
    for q in range(S):
        idq[S * r + q, 0:1, :] = R["seg"][q : q + 1, :].astype(F32)
        idq[S * r + q, 1:2, :] = R["var"][q : q + 1, :].astype(F32)
        idq[S * r + q, 2:3, :] = R["tim"][q : q + 1, :].astype(F32)
        idq[S * r + q, 3:8, :] = jnp.zeros((5, L), F32)
    GQ[r] = pltpu.roll(small[...], rows * r, 1)
    for m, name in enumerate(("wq", "wk", "wv", "wo")):
        loads[name].wait()
        for q in range(4):
            SA[q, :, QC * m : QC * (m + 1)] = SW[m, :, QC * q : QC * (q + 1)]
    WA[own, :] = SA[r]
    pl.semaphore_wait(barrier, len(others))

    def tile_sum(tile, got):
        first = [remote(tile.at[0], got.at[i], dev) for i, (dev, _) in enumerate(quad)]
        second = [remote(tile.at[1], got.at[4 + z], z_dev(d)) for d in range(1, Z)]
        third = remote(tile.at[2], got.at[3], peer)

        def round1():
            for copy in first:
                go(copy)

        def round2():
            for copy in first:
                copy.wait_recv()
            value = (tile[0] + got[0]) + (got[1] + got[2])
            tile[1] = value
            got[4 + z] = value
            for copy in second:
                go(copy)

        def round3():
            for copy in second:
                copy.wait_recv()
            value = got[4]
            for i in range(1, Z):
                value = value + got[4 + i]
            tile[2] = value
            go(third)

        def finish():
            third.wait_recv()
            return tile[2] + got[3]

        return round1, round2, round3, finish

    def quad_gather(block):
        to_sib, to_par = remote(block(r), block(r), sib), remote(block(r), block(r), par)
        passed = remote(block(r_par), block(r_par), sib)

        def start():
            go(to_par)
            go(to_sib)

        def forward():
            to_par.wait_recv()
            go(passed)

        def finish():
            to_sib.wait_recv()
            passed.wait_recv()

        return start, forward, finish

    chunks = [(WA, 0, 2 * QC), (WA, 2 * QC, 2 * QC), (WC, 0, D // 2), (WC, D // 2, D // 2)]
    chunks += [(WB, HF * k, HF) for k in range(4)] + [(GA, 0, B)]
    early, after = 3, {0: 2, 2: 4, 3: 5, 4: 6, 5: 7}

    def piece(k, group):
        ref, start, size = chunks[k]
        if ref is GA:
            return ref.at[:, lanes(B * group, B)]
        return ref.at[at(B * group, B), pl.ds(start, size)]

    a_sem, f_sem, o_sem = ([take(size) for _ in chunks] for size in (Z - 1, 1, Z))
    b_sem, e_sem = take(Z - 1), take()

    def across_y(other):
        return y + other * (1 - 2 * y)

    def along(k, d, other=0):
        block = piece(k, 2 * z + across_y(other))
        return remote(block, block, z_dev(d), (b_sem if other else a_sem[k]) + d - 1)

    def over(k, d):
        block = piece(k, 2 * z_src(d) + y)
        return remote(block, block, peer, o_sem[k] + d)

    def relay(k, other=0):
        block, end = piece(k, 2 * z_src(2) + across_y(other)), lax.div(z, 2)
        sems = (e_sem, b_sem + 2 * end) if other else (f_sem[k], a_sem[k] + 2 * end)
        return remote(block, block, 3 * end * 8 + y * 4 + r, *sems)

    def near(k, d, action):
        if k == 8:
            action()
        else:
            nearby(d, action)

    def both(k):
        return (0, 1) if k == early else (0,)

    def ag_start(k):
        for other in both(k):
            for d in range(1, Z):
                near(k, d, along(k, d, other).start)

    def ag_own(k):
        over(k, 0).start()

    def ag_forward(k):
        first = lax.div(3 - z, 3)
        for i in range(1, Z):
            d = i if not relays or i == 2 else 1 + 2 * first if i == 1 else 3 - 2 * first
            for other in both(k):
                along(k, d, other).wait_recv()
                if relays and i == 2 and k < 8:
                    pl.when(inner)(relay(k, other).start)
            if k != early:
                over(k, d).start()
        if k in after:
            ag_own(after[k])
        if 2 <= k <= 4:
            ag_start(k + 3)

    def ag_finish(k):
        for d in range(Z):
            if k != early:
                over(k, d).wait_recv()

    def ag_drain(k):
        for d in range(1 if k == early else Z):
            over(k, d).wait_send()
        for other in both(k):
            for d in range(1, Z):
                near(k, d, along(k, d, other).wait_send)
            if relays and k < 8:
                pl.when(inner)(relay(k, other).wait_send)

    sendG = [remote(GQ.at[r], GQ.at[r], dev) for dev, q in quad]
    sendA = [remote(SA.at[q], WA.at[own], dev) for dev, q in quad]
    sendB = [remote(SB.at[q], WB.at[own], dev) for dev, q in quad]
    mine = idq.at[pl.ds(S * r, S)]
    sendI = [remote(mine, mine, dev) for dev, q in quad]
    for copy in sendG + sendA + sendI:
        go(copy)
    loads["wd"].wait()
    ag_own(early)
    for copy in sendG:
        copy.wait_recv()
    GA[:, lanes(B * g, B)] = (GQ[0] + GQ[1]) + (GQ[2] + GQ[3])
    ag_start(8)
    ag_own(8)
    for copy in sendA:
        copy.wait_recv()
    ag_start(0)
    ag_own(0)
    ag_start(1)
    ag_own(1)
    ag_start(2)
    for copy in sendI:
        copy.wait_recv()

    lane = lax.broadcasted_iota(jnp.int32, (L, 128), 1)
    sub = lax.broadcasted_iota(jnp.int32, (L, 128), 0)
    front = lax.rem(lane, 64) < 32
    low = lane < 64
    freq = jnp.exp(-math.log(10000.0) * lax.rem(lane, 32).astype(F32) / 32)
    CT, ST = R["CT"], R["ST"]

    def tables(q):
        times = jnp.broadcast_to(idq[q, 2:3, :], (L, L)).T
        angles = times * freq
        CT[at(L * q, L), :] = jnp.cos(angles)
        sine = jnp.sin(angles)
        ST[at(L * q, L), :] = jnp.where(front, -sine, sine)

    loop(2 * S, tables)
    ag_forward(8)
    loop(2 * S, lambda q: tables(2 * S + q))
    loads["tok"].wait()
    ag_finish(8)
    step = 64

    def norm_in(i):
        x = tok[at(step * i, step), :].astype(F32)
        inv = lax.rsqrt(jnp.mean(x * x, axis=-1, keepdims=True) + EPSILON)
        h1Q[at(T * r + step * i, step), :] = (x * inv * GA[0:1, :]).astype(BF16)

    loop(T // step, norm_in)

    def token_block(ref):
        return lambda role: ref.at[at(T * role, T)]

    h1_start, h1_forward, h1_finish = quad_gather(token_block(h1Q))
    dy_start, dy_forward, dy_finish = quad_gather(token_block(dyQ))

    def att_block(chip, role):
        return attQ.at[at(2 * T * chip, 2 * T), lanes(QC * role, QC)]

    def att_copy(chip, role, device):
        return remote(att_block(chip, role), att_block(chip, role), device)

    needed, passed = att_copy(1 - xx, r, par), att_copy(xx, r_par, sib)
    near_needed, near_rest = att_copy(xx, r, sib), att_copy(1 - xx, r, sib)
    rest, passed_rest = att_copy(xx, r, par), att_copy(1 - xx, r_par, sib)
    wo_start, wo_forward, wo_finish = quad_gather(lambda role: WO.at[:, lanes(QC * role, QC)])
    h2_start, h2_forward, h2_finish = quad_gather(token_block(h2Q))
    h1_start()
    for name in ("wg", "wu"):
        loads[name].wait()
    for q in range(4):
        for j in range(G):
            half, within = divmod(B * j, HF)
            source = slice(B * (4 * j + q), B * (4 * j + q) + B)
            SB[q, :, half * FC + within : half * FC + within + B] = SG[0, :, source]
            SB[q, :, half * FC + HF + within : half * FC + HF + within + B] = SG[1, :, source]
    WB[own, :] = SB[r]
    for copy in sendB:
        go(copy)
    ag_forward(0)
    over(early, 0).wait_recv()
    ag_start(early)
    h1_forward()
    ag_forward(1)
    for copy in sendB:
        copy.wait_recv()
    ag_start(4)
    loads["cot"].wait()
    dy_start()
    h1_finish()
    ag_finish(0)
    ag_finish(1)
    ag_forward(2)

    qraw, kraw, qr, kr, vb, PR = (R[k] for k in ("qraw", "kraw", "qr", "kr", "vb", "PR"))
    spot = lax.broadcasted_iota(jnp.int32, (1, 128), 1)
    bias = [
        [jnp.sum(jnp.where(spot == QC // 64 * r + h, small[4 + m : 5 + m, :], 0.0)) for h in range(QC // 64)]
        for m in range(2)
    ]

    def swap(v):
        return jnp.where(front, pltpu.roll(v, 96, 1), pltpu.roll(v, 32, 1))

    def per_head(v):
        first = jnp.sum(jnp.where(low, v, 0.0), axis=-1, keepdims=True)
        second = jnp.sum(jnp.where(low, 0.0, v), axis=-1, keepdims=True)
        return jnp.where(low, first, second)

    def project_heads(q):
        at_q = at(L * q, L)
        value = mm(h1Q[at_q, :], WA[:, 0 : 3 * QC])
        cosine, sine = CT[at_q, :], ST[at_q, :]
        for m, (raw, ready) in enumerate(((qraw, qr), (kraw, kr))):
            raw[at_q, :] = value[:, QC * m : QC * (m + 1)]
            for j in range(QC // 128):
                v = value[:, QC * m + 128 * j : QC * m + 128 * (j + 1)]
                inv = lax.rsqrt(per_head(v * v) / 64 + EPSILON)
                v = v * inv * small[2 + m : 3 + m, :]
                v = v * cosine + swap(v) * sine
                if m == 0:
                    v = v * 0.125
                ready[at_q, 128 * j : 128 * (j + 1)] = v.astype(BF16)
        vb[at_q, :] = value[:, 2 * QC : 3 * QC].astype(BF16)

    loop(4 * S, project_heads)
    WO[:, lanes(QC * r, QC)] = WA[:, 3 * QC : 4 * QC]
    wo_start()
    dy_forward()

    def masks(q):
        segment = jnp.broadcast_to(idq[q, 0:1, :], (L, L))
        variate = jnp.broadcast_to(idq[q, 1:2, :], (L, L))
        allowed = (segment == segment.T) & ((segment != 0.0) | (lane == sub))
        return allowed, variate == variate.T

    heads = [jnp.where(low, 1.0, 0.0).astype(BF16), jnp.where(low, 0.0, 1.0).astype(BF16)]

    def attend(q):
        at_q = at(L * q, L)
        allowed, same = masks(q)
        for j in range(QC // 128):
            tile = slice(128 * j, 128 * (j + 1))
            q2, k2, v2 = qr[at_q, tile], kr[at_q, tile], vb[at_q, tile]
            outs = []
            for h in range(2):
                head = 2 * j + h
                score = mm(q2 * heads[h], k2, NT) + jnp.where(same, bias[1][head], bias[0][head])
                score = jnp.where(allowed, score, -1000000000.0)
                e = jnp.exp(score - jnp.max(score, axis=-1, keepdims=True))
                p = e / jnp.sum(e, axis=-1, keepdims=True)
                PR[q, head] = p
                outs.append(mm(p.astype(BF16), v2))
            attQ[at_q, lanes(QC * r + 128 * j, 128)] = jnp.where(low, outs[0], outs[1]).astype(BF16)

    loop(2 * S, lambda q: attend(2 * S * (1 - xx) + q))
    go(needed)
    ag_forward(3)
    loop(2 * S, lambda q: attend(2 * S * xx + q))
    go(near_needed)
    go(near_rest)
    ZR = R["ZR"]
    if relays:
        for k, end in ((0, 0), (2, 3)):

            @pl.when(z == end)
            def _():
                for unit in range(4):
                    ZR[unit, k] = jnp.zeros((B, FC), BF16)

    needed.wait_recv()
    go(passed)
    wo_forward()
    ag_forward(4)
    wo_finish()
    near_needed.wait_recv()
    passed.wait_recv()

    x1, dx1, acc = R["x1"], R["dx1"], R["acc"]

    def mix(i):
        x = tok[at(step * i, step), :].astype(F32) + mm(attQ[at(T * r + step * i, step), :], WO[...])
        x1[at(step * i, step), :] = x
        inv = lax.rsqrt(jnp.mean(x * x, axis=-1, keepdims=True) + EPSILON)
        h2Q[at(T * r + step * i, step), :] = (x * inv * GA[1:2, :]).astype(BF16)

    loop(T // step, mix)
    h2_start()
    go(rest)
    ag_forward(5)
    dy_finish()
    ag_forward(6)
    ag_finish(2)
    ag_finish(3)
    h2_forward()
    ag_finish(4)
    ag_finish(5)

    hid, dgdu = R["hid"], R["dgdu"]

    def ffn(half, role):
        def body(i):
            at_i = at(T * role + L * i, L)
            both = mm(h2Q[at_i, :], WB[:, half * FC : (half + 1) * FC])
            gate, up = both[:, 0:HF], both[:, HF:FC]
            sigma = 1.0 / (1.0 + jnp.exp(-gate))
            silu = gate * sigma
            hid[at_i, half * HF : (half + 1) * HF] = (silu * up).astype(BF16)
            d_hidden = mm(dyQ[at_i, :], WC[half * HF : (half + 1) * HF, :], NT)
            d_gate = d_hidden * up * (sigma * (1.0 + gate * (1.0 - sigma)))
            dgdu[at_i, half * FC : half * FC + HF] = d_gate.astype(BF16)
            dgdu[at_i, half * FC + HF : (half + 1) * FC] = (d_hidden * silu).astype(BF16)

        loop(T // L, body)

    ffn(0, r)
    ag_forward(7)
    h2_finish()
    rest.wait_recv()
    go(passed_rest)
    ffn(0, r_sib)
    ffn(0, r_par)
    ffn(0, r_dia)

    YS, YR, ZR, ZX, QS, QR = (R[k] for k in ("YS", "YR", "ZR", "ZX", "QS", "QR"))
    y_sem, z_sem, x_sem = ([take(size) for _ in range(4)] for size in (Z, Z - 1, 1))

    def gradient(unit, group, store):
        at_g = lanes(B * group, B)
        if unit == 0:
            store(slice(0, FC), mm(hid[:, at_g], dyQ[...], TN))
        elif unit < 3:
            store(slice(0, FC), mm(h2Q[:, at_g], dgdu[:, (unit - 1) * FC : unit * FC], TN))
        else:
            store(slice(0, 3 * QC), mm(h1Q[:, at_g], WC[:, 0 : 3 * QC], TN))
            store(slice(3 * QC, 4 * QC), mm(attQ[:, at_g], R["daR"][...], TN))

    slots = {1: 0, 2: 1, 0: 2, 3: 0}

    def y_copy(unit, i):
        return remote(YS.at[slots[unit], i], YR.at[unit, i], peer, y_sem[unit] + i)

    def z_copy(unit, d, i=0):
        return remote(YR.at[unit, i], ZR.at[unit, d - 1], z_dev(d), z_sem[unit] + d - 1)

    def x_copy(unit, i=0):
        return remote(YR.at[unit, i], ZX.at[unit], (1 + lax.div(z, 2)) * 8 + y * 4 + r, x_sem[unit])

    def target(unit, i):
        if not relays:
            return lax.rem(z + 1 + i, Z)
        even = 1 - lax.rem(z, 2)
        if unit == 0:
            return i + even * (1 - 2 * (i % 2 if isinstance(i, int) else lax.rem(i, 2)))
        o = (2 * i) % 3 + 3 * (i // 3) if isinstance(i, int) else lax.rem(2 * i, 3) + 3 * lax.div(i, 3)
        return o + even * (3 - 2 * o)

    def own_place(unit):
        if not relays:
            return Z - 1
        return 1 + 2 * lax.div(z, 2) if unit == 0 else 3 - lax.div(z * (3 - z), 2)

    def rs_first(unit, begin=0, count=Z):
        if unit == 3:
            for i in range(Z):
                y_copy(1, i).wait_send()

        def body(i):
            place = begin + i

            def store(cols, value):
                YS[slots[unit], place, :, cols] = value.astype(BF16)

            gradient(unit, 2 * target(unit, place) + 1 - y, store)
            y_copy(unit, place).start()

        loop(count, body)

    def rs_step(unit, i):
        goal = target(unit, i)
        d = lax.rem(goal + Z - z, Z)
        y_copy(unit, i).wait_recv()

        def store(cols, value):
            YR[unit, i, :, cols] = (value + YR[unit, i, :, cols].astype(F32)).astype(BF16)

        gradient(unit, 2 * goal + y, store)
        if not relays:
            pl.when(d != 0)(lambda: z_copy(unit, d, i).start())
            return
        far = outer & (goal + z == 3)
        pl.when(far)(lambda: x_copy(unit, i).start())
        pl.when((d != 0) & jnp.logical_not(far | (inner & (d == 2))))(lambda: z_copy(unit, d, i).start())

    def rs_relay(unit):
        i = 5 - 2 * z if unit == 0 else 3
        if relays:

            @pl.when(inner)
            def _():
                x_copy(unit).wait_recv()
                YR[unit, i] = (YR[unit, i].astype(F32) + ZX[unit].astype(F32)).astype(BF16)
                z_copy(unit, 2, i).start()

    def rs_second(unit, begin=0, count=Z):
        loop(count, lambda i: rs_step(unit, begin + i))

    quad_copies = {}

    def rs_third(unit):
        for d in range(1, Z):
            if relays and d != 2:
                pl.when(z != (0 if d == 1 else Z - 1))(z_copy(unit, d).wait_recv)
            else:
                z_copy(unit, d).wait_recv()
        width = 256
        for j in range(FC // width):
            cols = slice(width * j, width * (j + 1))
            value = YR[unit, own_place(unit), :, cols].astype(F32)
            for i in range(1, Z):
                value = value + ZR[unit, i - 1, :, cols].astype(F32)
            if unit == 0:
                R["gd"][:, cols] = value
            else:
                QS[unit - 1, :, cols] = value.astype(BF16)
        if unit:
            QR[unit - 1, r] = QS[unit - 1, at(rows * r, rows), :]
            quad_copies[unit] = [
                go(remote(QS.at[unit - 1, at(rows * q, rows)], QR.at[unit - 1, r], dev)) for dev, q in quad
            ]

    def rs_last(unit):
        for copy in quad_copies[unit]:
            copy.wait_recv()
        R["parts"][unit - 1] = QR[unit - 1]

    rsS, rsR = R["rsS"], R["rsR"]

    def quad_sum(kind, prepare_block, partial, fill=None):
        width = 512
        tiles = [slice(width * j, width * (j + 1)) for j in range(D // width)]
        copies = [
            remote(rsS.at[0], rsR.at[kind, 0], sib),
            remote(rsS.at[1], rsR.at[kind, 1], sib),
            remote(rsS.at[2], rsR.at[kind, 2], par),
        ]

        def blocks(role, store):
            def body(i):
                for cols in tiles:
                    store(at(L * i, L), cols, partial(at(T * role + L * i, L), cols))

            loop(T // L, body)

        def to_dia(at_i, cols, value):
            rsS[1, at_i, cols] = value.astype(BF16)

        def to_par(at_i, cols, value):
            rsS[2, at_i, cols] = (value + rsR[kind, 1, at_i, cols].astype(F32)).astype(BF16)

        def to_sib(at_i, cols, value):
            rsS[0, at_i, cols] = value.astype(BF16)

        def keep(at_i, cols, value):
            acc[at_i, cols] = value

        prepare_block(r_dia)
        blocks(r_dia, to_dia)
        copies[1].start()
        prepare_block(r_par)
        copies[1].wait_recv()
        blocks(r_par, to_par)
        copies[2].start()
        if fill:
            fill(0)
        prepare_block(r_sib)
        blocks(r_sib, to_sib)
        copies[0].start()
        if fill:
            fill(1)
        prepare_block(r)
        blocks(r, keep)

        def finish():
            copies[0].wait_recv()
            copies[2].wait_recv()
            for copy in copies:
                copy.wait_send()

        return finish

    def summed(kind, at_i):
        return acc[at_i, :] + (rsR[kind, 0, at_i, :].astype(F32) + rsR[kind, 2, at_i, :].astype(F32))

    def nothing(role):
        return None

    rs_first(1)
    rs_first(0, 0, Z // 2)
    ag_finish(6)
    ag_finish(7)
    h2_sum = quad_sum(
        0, functools.partial(ffn, 1), lambda at_i, cols: mm(dgdu[at_i, :], WB[cols, :], NT),
        lambda i: rs_second(1, i, 1),
    )
    rs_second(1, 2, 1)
    rs_first(2)
    h2_sum()

    TT, TR = R["TT"], R["TR"]
    daS, daR, dattS, dattR = (R[k] for k in ("daS", "daR", "dattS", "dattR"))
    TT[0] = jnp.zeros((8, D), F32)

    def norm_back(v, d_out, gain, row):
        inv = lax.rsqrt(jnp.mean(v * v, axis=-1, keepdims=True) + EPSILON)
        TT[0, row : row + 1, :] += jnp.sum(d_out * (v * inv), axis=0, keepdims=True)
        d = d_out * gain
        return inv * d - v * (inv * inv * inv * jnp.mean(d * v, axis=-1, keepdims=True))

    def mix_back(i):
        at_i = at(step * i, step)
        d = norm_back(x1[at_i, :], summed(0, at_i), GA[1:2, :], 1)
        d = d + dyQ[at(T * r + step * i, step), :].astype(F32)
        dx1[at_i, :] = d
        daS[at_i, :] = d.astype(BF16)

    loop(T // step, mix_back)
    sendD = [remote(daS.at[:, lanes(QC * q, QC)], daR.at[at(T * r, T)], dev) for dev, q in quad]
    sendT = [remote(dattS.at[:, lanes(QC * q, QC)], dattR.at[at(T * r, T)], dev) for dev, q in quad]

    def out_back(i):
        at_i = at(step * i, step)
        dattS[at_i, :] = mm(daS[at_i, :], WO[...], NT).astype(BF16)

    loop(T // step, out_back)
    for copy in sendT:
        go(copy)
    for copy in sendD:
        go(copy)
    dattR[at(T * r, T), :] = dattS[:, lanes(QC * r, QC)]
    daR[at(T * r, T), :] = daS[:, lanes(QC * r, QC)]
    rs_second(1, 3, 1)
    rs_first(0, Z // 2, Z // 2)
    rs_relay(1)
    rs_second(0, 0, Z // 2)
    out_sum = quad_sum(1, nothing, lambda at_i, cols: mm(hid[at_i, :], WC[:, cols]))
    ag_drain(2)
    ag_drain(3)
    for copy in sendT:
        copy.wait_recv()

    def write_out(i):
        at_i = at(step * i, step)
        R["act"][at_i, :] = (x1[at_i, :] + summed(1, at_i)).astype(BF16)

    HG, BG = R["HG"], R["BG"]
    HG[...] = jnp.zeros(HG.shape, F32)
    BG[...] = jnp.zeros(BG.shape, F32)

    def fold(v):
        return jnp.sum(v.reshape(L // 8, 8, 128), axis=0)

    def prepare_back(raw, d, m, j, cosine, sine, factor):
        if factor != 1.0:
            d = d * factor
        d = d * cosine - swap(d) * sine
        inv = lax.rsqrt(per_head(raw * raw) / 64 + EPSILON)
        HG[m, j] += fold(d * (raw * inv))
        d = d * small[2 + m : 3 + m, :]
        return inv * d - raw * (inv * inv * inv * (per_head(d * raw) / 64))

    def attend_back(q):
        at_q = at(L * q, L)
        _, same = masks(q)
        cosine, sine = CT[at_q, :], ST[at_q, :]
        for j in range(QC // 128):
            tile = slice(128 * j, 128 * (j + 1))
            q2, k2, v2, d2 = qr[at_q, tile], kr[at_q, tile], vb[at_q, tile], dattR[at_q, tile]
            dq, dk, dv = [], [], []
            for h in range(2):
                p = PR[q, 2 * j + h]
                dp = mm(d2 * heads[h], v2, NT)
                ds = (p * (dp - jnp.sum(p * dp, axis=-1, keepdims=True))).astype(BF16)
                wide = ds.astype(F32)
                BG[0, 2 * j + h] += fold(jnp.where(same, 0.0, wide))
                BG[1, 2 * j + h] += fold(jnp.where(same, wide, 0.0))
                dv.append(mm(p.astype(BF16), d2, TN))
                dq.append(mm(ds, k2))
                dk.append(mm(ds, q2, TN))
            d_query = jnp.where(low, dq[0], dq[1])
            d_key = jnp.where(low, dk[0], dk[1])
            d_query = prepare_back(qraw[at_q, tile], d_query, 0, j, cosine, sine, 0.125)
            d_key = prepare_back(kraw[at_q, tile], d_key, 1, j, cosine, sine, 1.0)
            WC[at_q, tile] = d_query.astype(BF16)
            WC[at_q, QC + 128 * j : QC + 128 * (j + 1)] = d_key.astype(BF16)
            WC[at_q, 2 * QC + 128 * j : 2 * QC + 128 * (j + 1)] = jnp.where(low, dv[0], dv[1]).astype(BF16)

    def attend_and_step(i):
        for q in range(S):
            attend_back(S * i + q)
        rs_step(2, i)

    loop(4, attend_and_step)
    for copy in sendD + [near_rest, passed_rest]:
        copy.wait_recv()
    rs_first(3)
    rs_relay(2)
    out_sum()
    loop(T // step, write_out)
    in_sum = quad_sum(
        2, nothing, lambda at_i, cols: mm(WC[at_i, 0 : 3 * QC], WA[cols, 0 : 3 * QC], NT),
        lambda i: rs_second(0, Z // 2 + i, 1),
    )
    rs_relay(0)
    rs_third(1)
    in_sum()

    def input_back(i):
        at_i = at(step * i, step)
        d = norm_back(tok[at_i, :].astype(F32), summed(2, at_i), GA[0:1, :], 0)
        R["ig"][at_i, :] = (dx1[at_i, :] + d).astype(BF16)

    loop(T // step, input_back)

    for m in range(2):
        value = HG[m, 0]
        for j in range(1, QC // 128):
            value = value + HG[m, j]
        TT[0, 2:3, 128 * m : 128 * (m + 1)] = jnp.sum(value, axis=0, keepdims=True)
    for m in range(2):
        line = jnp.zeros((1, 128), F32)
        for h in range(QC // 64):
            line = line + jnp.where(spot == QC // 64 * r + h, jnp.sum(BG[m, h]), 0.0)
        TT[0, 3 + m : 4 + m, 0:128] = line
    t1, t2, t3, t_finish = tile_sum(TT, TR)
    t1()
    rs_second(3, 0, 3)
    t2()
    rs_second(3, 3, 1)
    rs_relay(3)
    rs_third(2)
    rs_last(1)
    t3()
    rs_third(0)
    rs_third(3)
    rs_last(2)
    R["tot"][...] = t_finish()
    rs_last(3)
    for copy in sent:
        copy.wait_send()
    for k in range(len(chunks)):
        if k not in (2, 3):
            ag_drain(k)
    for unit in range(4):
        for i in range(Z):
            if unit != 1:
                y_copy(unit, i).wait_send()
            if i:
                nearby(i, z_copy(unit, i).wait_send)
        if relays:
            pl.when(outer)(x_copy(unit).wait_send)


LAST = ("act", "ig", "gq", "gk", "gv", "go", "gg", "gu", "gd", "ga", "gf", "ghq", "ghk", "gb")


def finishing(s, *refs):
    names = tuple(name + "_in" for name in OUTPUTS) + LAST
    R = dict(zip(names, refs, strict=True))
    D, rows, G, QC, FC, B, HD, H = (s[k] for k in ("D", "rows", "G", "QC", "FC", "B", "HD", "H"))
    HF = FC // 2
    for name in ("act", "ig", "gd"):
        R[name][...] = R[name + "_in"][...]
    parts = R["parts_in"]
    for q in range(4):
        for m, name in enumerate(("gq", "gk", "gv", "go")):
            R[name][:, QC * q : QC * (q + 1)] = parts[2, q, :, QC * m : QC * (m + 1)].astype(F32)
        for j in range(G):
            half, within = divmod(B * j, HF)
            target = slice(B * (4 * j + q), B * (4 * j + q) + B)
            R["gg"][:, target] = parts[half, q, :, within : within + B].astype(F32)
            R["gu"][:, target] = parts[half, q, :, HF + within : HF + within + B].astype(F32)
    tot = R["tot_in"]
    own = lax.axis_index("fsdp") * rows
    mine = pltpu.roll(tot[:, lanes(128 * lax.div(own, 128), 128)], lax.rem(128 - lax.rem(own, 128), 128), 1)
    R["ga"][...] = mine[0:1, 0:rows]
    R["gf"][...] = mine[1:2, 0:rows]
    both = tot[:, 0:256]
    both = both + pltpu.roll(both, 256 - HD, 1)
    R["ghq"][...] = both[2:3, 0:HD]
    R["ghk"][...] = both[2:3, 128 : 128 + HD]
    R["gb"][...] = tot[3:5, 0:H]


def layer(s, tokens, segment_ids, variate_ids, time_ids, w_query, w_key, w_value, w_out, w_gate, w_up, w_down,
          gain_attn, gain_ffn, gain_query, gain_key, variate_bias, cotangent):
    D, T, rows, B, FF, FC, HD, H = (s[k] for k in ("D", "T", "rows", "B", "FF", "FC", "HD", "H"))
    lines = [
        gain_attn[None], gain_ffn[None], jnp.tile(gain_query[None], (1, 2)), jnp.tile(gain_key[None], (1, 2)),
        variate_bias,
    ]
    small, line = jnp.zeros((8, 128), F32), 0
    for piece in lines:
        high, wide = piece.shape
        small = small + jnp.pad(piece.astype(F32), ((line, 8 - line - high), (0, 128 - wide)))
        line += high
    scratch = scratch_of(s)
    names = INPUTS + OUTPUTS + tuple(scratch)
    vmem, anywhere = pl.BlockSpec(memory_space=pltpu.VMEM), pl.BlockSpec(memory_space=pl.ANY)
    here = {"seg", "var", "tim", "small"}

    def shape(*dims, kind=F32):
        return jax.ShapeDtypeStruct(dims, kind)

    tokens_shape = shape(T, D, kind=BF16)
    outs = pl.pallas_call(
        functools.partial(fused, s, names),
        out_shape=[tokens_shape, tokens_shape, shape(B, D), shape(3, 4, rows, FC, kind=BF16), shape(8, D)],
        in_specs=[vmem if name in here else anywhere for name in INPUTS],
        out_specs=[vmem] * len(OUTPUTS),
        scratch_shapes=list(scratch.values()),
        compiler_params=pltpu.CompilerParams(
            collective_id=0, has_side_effects=True, vmem_limit_bytes=64 << 20
        ),
        name="fused_layer",
    )(
        tokens.reshape(T, D), cotangent.reshape(T, D), segment_ids, variate_ids, time_ids,
        w_query, w_key, w_value, w_out, w_gate, w_up, w_down, small,
    )
    last = pl.pallas_call(
        functools.partial(finishing, s),
        out_shape=[tokens_shape, tokens_shape] + [shape(rows, D)] * 4 + [shape(rows, FF)] * 2
        + [shape(B, D), shape(1, rows), shape(1, rows), shape(1, HD), shape(1, HD), shape(2, H)],
        in_specs=[vmem] * len(OUTPUTS),
        out_specs=[vmem] * len(LAST),
        name="finishing",
    )(*outs)
    flat = [value.reshape(-1) for value in last[9:13]]
    return (last[0].reshape(tokens.shape), last[1].reshape(tokens.shape), *last[2:9], *flat, last[13])


def local(tokens, segment_ids, variate_ids, time_ids, *rest):
    s = sizes_of(lax.axis_size("fsdp"), tokens, rest[0], rest[4], rest[9], rest[11])
    chosen = functools.partial(layer, s) if fits(s) else plain
    return chosen(tokens, segment_ids, variate_ids, time_ids, *rest)


def solution(mesh):
    placed = (
        P("fsdp", None, None),
        P("fsdp", None),
        P("fsdp", None),
        P("fsdp", None),
        P("fsdp", None),
        P("fsdp", None),
        P("fsdp", None),
        P("fsdp", None),
        P("fsdp", None),
        P("fsdp", None),
        P("fsdp", None),
        P("fsdp"),
        P("fsdp"),
        P(),
        P(),
        P(),
        P("fsdp", None, None),
    )
    return jax.shard_map(
        local,
        mesh=mesh,
        in_specs=placed,
        out_specs=(
            P("fsdp", None, None),
            P("fsdp", None, None),
            P("fsdp", None),
            P("fsdp", None),
            P("fsdp", None),
            P("fsdp", None),
            P("fsdp", None),
            P("fsdp", None),
            P("fsdp", None),
            P("fsdp"),
            P("fsdp"),
            P(),
            P(),
            P(),
        ),
        check_vma=False,
    )
```

```python
import functools
import math

import jax
import jax.numpy as jnp
from jax import lax
from jax.experimental import pallas as pl
from jax.experimental.pallas import tpu as pltpu
from jax.sharding import PartitionSpec as P

EPSILON = 1e-05


def normalize(values, scale_gain):
    return (
        values * lax.rsqrt(jnp.mean(values * values, axis=-1, keepdims=True) + EPSILON) * scale_gain
    )


def rotate(values, moments):
    halfway = values.shape[-1] // 2
    frequency = jnp.exp(-math.log(10000.0) * jnp.arange(halfway).astype(jnp.float32) / halfway)
    angles = moments.astype(jnp.float32)[:, None] * frequency[None, :]
    cosine = jnp.cos(angles)[:, None, :]
    sine_part = jnp.sin(angles)[:, None, :]
    former = values[..., :halfway]
    latter = values[..., halfway:]
    return jnp.concatenate(
        [former * cosine - latter * sine_part, former * sine_part + latter * cosine], axis=-1
    )


def prepare(raw_heads, head_gain, moments, factor):
    return rotate(normalize(raw_heads, head_gain), moments) * factor


def swiglu(gate_act, up_act):
    return jax.nn.silu(gate_act) * up_act


def attention_masks(segments, variates):
    length = segments.shape[0]
    diagonal = jnp.arange(length)[:, None] == jnp.arange(length)[None, :]
    allowed = (segments[:, None] == segments[None, :]) & ((segments[None, :] != 0) | diagonal)
    same_var = variates[:, None] == variates[None, :]
    return (allowed, same_var)


def scoring(q_rot, k_rot, bias_table, allowed, same_var):
    scores = jnp.einsum("qhe,khe->hqk", q_rot, k_rot, preferred_element_type=jnp.float32)
    scores = scores + jnp.where(
        same_var[None], bias_table[1][:, None, None], bias_table[0][:, None, None]
    )
    return jnp.where(allowed[None], scores, -1000000000.0)


def project(left, right):
    return jnp.dot(left, right, preferred_element_type=jnp.float32)


def across(left, right):
    return lax.dot_general(
        left, right, (((0,), (0,)), ((), ())), preferred_element_type=jnp.float32
    )


def against(left, weight):
    return lax.dot_general(
        left, weight, (((1,), (1,)), ((), ())), preferred_element_type=jnp.float32
    )


def forward(inputs_low, weights, side_params, segments, variates, moments):
    w_query, w_key, w_value, w_out, w_gate, w_up, w_down, gain_attn, gain_ffn = weights
    gain_query, gain_key, bias_table = side_params
    length, model_width = inputs_low.shape
    head_count = bias_table.shape[1]
    head_dim = gain_query.shape[0]
    inputs = inputs_low.astype(jnp.float32)
    normed = normalize(inputs, gain_attn.astype(jnp.float32)).astype(jnp.bfloat16)
    queries = project(normed, w_query).reshape(length, head_count, head_dim)
    key_raw = project(normed, w_key).reshape(length, head_count, head_dim)
    v_low = project(normed, w_value).reshape(length, head_count, head_dim).astype(jnp.bfloat16)
    q_rot = prepare(queries, gain_query, moments, head_dim ** (-0.5)).astype(jnp.bfloat16)
    k_rot = prepare(key_raw, gain_key, moments, 1.0).astype(jnp.bfloat16)
    allowed, same_var = attention_masks(segments, variates)
    scores = scoring(q_rot, k_rot, bias_table, allowed, same_var)
    maximum = jnp.max(scores, axis=-1, keepdims=True)
    exponent = jnp.exp(scores - maximum)
    row_total = jnp.sum(exponent, axis=-1, keepdims=True)
    log_total = maximum + jnp.log(row_total)
    softmax_probs = (exponent / row_total).astype(jnp.bfloat16)
    attended = jnp.einsum("hqk,khe->qhe", softmax_probs, v_low, preferred_element_type=jnp.float32)
    attended = attended.reshape(length, model_width).astype(jnp.bfloat16)
    mixed_state = inputs + project(attended, w_out)
    normed_ffn = normalize(mixed_state, gain_ffn.astype(jnp.float32)).astype(jnp.bfloat16)
    gate_act = project(normed_ffn, w_gate)
    up_act = project(normed_ffn, w_up)
    hidden = swiglu(gate_act, up_act).astype(jnp.bfloat16)
    result = mixed_state + project(hidden, w_down)
    kept_state = (
        inputs,
        normed,
        queries,
        key_raw,
        q_rot,
        k_rot,
        v_low,
        log_total,
        attended,
        mixed_state,
        normed_ffn,
        gate_act,
        up_act,
        hidden,
    )
    return (result, kept_state)


def backward(upstream, kept_state, weights, side_params, segments, variates, moments):
    (
        inputs,
        normed,
        queries,
        key_raw,
        q_rot,
        k_rot,
        v_low,
        log_total,
        attended,
        mixed_state,
        normed_ffn,
        gate_act,
        up_act,
        hidden,
    ) = kept_state
    w_query, w_key, w_value, w_out, w_gate, w_up, w_down, gain_attn, gain_ffn = weights
    gain_query, gain_key, bias_table = side_params
    length, head_count, head_dim = queries.shape
    grad_down = across(hidden, upstream)
    d_hidden = against(upstream, w_down)
    _, pullback = jax.vjp(swiglu, gate_act, up_act)
    d_gate, d_up = pullback(d_hidden)
    d_gate = d_gate.astype(jnp.bfloat16)
    d_up = d_up.astype(jnp.bfloat16)
    grad_gate = across(normed_ffn, d_gate)
    grad_up = across(normed_ffn, d_up)
    d_normed_ffn = against(d_gate, w_gate) + against(d_up, w_up)
    _, pullback = jax.vjp(normalize, mixed_state, gain_ffn.astype(jnp.float32))
    d_mixed, grad_gain_ffn = pullback(d_normed_ffn)
    d_mixed = d_mixed + upstream.astype(jnp.float32)
    d_branch = d_mixed.astype(jnp.bfloat16)
    grad_out = across(attended, d_branch)
    d_attended = against(d_branch, w_out).astype(jnp.bfloat16).reshape(length, head_count, head_dim)
    allowed, same_var = attention_masks(segments, variates)
    scores = scoring(q_rot, k_rot, bias_table, allowed, same_var)
    softmax_probs = jnp.exp(scores - log_total)
    d_probs = jnp.einsum("qhe,khe->hqk", d_attended, v_low, preferred_element_type=jnp.float32)
    d_values = jnp.einsum(
        "hqk,qhe->khe",
        softmax_probs.astype(jnp.bfloat16),
        d_attended,
        preferred_element_type=jnp.float32,
    )
    d_values = d_values.reshape(length, head_count * head_dim).astype(jnp.bfloat16)
    weighted = jnp.sum(softmax_probs * d_probs, axis=-1, keepdims=True)
    d_scores = (softmax_probs * (d_probs - weighted)).astype(jnp.bfloat16)
    d_float = d_scores.astype(jnp.float32)
    same_sum = jnp.sum(jnp.where(same_var[None], d_float, 0.0), axis=(1, 2))
    other_sum = jnp.sum(jnp.where(same_var[None], 0.0, d_float), axis=(1, 2))
    grad_bias = jnp.stack([other_sum, same_sum])
    d_qrot = jnp.einsum("hqk,khe->qhe", d_scores, k_rot, preferred_element_type=jnp.float32)
    d_krot = jnp.einsum("hqk,qhe->khe", d_scores, q_rot, preferred_element_type=jnp.float32)
    factor = head_dim ** (-0.5)
    _, pullback = jax.vjp(
        lambda raw_heads, head_gain: prepare(raw_heads, head_gain, moments, factor),
        queries,
        gain_query,
    )
    d_queries, grad_gain_query = pullback(d_qrot)
    _, pullback = jax.vjp(
        lambda raw_heads, head_gain: prepare(raw_heads, head_gain, moments, 1.0), key_raw, gain_key
    )
    d_keys, grad_gain_key = pullback(d_krot)
    d_queries = d_queries.reshape(length, head_count * head_dim).astype(jnp.bfloat16)
    d_keys = d_keys.reshape(length, head_count * head_dim).astype(jnp.bfloat16)
    grad_query = across(normed, d_queries)
    grad_key = across(normed, d_keys)
    grad_value = across(normed, d_values)
    d_normed = against(d_queries, w_query) + against(d_keys, w_key) + against(d_values, w_value)
    _, pullback = jax.vjp(normalize, inputs, gain_attn.astype(jnp.float32))
    d_inputs, grad_gain_attn = pullback(d_normed)
    row_grads = jnp.concatenate(
        [grad_query, grad_key, grad_value, grad_out, grad_gate, grad_up], axis=1
    )
    small = (grad_gain_query, grad_gain_key, grad_bias, grad_gain_attn, grad_gain_ffn)
    return (d_inputs + d_mixed, row_grads, grad_down, small)


def plain(
    tokens,
    segment_ids,
    variate_ids,
    time_ids,
    w_query,
    w_key,
    w_value,
    w_out,
    w_gate,
    w_up,
    w_down,
    gain_attn,
    gain_ffn,
    gain_query,
    gain_key,
    variate_bias,
    cotangent,
):
    devices = lax.axis_size("fsdp")
    owner = lax.axis_index("fsdp")
    width = w_query.shape[1]
    hidden_width = w_gate.shape[1]
    own_rows = w_query.shape[0]
    own_down = w_down.shape[0]
    side_params = (
        gain_query.astype(jnp.float32),
        gain_key.astype(jnp.float32),
        variate_bias.astype(jnp.float32),
    )
    rows_total = jnp.zeros((own_rows * devices, 4 * width + 2 * hidden_width), jnp.float32)
    down_total = jnp.zeros((own_down * devices, width), jnp.float32)
    side_totals = (
        jnp.zeros(gain_query.shape, jnp.float32),
        jnp.zeros(gain_key.shape, jnp.float32),
        jnp.zeros(variate_bias.shape, jnp.float32),
        jnp.zeros((own_rows * devices,), jnp.float32),
        jnp.zeros((own_rows * devices,), jnp.float32),
    )
    results = []
    input_grads = []
    for micro_index in range(tokens.shape[0]):
        segments = segment_ids[micro_index]
        variates = variate_ids[micro_index]
        moments = time_ids[micro_index]
        forward_weights = (
            lax.all_gather(w_query, "fsdp", axis=0, tiled=True),
            lax.all_gather(w_key, "fsdp", axis=0, tiled=True),
            lax.all_gather(w_value, "fsdp", axis=0, tiled=True),
            lax.all_gather(w_out, "fsdp", axis=0, tiled=True),
            lax.all_gather(w_gate, "fsdp", axis=0, tiled=True),
            lax.all_gather(w_up, "fsdp", axis=0, tiled=True),
            lax.all_gather(w_down, "fsdp", axis=0, tiled=True),
            lax.all_gather(gain_attn, "fsdp", axis=0, tiled=True),
            lax.all_gather(gain_ffn, "fsdp", axis=0, tiled=True),
        )
        result, kept_state = forward(
            tokens[micro_index], forward_weights, side_params, segments, variates, moments
        )
        results.append(result.astype(jnp.bfloat16))
        backward_weights = (
            lax.all_gather(w_query, "fsdp", axis=0, tiled=True),
            lax.all_gather(w_key, "fsdp", axis=0, tiled=True),
            lax.all_gather(w_value, "fsdp", axis=0, tiled=True),
            lax.all_gather(w_out, "fsdp", axis=0, tiled=True),
            lax.all_gather(w_gate, "fsdp", axis=0, tiled=True),
            lax.all_gather(w_up, "fsdp", axis=0, tiled=True),
            lax.all_gather(w_down, "fsdp", axis=0, tiled=True),
            lax.all_gather(gain_attn, "fsdp", axis=0, tiled=True),
            lax.all_gather(gain_ffn, "fsdp", axis=0, tiled=True),
        )
        d_inputs, row_grads, down_grads, small = backward(
            cotangent[micro_index],
            kept_state,
            backward_weights,
            side_params,
            segments,
            variates,
            moments,
        )
        input_grads.append(d_inputs.astype(jnp.bfloat16))
        rows_total = rows_total + row_grads
        down_total = down_total + down_grads
        side_totals = tuple((running + fresh for running, fresh in zip(side_totals, small)))
    owned_rows = lax.psum_scatter(rows_total, "fsdp", scatter_dimension=0, tiled=True)
    owned_down = lax.psum_scatter(down_total, "fsdp", scatter_dimension=0, tiled=True)
    shared = lax.psum(
        (side_totals[0], side_totals[1], side_totals[2], side_totals[3], side_totals[4]), "fsdp"
    )
    gain_attn_own = lax.dynamic_slice_in_dim(shared[3], owner * own_rows, own_rows, 0)
    gain_ffn_own = lax.dynamic_slice_in_dim(shared[4], owner * own_rows, own_rows, 0)
    grad_query = owned_rows[:, 0:width]
    grad_key = owned_rows[:, width : 2 * width]
    grad_value = owned_rows[:, 2 * width : 3 * width]
    grad_out = owned_rows[:, 3 * width : 4 * width]
    grad_gate = owned_rows[:, 4 * width : 4 * width + hidden_width]
    grad_up = owned_rows[:, 4 * width + hidden_width :]
    return (
        jnp.stack(results),
        jnp.stack(input_grads),
        grad_query,
        grad_key,
        grad_value,
        grad_out,
        grad_gate,
        grad_up,
        owned_down,
        gain_attn_own,
        gain_ffn_own,
        shared[0],
        shared[1],
        shared[2],
    )


F32 = jnp.float32
BF16 = jnp.bfloat16
MESH = pl.DeviceIdType.MESH
NT = (((1,), (1,)), ((), ()))
TN = (((0,), (0,)), ((), ()))


def mm(left, right, dims=(((1,), (0,)), ((), ()))):
    return lax.dot_general(left, right, dims, preferred_element_type=F32)


def at(start, size):
    return pl.ds(pl.multiple_of(start, size), size)


def lanes(start, size):
    return pl.ds(pl.multiple_of(start, 128), size)


def loop(count, body):
    lax.fori_loop(0, count, lambda i, carry: (body(i), carry)[1], 0)


def sizes_of(devices, tokens, w_query, w_gate, gain_query, bias):
    seqs, length, width = tokens.shape
    own_rows, hidden = w_query.shape[0], w_gate.shape[1]
    return dict(
        n=devices, S=seqs, L=length, D=width, FF=hidden, rows=own_rows, T=seqs * length,
        G=devices // 4, Z=devices // 8, QC=width // 4, FC=hidden // 4, B=4 * own_rows,
        HD=gain_query.shape[0], H=bias.shape[1],
    )


def fits(s):
    return (
        s["n"] % 8 == 0 and s["rows"] % 16 == 0 and s["L"] == 128 and s["HD"] == 64
        and s["H"] * s["HD"] == s["D"] and s["QC"] % 128 == 0 and s["FF"] == 4 * s["D"]
        and s["B"] == 128 and s["FC"] // 2 % s["B"] == 0 and s["FC"] == s["D"]
    )


def scratch_of(s):
    n, S, L, D, rows, T, G, Z, QC, FC, B = (
        s[k] for k in ("n", "S", "L", "D", "rows", "T", "G", "Z", "QC", "FC", "B")
    )
    Q = 4 * T
    vm = pltpu.VMEM
    return dict(
        WA=vm((D, 4 * QC), BF16), WB=vm((D, 2 * FC), BF16), WC=vm((FC, D), BF16), WO=vm((D, D), BF16),
        SA=vm((4, rows, 4 * QC), BF16), SB=vm((4, rows, 2 * FC), BF16),
        h1Q=vm((Q, D), BF16), dyQ=vm((Q, D), BF16), attQ=vm((Q, D), BF16), h2Q=vm((Q, D), BF16),
        qraw=vm((Q, QC), F32), kraw=vm((Q, QC), F32),
        qr=vm((Q, QC), BF16), kr=vm((Q, QC), BF16), vb=vm((Q, QC), BF16),
        PR=vm((4 * S, QC // 64, L, L), F32), CT=vm((Q, 128), F32), ST=vm((Q, 128), F32),
        x1=vm((T, D), F32), dx1=vm((T, D), F32), acc=vm((T, D), F32),
        hid=vm((Q, FC), BF16), dgdu=vm((Q, 2 * FC), BF16),
        rsS=vm((3, T, D), BF16), rsR=vm((3, 3, T, D), BF16),
        daS=vm((T, D), BF16), daR=vm((Q, QC), BF16), dattS=vm((T, D), BF16), dattR=vm((Q, QC), BF16),
        YS=vm((3, Z, B, FC), BF16), YR=vm((4, Z, B, FC), BF16), ZR=vm((4, Z - 1, B, FC), BF16), ZX=vm((4, B, FC), BF16),
        QS=vm((3, B, FC), BF16), QR=vm((3, 4, rows, FC), BF16),
        idq=vm((4 * S, 8, L), F32),
        SW=vm((4, rows, D), BF16), SG=vm((2, rows, s["FF"]), BF16), TK=vm((T, D), BF16),
        GQ=vm((4, 8, B), F32), GA=vm((8, D), F32), load=pltpu.SemaphoreType.DMA((9,)),
        TT=vm((3, 8, D), F32), TR=vm((4 + Z, 8, D), F32),
        HG=vm((4, QC // 128, 8, 128), F32), BG=vm((2, QC // 64, 8, 128), F32),
        send=pltpu.SemaphoreType.DMA((192,)), recv=pltpu.SemaphoreType.DMA((192,)),
    )


INPUTS = (
    "tok", "cot", "seg", "var", "tim", "wq", "wk", "wv", "wo", "wg", "wu", "wd", "small",
)
OUTPUTS = ("act", "ig", "gd", "parts", "tot")


def fused(s, names, *refs):
    R = dict(zip(names, refs, strict=True))
    n, S, L, D, rows, T, G, Z, QC, FC, B = (
        s[k] for k in ("n", "S", "L", "D", "rows", "T", "G", "Z", "QC", "FC", "B")
    )
    HF = FC // 2
    Q = 4 * T
    me = lax.axis_index("fsdp")
    r, c, xx, g = lax.rem(me, 4), lax.rem(me, 2), lax.rem(lax.div(me, 2), 2), lax.div(me, 4)
    y, z = lax.rem(g, 2), lax.div(g, 2)
    r_sib, r_par = r + 1 - 2 * c, r + 2 - 4 * xx
    r_dia = r_sib + 2 - 4 * xx
    sib, par, dia = me - r + r_sib, me - r + r_par, me - r + r_dia
    peer = me + 4 - 8 * y
    quad = ((sib, r_sib), (par, r_par), (dia, r_dia))

    def at_z(step):
        return lax.rem(z + step, Z)

    def z_dev(step):
        return at_z(step) * 8 + y * 4 + r

    def z_src(step):
        return lax.rem(z + Z - step, Z)

    relays = Z == 4
    inner, outer = lax.rem(z + 1, 4) >= 2, lax.rem(z + 1, 4) < 2

    def nearby(step, action):
        if relays and step != 2:
            pl.when(z != (Z - 1 if step == 1 else 0))(action)
        else:
            action()

    used = [0]
    sent = []

    def take(count=1):
        used[0] += count
        return used[0] - count

    def remote(src, dst, device, sem=None, arrival=None):
        sem = take() if sem is None else sem
        arrival = sem if arrival is None else arrival
        return pltpu.make_async_remote_copy(
            src_ref=src, dst_ref=dst, send_sem=R["send"].at[sem], recv_sem=R["recv"].at[arrival],
            device_id=(device,), device_id_type=MESH,
        )

    def go(copy):
        copy.start()
        sent.append(copy)
        return copy

    barrier = pltpu.get_barrier_semaphore()
    others = [sib, par, dia, peer] + [z_dev(d) for d in range(1, Z)]
    for device in others:
        pl.semaphore_signal(barrier, inc=1, device_id=(device,), device_id_type=MESH)

    SA, SB, SW, SG, WA, WB, WC, WO = (R[k] for k in ("SA", "SB", "SW", "SG", "WA", "WB", "WC", "WO"))
    dyQ, h1Q, h2Q, attQ, tok = R["dyQ"], R["h1Q"], R["h2Q"], R["attQ"], R["TK"]
    places = [("wq", SW.at[0]), ("wk", SW.at[1]), ("wv", SW.at[2]), ("wo", SW.at[3]), ("wd", WC.at[at(B * g, B)])]
    places += [("tok", tok), ("wg", SG.at[0]), ("wu", SG.at[1]), ("cot", dyQ.at[at(T * r, T)])]
    loads = {}
    for i, (name, place) in enumerate(places):
        loads[name] = pltpu.make_async_copy(R[name], place, R["load"].at[i])
        loads[name].start()
    own = at(B * g + rows * r, rows)
    idq, small, GQ, GA = R["idq"], R["small"], R["GQ"], R["GA"]
    for q in range(S):
        idq[S * r + q, 0:1, :] = R["seg"][q : q + 1, :].astype(F32)
        idq[S * r + q, 1:2, :] = R["var"][q : q + 1, :].astype(F32)
        idq[S * r + q, 2:3, :] = R["tim"][q : q + 1, :].astype(F32)
        idq[S * r + q, 3:8, :] = jnp.zeros((5, L), F32)
    GQ[r] = pltpu.roll(small[...], rows * r, 1)
    for m, name in enumerate(("wq", "wk", "wv", "wo")):
        loads[name].wait()
        for q in range(4):
            SA[q, :, QC * m : QC * (m + 1)] = SW[m, :, QC * q : QC * (q + 1)]
    WA[own, :] = SA[r]
    pl.semaphore_wait(barrier, len(others))

    def tile_sum(tile, got):
        first = [remote(tile.at[0], got.at[i], dev) for i, (dev, _) in enumerate(quad)]
        second = [remote(tile.at[1], got.at[4 + z], z_dev(d)) for d in range(1, Z)]
        third = remote(tile.at[2], got.at[3], peer)

        def round1():
            for copy in first:
                go(copy)

        def round2():
            for copy in first:
                copy.wait_recv()
            value = (tile[0] + got[0]) + (got[1] + got[2])
            tile[1] = value
            got[4 + z] = value
            for copy in second:
                go(copy)

        def round3():
            for copy in second:
                copy.wait_recv()
            value = got[4]
            for i in range(1, Z):
                value = value + got[4 + i]
            tile[2] = value
            go(third)

        def finish():
            third.wait_recv()
            return tile[2] + got[3]

        return round1, round2, round3, finish

    def quad_gather(block):
        to_sib, to_par = remote(block(r), block(r), sib), remote(block(r), block(r), par)
        passed = remote(block(r_par), block(r_par), sib)

        def start():
            go(to_par)
            go(to_sib)

        def forward():
            to_par.wait_recv()
            go(passed)

        def finish():
            to_sib.wait_recv()
            passed.wait_recv()

        return start, forward, finish

    chunks = [(WA, 0, 2 * QC), (WA, 2 * QC, 2 * QC), (WC, 0, D // 2), (WC, D // 2, D // 2)]
    chunks += [(WB, HF * k, HF) for k in range(4)] + [(GA, 0, B)]
    early, after = 99, {0: 2, 1: 3, 2: 4, 3: 5, 4: 6, 5: 7}

    def piece(k, group):
        ref, start, size = chunks[k]
        if ref is GA:
            return ref.at[:, lanes(B * group, B)]
        return ref.at[at(B * group, B), pl.ds(start, size)]

    a_sem, f_sem, o_sem = ([take(size) for _ in chunks] for size in (Z - 1, 1, Z))
    b_sem, e_sem = take(Z - 1), take()

    def across_y(other):
        return y + other * (1 - 2 * y)

    def along(k, d, other=0):
        block = piece(k, 2 * z + across_y(other))
        return remote(block, block, z_dev(d), (b_sem if other else a_sem[k]) + d - 1)

    def over(k, d):
        block = piece(k, 2 * z_src(d) + y)
        return remote(block, block, peer, o_sem[k] + d)

    def relay(k, other=0):
        block, end = piece(k, 2 * z_src(2) + across_y(other)), lax.div(z, 2)
        sems = (e_sem, b_sem + 2 * end) if other else (f_sem[k], a_sem[k] + 2 * end)
        return remote(block, block, 3 * end * 8 + y * 4 + r, *sems)

    def near(k, d, action):
        if k == 8:
            action()
        else:
            nearby(d, action)

    def both(k):
        return (0, 1) if k == early else (0,)

    def ag_start(k):
        for other in both(k):
            for d in range(1, Z):
                near(k, d, along(k, d, other).start)

    def ag_own(k):
        over(k, 0).start()

    def ag_forward(k):
        first = lax.div(3 - z, 3)
        for i in range(1, Z):
            d = i if not relays or i == 2 else 1 + 2 * first if i == 1 else 3 - 2 * first
            for other in both(k):
                along(k, d, other).wait_recv()
                if relays and i == 2 and k < 8:
                    pl.when(inner)(relay(k, other).start)
            if k != early:
                over(k, d).start()
        if k in after:
            ag_own(after[k])
        if 2 <= k <= 5:
            ag_start(k + 2)

    def ag_finish(k):
        for d in range(Z):
            if k != early:
                over(k, d).wait_recv()

    def ag_drain(k):
        for d in range(1 if k == early else Z):
            over(k, d).wait_send()
        for other in both(k):
            for d in range(1, Z):
                near(k, d, along(k, d, other).wait_send)
            if relays and k < 8:
                pl.when(inner)(relay(k, other).wait_send)

    sendG = [remote(GQ.at[r], GQ.at[r], dev) for dev, q in quad]
    sendA = [remote(SA.at[q], WA.at[own], dev) for dev, q in quad]
    sendB = [remote(SB.at[q], WB.at[own], dev) for dev, q in quad]
    mine = idq.at[pl.ds(S * r, S)]
    sendI = [remote(mine, mine, dev) for dev, q in quad]
    for copy in sendG + sendA + sendI:
        go(copy)
    loads["wd"].wait()
    for copy in sendG:
        copy.wait_recv()
    GA[:, lanes(B * g, B)] = (GQ[0] + GQ[1]) + (GQ[2] + GQ[3])
    ag_start(8)
    ag_own(8)
    for copy in sendA:
        copy.wait_recv()
    ag_start(0)
    ag_own(0)
    ag_start(1)
    ag_own(1)
    for copy in sendI:
        copy.wait_recv()

    lane = lax.broadcasted_iota(jnp.int32, (L, 128), 1)
    sub = lax.broadcasted_iota(jnp.int32, (L, 128), 0)
    front = lax.rem(lane, 64) < 32
    low = lane < 64
    freq = jnp.exp(-math.log(10000.0) * lax.rem(lane, 32).astype(F32) / 32)
    CT, ST = R["CT"], R["ST"]

    def tables(q):
        times = jnp.broadcast_to(idq[q, 2:3, :], (L, L)).T
        angles = times * freq
        CT[at(L * q, L), :] = jnp.cos(angles)
        sine = jnp.sin(angles)
        ST[at(L * q, L), :] = jnp.where(front, -sine, sine)

    loop(2 * S, tables)
    ag_forward(8)
    loop(2 * S, lambda q: tables(2 * S + q))
    loads["tok"].wait()
    ag_finish(8)
    step = 64

    def norm_in(i):
        x = tok[at(step * i, step), :].astype(F32)
        inv = lax.rsqrt(jnp.mean(x * x, axis=-1, keepdims=True) + EPSILON)
        h1Q[at(T * r + step * i, step), :] = (x * inv * GA[0:1, :]).astype(BF16)

    loop(T // step, norm_in)

    def token_block(ref):
        return lambda role: ref.at[at(T * role, T)]

    h1_start, h1_forward, h1_finish = quad_gather(token_block(h1Q))
    dy_start, dy_forward, dy_finish = quad_gather(token_block(dyQ))

    def att_block(chip, role):
        return attQ.at[at(2 * T * chip, 2 * T), lanes(QC * role, QC)]

    def att_copy(chip, role, device):
        return remote(att_block(chip, role), att_block(chip, role), device)

    needed, passed = att_copy(1 - xx, r, par), att_copy(xx, r_par, sib)
    near_needed, near_rest = att_copy(xx, r, sib), att_copy(1 - xx, r, sib)
    rest, passed_rest = att_copy(xx, r, par), att_copy(1 - xx, r_par, sib)
    wo_start, wo_forward, wo_finish = quad_gather(lambda role: WO.at[:, lanes(QC * role, QC)])
    h2_start, h2_forward, h2_finish = quad_gather(token_block(h2Q))
    h1_start()
    for name in ("wg", "wu"):
        loads[name].wait()
    for q in range(4):
        for j in range(G):
            half, within = divmod(B * j, HF)
            source = slice(B * (4 * j + q), B * (4 * j + q) + B)
            SB[q, :, half * FC + within : half * FC + within + B] = SG[0, :, source]
            SB[q, :, half * FC + HF + within : half * FC + HF + within + B] = SG[1, :, source]
    WB[own, :] = SB[r]
    for copy in sendB:
        go(copy)
    ag_forward(0)
    ag_start(2)
    h1_forward()
    ag_forward(1)
    ag_start(3)
    for copy in sendB:
        copy.wait_recv()
    loads["cot"].wait()
    dy_start()
    h1_finish()
    ag_finish(0)
    ag_finish(1)
    ag_forward(2)

    qraw, kraw, qr, kr, vb, PR = (R[k] for k in ("qraw", "kraw", "qr", "kr", "vb", "PR"))
    spot = lax.broadcasted_iota(jnp.int32, (1, 128), 1)
    bias = [
        [jnp.sum(jnp.where(spot == QC // 64 * r + h, small[4 + m : 5 + m, :], 0.0)) for h in range(QC // 64)]
        for m in range(2)
    ]

    def swap(v):
        return jnp.where(front, pltpu.roll(v, 96, 1), pltpu.roll(v, 32, 1))

    def per_head(v):
        first = jnp.sum(jnp.where(low, v, 0.0), axis=-1, keepdims=True)
        second = jnp.sum(jnp.where(low, 0.0, v), axis=-1, keepdims=True)
        return jnp.where(low, first, second)

    def project_heads(q):
        at_q = at(L * q, L)
        value = mm(h1Q[at_q, :], WA[:, 0 : 3 * QC])
        cosine, sine = CT[at_q, :], ST[at_q, :]
        for m, (raw, ready) in enumerate(((qraw, qr), (kraw, kr))):
            raw[at_q, :] = value[:, QC * m : QC * (m + 1)]
            for j in range(QC // 128):
                v = value[:, QC * m + 128 * j : QC * m + 128 * (j + 1)]
                inv = lax.rsqrt(per_head(v * v) / 64 + EPSILON)
                v = v * inv * small[2 + m : 3 + m, :]
                v = v * cosine + swap(v) * sine
                if m == 0:
                    v = v * 0.125
                ready[at_q, 128 * j : 128 * (j + 1)] = v.astype(BF16)
        vb[at_q, :] = value[:, 2 * QC : 3 * QC].astype(BF16)

    loop(4 * S, project_heads)
    WO[:, lanes(QC * r, QC)] = WA[:, 3 * QC : 4 * QC]
    wo_start()
    dy_forward()

    def masks(q):
        segment = jnp.broadcast_to(idq[q, 0:1, :], (L, L))
        variate = jnp.broadcast_to(idq[q, 1:2, :], (L, L))
        allowed = (segment == segment.T) & ((segment != 0.0) | (lane == sub))
        return allowed, variate == variate.T

    heads = [jnp.where(low, 1.0, 0.0).astype(BF16), jnp.where(low, 0.0, 1.0).astype(BF16)]

    def attend(q):
        at_q = at(L * q, L)
        allowed, same = masks(q)
        for j in range(QC // 128):
            tile = slice(128 * j, 128 * (j + 1))
            q2, k2, v2 = qr[at_q, tile], kr[at_q, tile], vb[at_q, tile]
            outs = []
            for h in range(2):
                head = 2 * j + h
                score = mm(q2 * heads[h], k2, NT) + jnp.where(same, bias[1][head], bias[0][head])
                score = jnp.where(allowed, score, -1000000000.0)
                e = jnp.exp(score - jnp.max(score, axis=-1, keepdims=True))
                p = e / jnp.sum(e, axis=-1, keepdims=True)
                PR[q, head] = p
                outs.append(mm(p.astype(BF16), v2))
            attQ[at_q, lanes(QC * r + 128 * j, 128)] = jnp.where(low, outs[0], outs[1]).astype(BF16)

    loop(2 * S, lambda q: attend(2 * S * (1 - xx) + q))
    go(needed)
    ag_forward(3)
    loop(2 * S, lambda q: attend(2 * S * xx + q))
    go(near_needed)
    go(near_rest)
    ZR = R["ZR"]
    if relays:
        for k, end in ((0, 0), (2, 3)):

            @pl.when(z == end)
            def _():
                for unit in range(4):
                    ZR[unit, k] = jnp.zeros((B, FC), BF16)

    needed.wait_recv()
    go(passed)
    wo_forward()
    ag_forward(4)
    wo_finish()
    near_needed.wait_recv()
    passed.wait_recv()

    x1, dx1, acc = R["x1"], R["dx1"], R["acc"]

    def mix(i):
        x = tok[at(step * i, step), :].astype(F32) + mm(attQ[at(T * r + step * i, step), :], WO[...])
        x1[at(step * i, step), :] = x
        inv = lax.rsqrt(jnp.mean(x * x, axis=-1, keepdims=True) + EPSILON)
        h2Q[at(T * r + step * i, step), :] = (x * inv * GA[1:2, :]).astype(BF16)

    loop(T // step, mix)
    h2_start()
    go(rest)
    ag_forward(5)
    dy_finish()
    ag_forward(6)
    ag_finish(2)
    ag_finish(3)
    h2_forward()
    ag_finish(4)
    ag_finish(5)

    hid, dgdu = R["hid"], R["dgdu"]

    def ffn(half, role):
        def body(i):
            at_i = at(T * role + L * i, L)
            both = mm(h2Q[at_i, :], WB[:, half * FC : (half + 1) * FC])
            gate, up = both[:, 0:HF], both[:, HF:FC]
            sigma = 1.0 / (1.0 + jnp.exp(-gate))
            silu = gate * sigma
            hid[at_i, half * HF : (half + 1) * HF] = (silu * up).astype(BF16)
            d_hidden = mm(dyQ[at_i, :], WC[half * HF : (half + 1) * HF, :], NT)
            d_gate = d_hidden * up * (sigma * (1.0 + gate * (1.0 - sigma)))
            dgdu[at_i, half * FC : half * FC + HF] = d_gate.astype(BF16)
            dgdu[at_i, half * FC + HF : (half + 1) * FC] = (d_hidden * silu).astype(BF16)

        loop(T // L, body)

    ffn(0, r)
    ag_forward(7)
    h2_finish()
    rest.wait_recv()
    go(passed_rest)
    ffn(0, r_sib)
    ffn(0, r_par)
    ffn(0, r_dia)

    YS, YR, ZR, ZX, QS, QR = (R[k] for k in ("YS", "YR", "ZR", "ZX", "QS", "QR"))
    y_sem, z_sem, x_sem = ([take(size) for _ in range(4)] for size in (Z, Z - 1, 1))

    def gradient(unit, group, store):
        at_g = lanes(B * group, B)
        if unit == 0:
            store(slice(0, FC), mm(hid[:, at_g], dyQ[...], TN))
        elif unit < 3:
            store(slice(0, FC), mm(h2Q[:, at_g], dgdu[:, (unit - 1) * FC : unit * FC], TN))
        else:
            store(slice(0, 3 * QC), mm(h1Q[:, at_g], WC[:, 0 : 3 * QC], TN))
            store(slice(3 * QC, 4 * QC), mm(attQ[:, at_g], R["daR"][...], TN))

    slots = {1: 0, 2: 1, 0: 2, 3: 0}

    def y_copy(unit, i):
        return remote(YS.at[slots[unit], i], YR.at[unit, i], peer, y_sem[unit] + i)

    def z_copy(unit, d, i=0):
        return remote(YR.at[unit, i], ZR.at[unit, d - 1], z_dev(d), z_sem[unit] + d - 1)

    def x_copy(unit, i=0):
        return remote(YR.at[unit, i], ZX.at[unit], (1 + lax.div(z, 2)) * 8 + y * 4 + r, x_sem[unit])

    def target(unit, i):
        if not relays:
            return lax.rem(z + 1 + i, Z)
        even = 1 - lax.rem(z, 2)
        if unit == 0:
            return i + even * (1 - 2 * (i % 2 if isinstance(i, int) else lax.rem(i, 2)))
        o = (2 * i) % 3 + 3 * (i // 3) if isinstance(i, int) else lax.rem(2 * i, 3) + 3 * lax.div(i, 3)
        return o + even * (3 - 2 * o)

    def own_place(unit):
        if not relays:
            return Z - 1
        return 1 + 2 * lax.div(z, 2) if unit == 0 else 3 - lax.div(z * (3 - z), 2)

    def rs_first(unit, begin=0, count=Z):
        if unit == 3:
            for i in range(Z):
                y_copy(1, i).wait_send()

        def body(i):
            place = begin + i

            def store(cols, value):
                YS[slots[unit], place, :, cols] = value.astype(BF16)

            gradient(unit, 2 * target(unit, place) + 1 - y, store)
            y_copy(unit, place).start()

        loop(count, body)

    def rs_step(unit, i):
        goal = target(unit, i)
        d = lax.rem(goal + Z - z, Z)
        y_copy(unit, i).wait_recv()

        def store(cols, value):
            YR[unit, i, :, cols] = (value + YR[unit, i, :, cols].astype(F32)).astype(BF16)

        gradient(unit, 2 * goal + y, store)
        if not relays:
            pl.when(d != 0)(lambda: z_copy(unit, d, i).start())
            return
        far = outer & (goal + z == 3)
        pl.when(far)(lambda: x_copy(unit, i).start())
        pl.when((d != 0) & jnp.logical_not(far | (inner & (d == 2))))(lambda: z_copy(unit, d, i).start())

    def rs_relay(unit):
        i = 5 - 2 * z if unit == 0 else 3
        if relays:

            @pl.when(inner)
            def _():
                x_copy(unit).wait_recv()
                YR[unit, i] = (YR[unit, i].astype(F32) + ZX[unit].astype(F32)).astype(BF16)
                z_copy(unit, 2, i).start()

    def rs_second(unit, begin=0, count=Z):
        loop(count, lambda i: rs_step(unit, begin + i))

    quad_copies = {}

    def rs_third(unit):
        for d in range(1, Z):
            if relays and d != 2:
                pl.when(z != (0 if d == 1 else Z - 1))(z_copy(unit, d).wait_recv)
            else:
                z_copy(unit, d).wait_recv()
        width = 256
        for j in range(FC // width):
            cols = slice(width * j, width * (j + 1))
            value = YR[unit, own_place(unit), :, cols].astype(F32)
            for i in range(1, Z):
                value = value + ZR[unit, i - 1, :, cols].astype(F32)
            if unit == 0:
                R["gd"][:, cols] = value
            else:
                QS[unit - 1, :, cols] = value.astype(BF16)
        if unit:
            QR[unit - 1, r] = QS[unit - 1, at(rows * r, rows), :]
            quad_copies[unit] = [
                go(remote(QS.at[unit - 1, at(rows * q, rows)], QR.at[unit - 1, r], dev)) for dev, q in quad
            ]

    def rs_last(unit):
        for copy in quad_copies[unit]:
            copy.wait_recv()
        R["parts"][unit - 1] = QR[unit - 1]

    rsS, rsR = R["rsS"], R["rsR"]

    def quad_sum(kind, prepare_block, partial, fill=None):
        width = 512
        tiles = [slice(width * j, width * (j + 1)) for j in range(D // width)]
        copies = [
            remote(rsS.at[0], rsR.at[kind, 0], sib),
            remote(rsS.at[1], rsR.at[kind, 1], sib),
            remote(rsS.at[2], rsR.at[kind, 2], par),
        ]

        def blocks(role, store):
            def body(i):
                for cols in tiles:
                    store(at(L * i, L), cols, partial(at(T * role + L * i, L), cols))

            loop(T // L, body)

        def to_dia(at_i, cols, value):
            rsS[1, at_i, cols] = value.astype(BF16)

        def to_par(at_i, cols, value):
            rsS[2, at_i, cols] = (value + rsR[kind, 1, at_i, cols].astype(F32)).astype(BF16)

        def to_sib(at_i, cols, value):
            rsS[0, at_i, cols] = value.astype(BF16)

        def keep(at_i, cols, value):
            acc[at_i, cols] = value

        prepare_block(r_dia)
        blocks(r_dia, to_dia)
        copies[1].start()
        prepare_block(r_par)
        copies[1].wait_recv()
        blocks(r_par, to_par)
        copies[2].start()
        if fill:
            fill(0)
        prepare_block(r_sib)
        blocks(r_sib, to_sib)
        copies[0].start()
        if fill:
            fill(1)
        prepare_block(r)
        blocks(r, keep)

        def finish():
            copies[0].wait_recv()
            copies[2].wait_recv()
            for copy in copies:
                copy.wait_send()

        return finish

    def summed(kind, at_i):
        return acc[at_i, :] + (rsR[kind, 0, at_i, :].astype(F32) + rsR[kind, 2, at_i, :].astype(F32))

    def nothing(role):
        return None

    rs_first(1)
    rs_first(0, 0, Z // 2)
    ag_finish(6)
    ag_finish(7)
    h2_sum = quad_sum(
        0, functools.partial(ffn, 1), lambda at_i, cols: mm(dgdu[at_i, :], WB[cols, :], NT),
        lambda i: rs_second(1, i, 1),
    )
    rs_second(1, 2, 1)
    rs_first(2)
    h2_sum()

    TT, TR = R["TT"], R["TR"]
    daS, daR, dattS, dattR = (R[k] for k in ("daS", "daR", "dattS", "dattR"))
    TT[0] = jnp.zeros((8, D), F32)

    def norm_back(v, d_out, gain, row):
        inv = lax.rsqrt(jnp.mean(v * v, axis=-1, keepdims=True) + EPSILON)
        TT[0, row : row + 1, :] += jnp.sum(d_out * (v * inv), axis=0, keepdims=True)
        d = d_out * gain
        return inv * d - v * (inv * inv * inv * jnp.mean(d * v, axis=-1, keepdims=True))

    def mix_back(i):
        at_i = at(step * i, step)
        d = norm_back(x1[at_i, :], summed(0, at_i), GA[1:2, :], 1)
        d = d + dyQ[at(T * r + step * i, step), :].astype(F32)
        dx1[at_i, :] = d
        daS[at_i, :] = d.astype(BF16)

    loop(T // step, mix_back)
    sendD = [remote(daS.at[:, lanes(QC * q, QC)], daR.at[at(T * r, T)], dev) for dev, q in quad]
    sendT = [remote(dattS.at[:, lanes(QC * q, QC)], dattR.at[at(T * r, T)], dev) for dev, q in quad]

    def out_back(i):
        at_i = at(step * i, step)
        dattS[at_i, :] = mm(daS[at_i, :], WO[...], NT).astype(BF16)

    loop(T // step, out_back)
    for copy in sendT:
        go(copy)
    for copy in sendD:
        go(copy)
    dattR[at(T * r, T), :] = dattS[:, lanes(QC * r, QC)]
    daR[at(T * r, T), :] = daS[:, lanes(QC * r, QC)]
    rs_second(1, 3, 1)
    rs_first(0, Z // 2, Z // 2)
    rs_relay(1)
    rs_second(0, 0, Z // 2)
    out_sum = quad_sum(1, nothing, lambda at_i, cols: mm(hid[at_i, :], WC[:, cols]))
    ag_drain(2)
    ag_drain(3)
    for copy in sendT:
        copy.wait_recv()

    def write_out(i):
        at_i = at(step * i, step)
        R["act"][at_i, :] = (x1[at_i, :] + summed(1, at_i)).astype(BF16)

    HG, BG = R["HG"], R["BG"]
    HG[...] = jnp.zeros(HG.shape, F32)
    BG[...] = jnp.zeros(BG.shape, F32)

    def fold(v):
        return jnp.sum(v.reshape(L // 8, 8, 128), axis=0)

    def prepare_back(raw, d, m, j, cosine, sine, factor):
        if factor != 1.0:
            d = d * factor
        d = d * cosine - swap(d) * sine
        inv = lax.rsqrt(per_head(raw * raw) / 64 + EPSILON)
        HG[m, j] += fold(d * (raw * inv))
        d = d * small[2 + m : 3 + m, :]
        return inv * d - raw * (inv * inv * inv * (per_head(d * raw) / 64))

    def attend_back(q):
        at_q = at(L * q, L)
        _, same = masks(q)
        cosine, sine = CT[at_q, :], ST[at_q, :]
        for j in range(QC // 128):
            tile = slice(128 * j, 128 * (j + 1))
            q2, k2, v2, d2 = qr[at_q, tile], kr[at_q, tile], vb[at_q, tile], dattR[at_q, tile]
            dq, dk, dv = [], [], []
            for h in range(2):
                p = PR[q, 2 * j + h]
                dp = mm(d2 * heads[h], v2, NT)
                ds = (p * (dp - jnp.sum(p * dp, axis=-1, keepdims=True))).astype(BF16)
                wide = ds.astype(F32)
                BG[0, 2 * j + h] += fold(jnp.where(same, 0.0, wide))
                BG[1, 2 * j + h] += fold(jnp.where(same, wide, 0.0))
                dv.append(mm(p.astype(BF16), d2, TN))
                dq.append(mm(ds, k2))
                dk.append(mm(ds, q2, TN))
            d_query = jnp.where(low, dq[0], dq[1])
            d_key = jnp.where(low, dk[0], dk[1])
            d_query = prepare_back(qraw[at_q, tile], d_query, 0, j, cosine, sine, 0.125)
            d_key = prepare_back(kraw[at_q, tile], d_key, 1, j, cosine, sine, 1.0)
            WC[at_q, tile] = d_query.astype(BF16)
            WC[at_q, QC + 128 * j : QC + 128 * (j + 1)] = d_key.astype(BF16)
            WC[at_q, 2 * QC + 128 * j : 2 * QC + 128 * (j + 1)] = jnp.where(low, dv[0], dv[1]).astype(BF16)

    def attend_and_step(i):
        for q in range(S):
            attend_back(S * i + q)
        rs_step(2, i)

    loop(4, attend_and_step)
    for copy in sendD + [near_rest, passed_rest]:
        copy.wait_recv()
    rs_first(3)
    rs_relay(2)
    out_sum()
    loop(T // step, write_out)
    in_sum = quad_sum(
        2, nothing, lambda at_i, cols: mm(WC[at_i, 0 : 3 * QC], WA[cols, 0 : 3 * QC], NT),
        lambda i: rs_second(0, Z // 2 + i, 1),
    )
    rs_relay(0)
    for k in range(len(chunks)):
        if k not in (2, 3):
            ag_drain(k)
    rs_third(1)
    in_sum()

    def input_back(i):
        at_i = at(step * i, step)
        d = norm_back(tok[at_i, :].astype(F32), summed(2, at_i), GA[0:1, :], 0)
        R["ig"][at_i, :] = (dx1[at_i, :] + d).astype(BF16)

    loop(T // step, input_back)

    for m in range(2):
        value = HG[m, 0]
        for j in range(1, QC // 128):
            value = value + HG[m, j]
        TT[0, 2:3, 128 * m : 128 * (m + 1)] = jnp.sum(value, axis=0, keepdims=True)
    for m in range(2):
        line = jnp.zeros((1, 128), F32)
        for h in range(QC // 64):
            line = line + jnp.where(spot == QC // 64 * r + h, jnp.sum(BG[m, h]), 0.0)
        TT[0, 3 + m : 4 + m, 0:128] = line
    t1, t2, t3, t_finish = tile_sum(TT, TR)
    t1()
    rs_second(3, 0, 3)
    t2()
    rs_second(3, 3, 1)
    rs_relay(3)
    rs_third(2)
    rs_last(1)
    t3()
    rs_third(0)
    rs_third(3)
    rs_last(2)
    R["tot"][...] = t_finish()
    rs_last(3)
    for copy in sent:
        copy.wait_send()
    for unit in range(4):
        for i in range(Z):
            if unit != 1:
                y_copy(unit, i).wait_send()
            if i:
                nearby(i, z_copy(unit, i).wait_send)
        if relays:
            pl.when(outer)(x_copy(unit).wait_send)


LAST = ("act", "ig", "gq", "gk", "gv", "go", "gg", "gu", "gd", "ga", "gf", "ghq", "ghk", "gb")


def finishing(s, *refs):
    names = tuple(name + "_in" for name in OUTPUTS) + LAST
    R = dict(zip(names, refs, strict=True))
    D, rows, G, QC, FC, B, HD, H = (s[k] for k in ("D", "rows", "G", "QC", "FC", "B", "HD", "H"))
    HF = FC // 2
    for name in ("act", "ig", "gd"):
        R[name][...] = R[name + "_in"][...]
    parts = R["parts_in"]
    for q in range(4):
        for m, name in enumerate(("gq", "gk", "gv", "go")):
            R[name][:, QC * q : QC * (q + 1)] = parts[2, q, :, QC * m : QC * (m + 1)].astype(F32)
        for j in range(G):
            half, within = divmod(B * j, HF)
            target = slice(B * (4 * j + q), B * (4 * j + q) + B)
            R["gg"][:, target] = parts[half, q, :, within : within + B].astype(F32)
            R["gu"][:, target] = parts[half, q, :, HF + within : HF + within + B].astype(F32)
    tot = R["tot_in"]
    own = lax.axis_index("fsdp") * rows
    mine = pltpu.roll(tot[:, lanes(128 * lax.div(own, 128), 128)], lax.rem(128 - lax.rem(own, 128), 128), 1)
    R["ga"][...] = mine[0:1, 0:rows]
    R["gf"][...] = mine[1:2, 0:rows]
    both = tot[:, 0:256]
    both = both + pltpu.roll(both, 256 - HD, 1)
    R["ghq"][...] = both[2:3, 0:HD]
    R["ghk"][...] = both[2:3, 128 : 128 + HD]
    R["gb"][...] = tot[3:5, 0:H]


def layer(s, tokens, segment_ids, variate_ids, time_ids, w_query, w_key, w_value, w_out, w_gate, w_up, w_down,
          gain_attn, gain_ffn, gain_query, gain_key, variate_bias, cotangent):
    D, T, rows, B, FF, FC, HD, H = (s[k] for k in ("D", "T", "rows", "B", "FF", "FC", "HD", "H"))
    lines = [
        gain_attn[None], gain_ffn[None], jnp.tile(gain_query[None], (1, 2)), jnp.tile(gain_key[None], (1, 2)),
        variate_bias,
    ]
    small, line = jnp.zeros((8, 128), F32), 0
    for piece in lines:
        high, wide = piece.shape
        small = small + jnp.pad(piece.astype(F32), ((line, 8 - line - high), (0, 128 - wide)))
        line += high
    scratch = scratch_of(s)
    names = INPUTS + OUTPUTS + tuple(scratch)
    vmem, anywhere = pl.BlockSpec(memory_space=pltpu.VMEM), pl.BlockSpec(memory_space=pl.ANY)
    here = {"seg", "var", "tim", "small"}

    def shape(*dims, kind=F32):
        return jax.ShapeDtypeStruct(dims, kind)

    tokens_shape = shape(T, D, kind=BF16)
    outs = pl.pallas_call(
        functools.partial(fused, s, names),
        out_shape=[tokens_shape, tokens_shape, shape(B, D), shape(3, 4, rows, FC, kind=BF16), shape(8, D)],
        in_specs=[vmem if name in here else anywhere for name in INPUTS],
        out_specs=[vmem] * len(OUTPUTS),
        scratch_shapes=list(scratch.values()),
        compiler_params=pltpu.CompilerParams(
            collective_id=0, has_side_effects=True, vmem_limit_bytes=64 << 20
        ),
        name="fused_layer",
    )(
        tokens.reshape(T, D), cotangent.reshape(T, D), segment_ids, variate_ids, time_ids,
        w_query, w_key, w_value, w_out, w_gate, w_up, w_down, small,
    )
    last = pl.pallas_call(
        functools.partial(finishing, s),
        out_shape=[tokens_shape, tokens_shape] + [shape(rows, D)] * 4 + [shape(rows, FF)] * 2
        + [shape(B, D), shape(1, rows), shape(1, rows), shape(1, HD), shape(1, HD), shape(2, H)],
        in_specs=[vmem] * len(OUTPUTS),
        out_specs=[vmem] * len(LAST),
        name="finishing",
    )(*outs)
    flat = [value.reshape(-1) for value in last[9:13]]
    return (last[0].reshape(tokens.shape), last[1].reshape(tokens.shape), *last[2:9], *flat, last[13])


def local(tokens, segment_ids, variate_ids, time_ids, *rest):
    s = sizes_of(lax.axis_size("fsdp"), tokens, rest[0], rest[4], rest[9], rest[11])
    chosen = functools.partial(layer, s) if fits(s) else plain
    return chosen(tokens, segment_ids, variate_ids, time_ids, *rest)


def solution(mesh):
    placed = (
        P("fsdp", None, None),
        P("fsdp", None),
        P("fsdp", None),
        P("fsdp", None),
        P("fsdp", None),
        P("fsdp", None),
        P("fsdp", None),
        P("fsdp", None),
        P("fsdp", None),
        P("fsdp", None),
        P("fsdp", None),
        P("fsdp"),
        P("fsdp"),
        P(),
        P(),
        P(),
        P("fsdp", None, None),
    )
    return jax.shard_map(
        local,
        mesh=mesh,
        in_specs=placed,
        out_specs=(
            P("fsdp", None, None),
            P("fsdp", None, None),
            P("fsdp", None),
            P("fsdp", None),
            P("fsdp", None),
            P("fsdp", None),
            P("fsdp", None),
            P("fsdp", None),
            P("fsdp", None),
            P("fsdp"),
            P("fsdp"),
            P(),
            P(),
            P(),
        ),
        check_vma=False,
    )
```

```python
import functools
import math

import jax
import jax.numpy as jnp
from jax import lax
from jax.experimental import pallas as pl
from jax.experimental.pallas import tpu as pltpu
from jax.sharding import PartitionSpec as P

EPSILON = 1e-05


def normalize(values, scale_gain):
    return (
        values * lax.rsqrt(jnp.mean(values * values, axis=-1, keepdims=True) + EPSILON) * scale_gain
    )


def rotate(values, moments):
    halfway = values.shape[-1] // 2
    frequency = jnp.exp(-math.log(10000.0) * jnp.arange(halfway).astype(jnp.float32) / halfway)
    angles = moments.astype(jnp.float32)[:, None] * frequency[None, :]
    cosine = jnp.cos(angles)[:, None, :]
    sine_part = jnp.sin(angles)[:, None, :]
    former = values[..., :halfway]
    latter = values[..., halfway:]
    return jnp.concatenate(
        [former * cosine - latter * sine_part, former * sine_part + latter * cosine], axis=-1
    )


def prepare(raw_heads, head_gain, moments, factor):
    return rotate(normalize(raw_heads, head_gain), moments) * factor


def swiglu(gate_act, up_act):
    return jax.nn.silu(gate_act) * up_act


def attention_masks(segments, variates):
    length = segments.shape[0]
    diagonal = jnp.arange(length)[:, None] == jnp.arange(length)[None, :]
    allowed = (segments[:, None] == segments[None, :]) & ((segments[None, :] != 0) | diagonal)
    same_var = variates[:, None] == variates[None, :]
    return (allowed, same_var)


def scoring(q_rot, k_rot, bias_table, allowed, same_var):
    scores = jnp.einsum("qhe,khe->hqk", q_rot, k_rot, preferred_element_type=jnp.float32)
    scores = scores + jnp.where(
        same_var[None], bias_table[1][:, None, None], bias_table[0][:, None, None]
    )
    return jnp.where(allowed[None], scores, -1000000000.0)


def project(left, right):
    return jnp.dot(left, right, preferred_element_type=jnp.float32)


def across(left, right):
    return lax.dot_general(
        left, right, (((0,), (0,)), ((), ())), preferred_element_type=jnp.float32
    )


def against(left, weight):
    return lax.dot_general(
        left, weight, (((1,), (1,)), ((), ())), preferred_element_type=jnp.float32
    )


def forward(inputs_low, weights, side_params, segments, variates, moments):
    w_query, w_key, w_value, w_out, w_gate, w_up, w_down, gain_attn, gain_ffn = weights
    gain_query, gain_key, bias_table = side_params
    length, model_width = inputs_low.shape
    head_count = bias_table.shape[1]
    head_dim = gain_query.shape[0]
    inputs = inputs_low.astype(jnp.float32)
    normed = normalize(inputs, gain_attn.astype(jnp.float32)).astype(jnp.bfloat16)
    queries = project(normed, w_query).reshape(length, head_count, head_dim)
    key_raw = project(normed, w_key).reshape(length, head_count, head_dim)
    v_low = project(normed, w_value).reshape(length, head_count, head_dim).astype(jnp.bfloat16)
    q_rot = prepare(queries, gain_query, moments, head_dim ** (-0.5)).astype(jnp.bfloat16)
    k_rot = prepare(key_raw, gain_key, moments, 1.0).astype(jnp.bfloat16)
    allowed, same_var = attention_masks(segments, variates)
    scores = scoring(q_rot, k_rot, bias_table, allowed, same_var)
    maximum = jnp.max(scores, axis=-1, keepdims=True)
    exponent = jnp.exp(scores - maximum)
    row_total = jnp.sum(exponent, axis=-1, keepdims=True)
    log_total = maximum + jnp.log(row_total)
    softmax_probs = (exponent / row_total).astype(jnp.bfloat16)
    attended = jnp.einsum("hqk,khe->qhe", softmax_probs, v_low, preferred_element_type=jnp.float32)
    attended = attended.reshape(length, model_width).astype(jnp.bfloat16)
    mixed_state = inputs + project(attended, w_out)
    normed_ffn = normalize(mixed_state, gain_ffn.astype(jnp.float32)).astype(jnp.bfloat16)
    gate_act = project(normed_ffn, w_gate)
    up_act = project(normed_ffn, w_up)
    hidden = swiglu(gate_act, up_act).astype(jnp.bfloat16)
    result = mixed_state + project(hidden, w_down)
    kept_state = (
        inputs,
        normed,
        queries,
        key_raw,
        q_rot,
        k_rot,
        v_low,
        log_total,
        attended,
        mixed_state,
        normed_ffn,
        gate_act,
        up_act,
        hidden,
    )
    return (result, kept_state)


def backward(upstream, kept_state, weights, side_params, segments, variates, moments):
    (
        inputs,
        normed,
        queries,
        key_raw,
        q_rot,
        k_rot,
        v_low,
        log_total,
        attended,
        mixed_state,
        normed_ffn,
        gate_act,
        up_act,
        hidden,
    ) = kept_state
    w_query, w_key, w_value, w_out, w_gate, w_up, w_down, gain_attn, gain_ffn = weights
    gain_query, gain_key, bias_table = side_params
    length, head_count, head_dim = queries.shape
    grad_down = across(hidden, upstream)
    d_hidden = against(upstream, w_down)
    _, pullback = jax.vjp(swiglu, gate_act, up_act)
    d_gate, d_up = pullback(d_hidden)
    d_gate = d_gate.astype(jnp.bfloat16)
    d_up = d_up.astype(jnp.bfloat16)
    grad_gate = across(normed_ffn, d_gate)
    grad_up = across(normed_ffn, d_up)
    d_normed_ffn = against(d_gate, w_gate) + against(d_up, w_up)
    _, pullback = jax.vjp(normalize, mixed_state, gain_ffn.astype(jnp.float32))
    d_mixed, grad_gain_ffn = pullback(d_normed_ffn)
    d_mixed = d_mixed + upstream.astype(jnp.float32)
    d_branch = d_mixed.astype(jnp.bfloat16)
    grad_out = across(attended, d_branch)
    d_attended = against(d_branch, w_out).astype(jnp.bfloat16).reshape(length, head_count, head_dim)
    allowed, same_var = attention_masks(segments, variates)
    scores = scoring(q_rot, k_rot, bias_table, allowed, same_var)
    softmax_probs = jnp.exp(scores - log_total)
    d_probs = jnp.einsum("qhe,khe->hqk", d_attended, v_low, preferred_element_type=jnp.float32)
    d_values = jnp.einsum(
        "hqk,qhe->khe",
        softmax_probs.astype(jnp.bfloat16),
        d_attended,
        preferred_element_type=jnp.float32,
    )
    d_values = d_values.reshape(length, head_count * head_dim).astype(jnp.bfloat16)
    weighted = jnp.sum(softmax_probs * d_probs, axis=-1, keepdims=True)
    d_scores = (softmax_probs * (d_probs - weighted)).astype(jnp.bfloat16)
    d_float = d_scores.astype(jnp.float32)
    same_sum = jnp.sum(jnp.where(same_var[None], d_float, 0.0), axis=(1, 2))
    other_sum = jnp.sum(jnp.where(same_var[None], 0.0, d_float), axis=(1, 2))
    grad_bias = jnp.stack([other_sum, same_sum])
    d_qrot = jnp.einsum("hqk,khe->qhe", d_scores, k_rot, preferred_element_type=jnp.float32)
    d_krot = jnp.einsum("hqk,qhe->khe", d_scores, q_rot, preferred_element_type=jnp.float32)
    factor = head_dim ** (-0.5)
    _, pullback = jax.vjp(
        lambda raw_heads, head_gain: prepare(raw_heads, head_gain, moments, factor),
        queries,
        gain_query,
    )
    d_queries, grad_gain_query = pullback(d_qrot)
    _, pullback = jax.vjp(
        lambda raw_heads, head_gain: prepare(raw_heads, head_gain, moments, 1.0), key_raw, gain_key
    )
    d_keys, grad_gain_key = pullback(d_krot)
    d_queries = d_queries.reshape(length, head_count * head_dim).astype(jnp.bfloat16)
    d_keys = d_keys.reshape(length, head_count * head_dim).astype(jnp.bfloat16)
    grad_query = across(normed, d_queries)
    grad_key = across(normed, d_keys)
    grad_value = across(normed, d_values)
    d_normed = against(d_queries, w_query) + against(d_keys, w_key) + against(d_values, w_value)
    _, pullback = jax.vjp(normalize, inputs, gain_attn.astype(jnp.float32))
    d_inputs, grad_gain_attn = pullback(d_normed)
    row_grads = jnp.concatenate(
        [grad_query, grad_key, grad_value, grad_out, grad_gate, grad_up], axis=1
    )
    small = (grad_gain_query, grad_gain_key, grad_bias, grad_gain_attn, grad_gain_ffn)
    return (d_inputs + d_mixed, row_grads, grad_down, small)


def plain(
    tokens,
    segment_ids,
    variate_ids,
    time_ids,
    w_query,
    w_key,
    w_value,
    w_out,
    w_gate,
    w_up,
    w_down,
    gain_attn,
    gain_ffn,
    gain_query,
    gain_key,
    variate_bias,
    cotangent,
):
    devices = lax.axis_size("fsdp")
    owner = lax.axis_index("fsdp")
    width = w_query.shape[1]
    hidden_width = w_gate.shape[1]
    own_rows = w_query.shape[0]
    own_down = w_down.shape[0]
    side_params = (
        gain_query.astype(jnp.float32),
        gain_key.astype(jnp.float32),
        variate_bias.astype(jnp.float32),
    )
    rows_total = jnp.zeros((own_rows * devices, 4 * width + 2 * hidden_width), jnp.float32)
    down_total = jnp.zeros((own_down * devices, width), jnp.float32)
    side_totals = (
        jnp.zeros(gain_query.shape, jnp.float32),
        jnp.zeros(gain_key.shape, jnp.float32),
        jnp.zeros(variate_bias.shape, jnp.float32),
        jnp.zeros((own_rows * devices,), jnp.float32),
        jnp.zeros((own_rows * devices,), jnp.float32),
    )
    results = []
    input_grads = []
    for micro_index in range(tokens.shape[0]):
        segments = segment_ids[micro_index]
        variates = variate_ids[micro_index]
        moments = time_ids[micro_index]
        forward_weights = (
            lax.all_gather(w_query, "fsdp", axis=0, tiled=True),
            lax.all_gather(w_key, "fsdp", axis=0, tiled=True),
            lax.all_gather(w_value, "fsdp", axis=0, tiled=True),
            lax.all_gather(w_out, "fsdp", axis=0, tiled=True),
            lax.all_gather(w_gate, "fsdp", axis=0, tiled=True),
            lax.all_gather(w_up, "fsdp", axis=0, tiled=True),
            lax.all_gather(w_down, "fsdp", axis=0, tiled=True),
            lax.all_gather(gain_attn, "fsdp", axis=0, tiled=True),
            lax.all_gather(gain_ffn, "fsdp", axis=0, tiled=True),
        )
        result, kept_state = forward(
            tokens[micro_index], forward_weights, side_params, segments, variates, moments
        )
        results.append(result.astype(jnp.bfloat16))
        backward_weights = (
            lax.all_gather(w_query, "fsdp", axis=0, tiled=True),
            lax.all_gather(w_key, "fsdp", axis=0, tiled=True),
            lax.all_gather(w_value, "fsdp", axis=0, tiled=True),
            lax.all_gather(w_out, "fsdp", axis=0, tiled=True),
            lax.all_gather(w_gate, "fsdp", axis=0, tiled=True),
            lax.all_gather(w_up, "fsdp", axis=0, tiled=True),
            lax.all_gather(w_down, "fsdp", axis=0, tiled=True),
            lax.all_gather(gain_attn, "fsdp", axis=0, tiled=True),
            lax.all_gather(gain_ffn, "fsdp", axis=0, tiled=True),
        )
        d_inputs, row_grads, down_grads, small = backward(
            cotangent[micro_index],
            kept_state,
            backward_weights,
            side_params,
            segments,
            variates,
            moments,
        )
        input_grads.append(d_inputs.astype(jnp.bfloat16))
        rows_total = rows_total + row_grads
        down_total = down_total + down_grads
        side_totals = tuple((running + fresh for running, fresh in zip(side_totals, small)))
    owned_rows = lax.psum_scatter(rows_total, "fsdp", scatter_dimension=0, tiled=True)
    owned_down = lax.psum_scatter(down_total, "fsdp", scatter_dimension=0, tiled=True)
    shared = lax.psum(
        (side_totals[0], side_totals[1], side_totals[2], side_totals[3], side_totals[4]), "fsdp"
    )
    gain_attn_own = lax.dynamic_slice_in_dim(shared[3], owner * own_rows, own_rows, 0)
    gain_ffn_own = lax.dynamic_slice_in_dim(shared[4], owner * own_rows, own_rows, 0)
    grad_query = owned_rows[:, 0:width]
    grad_key = owned_rows[:, width : 2 * width]
    grad_value = owned_rows[:, 2 * width : 3 * width]
    grad_out = owned_rows[:, 3 * width : 4 * width]
    grad_gate = owned_rows[:, 4 * width : 4 * width + hidden_width]
    grad_up = owned_rows[:, 4 * width + hidden_width :]
    return (
        jnp.stack(results),
        jnp.stack(input_grads),
        grad_query,
        grad_key,
        grad_value,
        grad_out,
        grad_gate,
        grad_up,
        owned_down,
        gain_attn_own,
        gain_ffn_own,
        shared[0],
        shared[1],
        shared[2],
    )


F32 = jnp.float32
BF16 = jnp.bfloat16
MESH = pl.DeviceIdType.MESH
NT = (((1,), (1,)), ((), ()))
TN = (((0,), (0,)), ((), ()))


def mm(left, right, dims=(((1,), (0,)), ((), ()))):
    return lax.dot_general(left, right, dims, preferred_element_type=F32)


def at(start, size):
    return pl.ds(pl.multiple_of(start, size), size)


def lanes(start, size):
    return pl.ds(pl.multiple_of(start, 128), size)


def loop(count, body):
    lax.fori_loop(0, count, lambda i, carry: (body(i), carry)[1], 0)


def sizes_of(devices, tokens, w_query, w_gate, gain_query, bias):
    seqs, length, width = tokens.shape
    own_rows, hidden = w_query.shape[0], w_gate.shape[1]
    return dict(
        n=devices, S=seqs, L=length, D=width, FF=hidden, rows=own_rows, T=seqs * length,
        G=devices // 4, Z=devices // 8, QC=width // 4, FC=hidden // 4, B=4 * own_rows,
        HD=gain_query.shape[0], H=bias.shape[1],
    )


def fits(s):
    return (
        s["n"] % 8 == 0 and s["rows"] % 16 == 0 and s["L"] == 128 and s["HD"] == 64
        and s["H"] * s["HD"] == s["D"] and s["QC"] % 128 == 0 and s["FF"] == 4 * s["D"]
        and s["B"] == 128 and s["FC"] // 2 % s["B"] == 0 and s["FC"] == s["D"]
    )


def scratch_of(s):
    n, S, L, D, rows, T, G, Z, QC, FC, B = (
        s[k] for k in ("n", "S", "L", "D", "rows", "T", "G", "Z", "QC", "FC", "B")
    )
    Q = 4 * T
    vm = pltpu.VMEM
    return dict(
        WA=vm((D, 4 * QC), BF16), WB=vm((D, 2 * FC), BF16), WC=vm((FC, D), BF16), WO=vm((D, D), BF16),
        SA=vm((4, rows, 4 * QC), BF16), SB=vm((4, rows, 2 * FC), BF16),
        h1Q=vm((Q, D), BF16), dyQ=vm((Q, D), BF16), attQ=vm((Q, D), BF16), h2Q=vm((Q, D), BF16),
        qraw=vm((Q, QC), F32), kraw=vm((Q, QC), F32),
        qr=vm((Q, QC), BF16), kr=vm((Q, QC), BF16), vb=vm((Q, QC), BF16),
        PR=vm((4 * S, QC // 64, L, L), F32), CT=vm((Q, 128), F32), ST=vm((Q, 128), F32),
        x1=vm((T, D), F32), dx1=vm((T, D), F32), acc=vm((T, D), F32),
        hid=vm((Q, FC), BF16), dgdu=vm((Q, 2 * FC), BF16),
        rsS=vm((3, T, D), BF16), rsR=vm((3, 3, T, D), BF16),
        daS=vm((T, D), BF16), daR=vm((Q, QC), BF16), dattS=vm((T, D), BF16), dattR=vm((Q, QC), BF16),
        YS=vm((3, Z, B, FC), BF16), YR=vm((4, Z, B, FC), BF16), ZR=vm((4, Z - 1, B, FC), BF16), ZX=vm((4, B, FC), BF16),
        FS=vm((Z, 2, B, FC // 2), BF16), FR=vm((Z - 1, 2, B, FC // 2), BF16), FX=vm((2, B, FC // 2), BF16),
        FT=vm((2, B, FC // 2), BF16), FK=vm((B, FC // 2), F32),
        QS=vm((3, B, FC), BF16), QR=vm((3, 4, rows, FC), BF16),
        idq=vm((4 * S, 8, L), F32),
        SW=vm((4, rows, D), BF16), SG=vm((2, rows, s["FF"]), BF16), TK=vm((T, D), BF16),
        GQ=vm((4, 8, B), F32), GA=vm((8, D), F32), load=pltpu.SemaphoreType.DMA((9,)),
        TT=vm((3, 8, D), F32), TR=vm((4 + Z, 8, D), F32),
        HG=vm((4, QC // 128, 8, 128), F32), BG=vm((2, QC // 64, 8, 128), F32),
        send=pltpu.SemaphoreType.DMA((192,)), recv=pltpu.SemaphoreType.DMA((192,)),
    )


INPUTS = (
    "tok", "cot", "seg", "var", "tim", "wq", "wk", "wv", "wo", "wg", "wu", "wd", "small",
)
OUTPUTS = ("act", "ig", "gd", "parts", "tot")


def fused(s, names, *refs):
    R = dict(zip(names, refs, strict=True))
    n, S, L, D, rows, T, G, Z, QC, FC, B = (
        s[k] for k in ("n", "S", "L", "D", "rows", "T", "G", "Z", "QC", "FC", "B")
    )
    HF = FC // 2
    Q = 4 * T
    me = lax.axis_index("fsdp")
    r, c, xx, g = lax.rem(me, 4), lax.rem(me, 2), lax.rem(lax.div(me, 2), 2), lax.div(me, 4)
    y, z = lax.rem(g, 2), lax.div(g, 2)
    r_sib, r_par = r + 1 - 2 * c, r + 2 - 4 * xx
    r_dia = r_sib + 2 - 4 * xx
    sib, par, dia = me - r + r_sib, me - r + r_par, me - r + r_dia
    peer = me + 4 - 8 * y
    quad = ((sib, r_sib), (par, r_par), (dia, r_dia))

    def at_z(step):
        return lax.rem(z + step, Z)

    def z_dev(step):
        return at_z(step) * 8 + y * 4 + r

    def z_src(step):
        return lax.rem(z + Z - step, Z)

    relays = Z == 4
    inner, outer = lax.rem(z + 1, 4) >= 2, lax.rem(z + 1, 4) < 2

    def nearby(step, action):
        if relays and step != 2:
            pl.when(z != (Z - 1 if step == 1 else 0))(action)
        else:
            action()

    used = [0]
    sent = []

    def take(count=1):
        used[0] += count
        return used[0] - count

    def remote(src, dst, device, sem=None, arrival=None):
        sem = take() if sem is None else sem
        arrival = sem if arrival is None else arrival
        return pltpu.make_async_remote_copy(
            src_ref=src, dst_ref=dst, send_sem=R["send"].at[sem], recv_sem=R["recv"].at[arrival],
            device_id=(device,), device_id_type=MESH,
        )

    def go(copy):
        copy.start()
        sent.append(copy)
        return copy

    barrier = pltpu.get_barrier_semaphore()
    others = [sib, par, dia, peer] + [z_dev(d) for d in range(1, Z)]
    for device in others:
        pl.semaphore_signal(barrier, inc=1, device_id=(device,), device_id_type=MESH)

    SA, SB, SW, SG, WA, WB, WC, WO = (R[k] for k in ("SA", "SB", "SW", "SG", "WA", "WB", "WC", "WO"))
    dyQ, h1Q, h2Q, attQ, tok = R["dyQ"], R["h1Q"], R["h2Q"], R["attQ"], R["TK"]
    places = [("wq", SW.at[0]), ("wk", SW.at[1]), ("wv", SW.at[2]), ("wo", SW.at[3]), ("wd", WC.at[at(B * g, B)])]
    places += [("tok", tok), ("wg", SG.at[0]), ("wu", SG.at[1]), ("cot", dyQ.at[at(T * r, T)])]
    loads = {}
    for i, (name, place) in enumerate(places):
        loads[name] = pltpu.make_async_copy(R[name], place, R["load"].at[i])
        loads[name].start()
    own = at(B * g + rows * r, rows)
    idq, small, GQ, GA = R["idq"], R["small"], R["GQ"], R["GA"]
    for q in range(S):
        idq[S * r + q, 0:1, :] = R["seg"][q : q + 1, :].astype(F32)
        idq[S * r + q, 1:2, :] = R["var"][q : q + 1, :].astype(F32)
        idq[S * r + q, 2:3, :] = R["tim"][q : q + 1, :].astype(F32)
        idq[S * r + q, 3:8, :] = jnp.zeros((5, L), F32)
    GQ[r] = pltpu.roll(small[...], rows * r, 1)
    for m, name in enumerate(("wq", "wk", "wv", "wo")):
        loads[name].wait()
        for q in range(4):
            SA[q, :, QC * m : QC * (m + 1)] = SW[m, :, QC * q : QC * (q + 1)]
    WA[own, :] = SA[r]
    pl.semaphore_wait(barrier, len(others))

    def tile_sum(tile, got):
        first = [remote(tile.at[0], got.at[i], dev) for i, (dev, _) in enumerate(quad)]
        second = [remote(tile.at[1], got.at[4 + z], z_dev(d)) for d in range(1, Z)]
        third = remote(tile.at[2], got.at[3], peer)

        def round1():
            for copy in first:
                go(copy)

        def round2():
            for copy in first:
                copy.wait_recv()
            value = (tile[0] + got[0]) + (got[1] + got[2])
            tile[1] = value
            got[4 + z] = value
            for copy in second:
                go(copy)

        def round3():
            for copy in second:
                copy.wait_recv()
            value = got[4]
            for i in range(1, Z):
                value = value + got[4 + i]
            tile[2] = value
            go(third)

        def finish():
            third.wait_recv()
            return tile[2] + got[3]

        return round1, round2, round3, finish

    def quad_gather(block):
        to_sib, to_par = remote(block(r), block(r), sib), remote(block(r), block(r), par)
        passed = remote(block(r_par), block(r_par), sib)

        def start():
            go(to_par)
            go(to_sib)

        def forward():
            to_par.wait_recv()
            go(passed)

        def finish():
            to_sib.wait_recv()
            passed.wait_recv()

        return start, forward, finish

    chunks = [(WA, 0, 2 * QC), (WA, 2 * QC, 2 * QC), (WC, 0, D // 2), (WC, D // 2, D // 2)]
    chunks += [(WB, HF * k, HF) for k in range(4)] + [(GA, 0, B)]
    early, after = 7, {0: 2, 1: 3, 2: 4, 3: 5, 4: 6}

    def piece(k, group):
        ref, start, size = chunks[k]
        if ref is GA:
            return ref.at[:, lanes(B * group, B)]
        return ref.at[at(B * group, B), pl.ds(start, size)]

    a_sem, f_sem, o_sem = ([take(size) for _ in chunks] for size in (Z - 1, 1, Z))
    b_sem, e_sem = take(Z - 1), take()

    def across_y(other):
        return y + other * (1 - 2 * y)

    def along(k, d, other=0):
        block = piece(k, 2 * z + across_y(other))
        return remote(block, block, z_dev(d), (b_sem if other else a_sem[k]) + d - 1)

    def over(k, d):
        block = piece(k, 2 * z_src(d) + y)
        return remote(block, block, peer, o_sem[k] + d)

    def relay(k, other=0):
        block, end = piece(k, 2 * z_src(2) + across_y(other)), lax.div(z, 2)
        sems = (e_sem, b_sem + 2 * end) if other else (f_sem[k], a_sem[k] + 2 * end)
        return remote(block, block, 3 * end * 8 + y * 4 + r, *sems)

    def near(k, d, action):
        if k == 8:
            action()
        else:
            nearby(d, action)

    def both(k):
        return (0, 1) if k == early else (0,)

    def ag_start(k):
        for other in both(k):
            for d in range(1, Z):
                near(k, d, along(k, d, other).start)

    def ag_own(k):
        over(k, 0).start()

    def ag_forward(k):
        first = lax.div(3 - z, 3)
        for i in range(1, Z):
            d = i if not relays or i == 2 else 1 + 2 * first if i == 1 else 3 - 2 * first
            for other in both(k):
                along(k, d, other).wait_recv()
                if relays and i == 2 and k < 8:
                    pl.when(inner)(relay(k, other).start)
            if k != early:
                over(k, d).start()
        if k in after:
            ag_own(after[k])
        if 2 <= k <= 4:
            ag_start(k + 3)

    def ag_finish(k):
        for d in range(Z):
            if k != early:
                over(k, d).wait_recv()

    def ag_drain(k):
        for d in range(1 if k == early else Z):
            over(k, d).wait_send()
        for other in both(k):
            for d in range(1, Z):
                near(k, d, along(k, d, other).wait_send)
            if relays and k < 8:
                pl.when(inner)(relay(k, other).wait_send)

    sendG = [remote(GQ.at[r], GQ.at[r], dev) for dev, q in quad]
    sendA = [remote(SA.at[q], WA.at[own], dev) for dev, q in quad]
    sendB = [remote(SB.at[q], WB.at[own], dev) for dev, q in quad]
    mine = idq.at[pl.ds(S * r, S)]
    sendI = [remote(mine, mine, dev) for dev, q in quad]
    for copy in sendG + sendA + sendI:
        go(copy)
    loads["wd"].wait()
    for copy in sendG:
        copy.wait_recv()
    GA[:, lanes(B * g, B)] = (GQ[0] + GQ[1]) + (GQ[2] + GQ[3])
    ag_start(8)
    ag_own(8)
    for copy in sendA:
        copy.wait_recv()
    ag_start(0)
    ag_own(0)
    ag_start(1)
    ag_own(1)
    for name in ("wg", "wu"):
        loads[name].wait()
    for q in range(4):
        for j in range(G):
            half, within = divmod(B * j, HF)
            source = slice(B * (4 * j + q), B * (4 * j + q) + B)
            SB[q, :, half * FC + within : half * FC + within + B] = SG[0, :, source]
            SB[q, :, half * FC + HF + within : half * FC + HF + within + B] = SG[1, :, source]
    WB[own, :] = SB[r]
    for copy in sendB:
        go(copy)
    for copy in sendI:
        copy.wait_recv()

    lane = lax.broadcasted_iota(jnp.int32, (L, 128), 1)
    sub = lax.broadcasted_iota(jnp.int32, (L, 128), 0)
    front = lax.rem(lane, 64) < 32
    low = lane < 64
    freq = jnp.exp(-math.log(10000.0) * lax.rem(lane, 32).astype(F32) / 32)
    CT, ST = R["CT"], R["ST"]

    def tables(q):
        times = jnp.broadcast_to(idq[q, 2:3, :], (L, L)).T
        angles = times * freq
        CT[at(L * q, L), :] = jnp.cos(angles)
        sine = jnp.sin(angles)
        ST[at(L * q, L), :] = jnp.where(front, -sine, sine)

    loop(2 * S, tables)
    ag_forward(8)
    loop(2 * S, lambda q: tables(2 * S + q))
    loads["tok"].wait()
    ag_finish(8)
    step = 64

    def norm_in(i):
        x = tok[at(step * i, step), :].astype(F32)
        inv = lax.rsqrt(jnp.mean(x * x, axis=-1, keepdims=True) + EPSILON)
        h1Q[at(T * r + step * i, step), :] = (x * inv * GA[0:1, :]).astype(BF16)

    loop(T // step, norm_in)

    def token_block(ref):
        return lambda role: ref.at[at(T * role, T)]

    h1_start, h1_forward, h1_finish = quad_gather(token_block(h1Q))
    dy_start, dy_forward, dy_finish = quad_gather(token_block(dyQ))

    def att_block(chip, role):
        return attQ.at[at(2 * T * chip, 2 * T), lanes(QC * role, QC)]

    def att_copy(chip, role, device):
        return remote(att_block(chip, role), att_block(chip, role), device)

    needed, passed = att_copy(1 - xx, r, par), att_copy(xx, r_par, sib)
    near_needed, near_rest = att_copy(xx, r, sib), att_copy(1 - xx, r, sib)
    rest, passed_rest = att_copy(xx, r, par), att_copy(1 - xx, r_par, sib)
    wo_start, wo_forward, wo_finish = quad_gather(lambda role: WO.at[:, lanes(QC * role, QC)])
    h2_start, h2_forward, h2_finish = quad_gather(token_block(h2Q))
    h1_start()
    for copy in sendB:
        copy.wait_recv()
    ag_own(early)
    ag_forward(0)
    ag_start(2)
    h1_forward()
    ag_forward(1)
    ag_start(3)
    ag_start(4)
    loads["cot"].wait()
    dy_start()
    h1_finish()
    ag_finish(0)
    ag_finish(1)
    ag_forward(2)

    qraw, kraw, qr, kr, vb, PR = (R[k] for k in ("qraw", "kraw", "qr", "kr", "vb", "PR"))
    spot = lax.broadcasted_iota(jnp.int32, (1, 128), 1)
    bias = [
        [jnp.sum(jnp.where(spot == QC // 64 * r + h, small[4 + m : 5 + m, :], 0.0)) for h in range(QC // 64)]
        for m in range(2)
    ]

    def swap(v):
        return jnp.where(front, pltpu.roll(v, 96, 1), pltpu.roll(v, 32, 1))

    def per_head(v):
        first = jnp.sum(jnp.where(low, v, 0.0), axis=-1, keepdims=True)
        second = jnp.sum(jnp.where(low, 0.0, v), axis=-1, keepdims=True)
        return jnp.where(low, first, second)

    def project_heads(q):
        at_q = at(L * q, L)
        value = mm(h1Q[at_q, :], WA[:, 0 : 3 * QC])
        cosine, sine = CT[at_q, :], ST[at_q, :]
        for m, (raw, ready) in enumerate(((qraw, qr), (kraw, kr))):
            raw[at_q, :] = value[:, QC * m : QC * (m + 1)]
            for j in range(QC // 128):
                v = value[:, QC * m + 128 * j : QC * m + 128 * (j + 1)]
                inv = lax.rsqrt(per_head(v * v) / 64 + EPSILON)
                v = v * inv * small[2 + m : 3 + m, :]
                v = v * cosine + swap(v) * sine
                if m == 0:
                    v = v * 0.125
                ready[at_q, 128 * j : 128 * (j + 1)] = v.astype(BF16)
        vb[at_q, :] = value[:, 2 * QC : 3 * QC].astype(BF16)

    loop(4 * S, project_heads)
    WO[:, lanes(QC * r, QC)] = WA[:, 3 * QC : 4 * QC]
    wo_start()
    dy_forward()

    def masks(q):
        segment = jnp.broadcast_to(idq[q, 0:1, :], (L, L))
        variate = jnp.broadcast_to(idq[q, 1:2, :], (L, L))
        allowed = (segment == segment.T) & ((segment != 0.0) | (lane == sub))
        return allowed, variate == variate.T

    heads = [jnp.where(low, 1.0, 0.0).astype(BF16), jnp.where(low, 0.0, 1.0).astype(BF16)]

    def attend(q):
        at_q = at(L * q, L)
        allowed, same = masks(q)
        for j in range(QC // 128):
            tile = slice(128 * j, 128 * (j + 1))
            q2, k2, v2 = qr[at_q, tile], kr[at_q, tile], vb[at_q, tile]
            outs = []
            for h in range(2):
                head = 2 * j + h
                score = mm(q2 * heads[h], k2, NT) + jnp.where(same, bias[1][head], bias[0][head])
                score = jnp.where(allowed, score, -1000000000.0)
                e = jnp.exp(score - jnp.max(score, axis=-1, keepdims=True))
                p = e / jnp.sum(e, axis=-1, keepdims=True)
                PR[q, head] = p
                outs.append(mm(p.astype(BF16), v2))
            attQ[at_q, lanes(QC * r + 128 * j, 128)] = jnp.where(low, outs[0], outs[1]).astype(BF16)

    def attend_pair(q):
        attend(q)
        attend(q + 1)

    loop(S, lambda i: attend_pair(2 * S * (1 - xx) + 2 * i))
    go(needed)
    ag_forward(3)
    loop(S, lambda i: attend_pair(2 * S * xx + 2 * i))
    go(near_needed)
    go(near_rest)
    ZR, FR = R["ZR"], R["FR"]
    if relays:
        for k, end in ((0, 0), (2, 3)):

            @pl.when(z == end)
            def _():
                FR[k] = jnp.zeros((2, B, HF), BF16)
                for unit in range(4):
                    ZR[unit, k] = jnp.zeros((B, FC), BF16)

    needed.wait_recv()
    go(passed)
    wo_forward()
    over(early, 0).wait_recv()
    ag_forward(4)
    wo_finish()
    near_needed.wait_recv()
    passed.wait_recv()

    x1, dx1, acc = R["x1"], R["dx1"], R["acc"]

    wide = 256

    def mix_sum(j):
        cols = lanes(wide * j, wide)
        x1[:, cols] = tok[:, cols].astype(F32) + mm(attQ[at(T * r, T), :], WO[:, cols])

    loop(D // wide, mix_sum)

    def mix(i):
        x = x1[at(step * i, step), :]
        inv = lax.rsqrt(jnp.mean(x * x, axis=-1, keepdims=True) + EPSILON)
        h2Q[at(T * r + step * i, step), :] = (x * inv * GA[1:2, :]).astype(BF16)

    loop(T // step, mix)
    h2_start()
    go(rest)
    ag_forward(5)
    dy_finish()
    ag_forward(6)
    ag_finish(2)
    ag_finish(3)
    h2_forward()
    ag_finish(4)
    ag_finish(5)

    hid, dgdu = R["hid"], R["dgdu"]

    def ffn(half, role):
        at_r = at(T * role, T)

        def body(j):
            to_gate = lanes(half * FC + wide * j, wide)
            to_up = lanes(half * FC + HF + wide * j, wide)
            gate, up = mm(h2Q[at_r, :], WB[:, to_gate]), mm(h2Q[at_r, :], WB[:, to_up])
            sigma = 1.0 / (1.0 + jnp.exp(-gate))
            silu = gate * sigma
            hid[at_r, lanes(half * HF + wide * j, wide)] = (silu * up).astype(BF16)
            d_hidden = mm(dyQ[at_r, :], WC[at(half * HF + wide * j, wide), :], NT)
            d_gate = d_hidden * up * (sigma * (1.0 + gate * (1.0 - sigma)))
            dgdu[at_r, to_gate] = d_gate.astype(BF16)
            dgdu[at_r, to_up] = (d_hidden * silu).astype(BF16)

        loop(HF // wide, body)

    ffn(0, r)
    ag_forward(7)
    h2_finish()
    rest.wait_recv()
    go(passed_rest)
    ffn(0, r_sib)
    ffn(0, r_par)
    ffn(0, r_dia)

    YS, YR, ZR, ZX, QS, QR = (R[k] for k in ("YS", "YR", "ZR", "ZX", "QS", "QR"))
    y_sem, z_sem, x_sem = ([take(size) for _ in range(4)] for size in (Z, Z - 1, 1))

    def gradient(unit, group, store):
        at_g = lanes(B * group, B)
        if unit == 0:
            store(slice(0, FC), mm(hid[:, at_g], dyQ[...], TN))
        elif unit == 1:
            store(slice(HF, FC), mm(h2Q[:, at_g], dgdu[:, HF:FC], TN))
        elif unit == 2:
            store(slice(0, FC), mm(h2Q[:, at_g], dgdu[:, FC : 2 * FC], TN))
        else:
            store(slice(0, 3 * QC), mm(h1Q[:, at_g], WC[:, 0 : 3 * QC], TN))
            store(slice(3 * QC, 4 * QC), mm(attQ[:, at_g], R["daR"][...], TN))

    slots = {1: 0, 2: 1, 0: 2, 3: 0}

    def part(unit, ref):
        return ref.at[:, pl.ds(HF, HF)] if unit == 1 else ref

    def y_copy(unit, i):
        return remote(part(unit, YS.at[slots[unit], i]), part(unit, YR.at[unit, i]), peer, y_sem[unit] + i)

    def z_copy(unit, d, i=0):
        return remote(part(unit, YR.at[unit, i]), part(unit, ZR.at[unit, d - 1]), z_dev(d), z_sem[unit] + d - 1)

    middle = (1 + lax.div(z, 2)) * 8 + y * 4 + r

    def x_copy(unit, i=0):
        return remote(part(unit, YR.at[unit, i]), part(unit, ZX.at[unit]), middle, x_sem[unit])

    def target(unit, i):
        if not relays:
            return lax.rem(z + 1 + i, Z)
        even = 1 - lax.rem(z, 2)
        if unit == 0:
            return i + even * (1 - 2 * (i % 2 if isinstance(i, int) else lax.rem(i, 2)))
        o = (2 * i) % 3 + 3 * (i // 3) if isinstance(i, int) else lax.rem(2 * i, 3) + 3 * lax.div(i, 3)
        return o + even * (3 - 2 * o)

    def own_place(unit):
        if not relays:
            return Z - 1
        return 1 + 2 * lax.div(z, 2) if unit == 0 else 3 - lax.div(z * (3 - z), 2)

    def rs_first(unit, begin=0, count=Z):
        if unit == 3:
            for i in range(Z):
                y_copy(1, i).wait_send()

        def body(i):
            place = begin + i

            def store(cols, value):
                YS[slots[unit], place, :, cols] = value.astype(BF16)

            gradient(unit, 2 * target(unit, place) + 1 - y, store)
            y_copy(unit, place).start()

        loop(count, body)

    def rs_step(unit, i):
        goal = target(unit, i)
        d = lax.rem(goal + Z - z, Z)
        y_copy(unit, i).wait_recv()

        def store(cols, value):
            YR[unit, i, :, cols] = (value + YR[unit, i, :, cols].astype(F32)).astype(BF16)

        gradient(unit, 2 * goal + y, store)
        if not relays:
            pl.when(d != 0)(lambda: z_copy(unit, d, i).start())
            return
        far = outer & (goal + z == 3)
        pl.when(far)(lambda: x_copy(unit, i).start())
        pl.when((d != 0) & jnp.logical_not(far | (inner & (d == 2))))(lambda: z_copy(unit, d, i).start())

    def rs_relay(unit):
        i = 5 - 2 * z if unit == 0 else 3
        if relays:

            @pl.when(inner)
            def _():
                x_copy(unit).wait_recv()
                cols = slice(HF if unit == 1 else 0, FC)
                YR[unit, i, :, cols] = (YR[unit, i, :, cols].astype(F32) + ZX[unit, :, cols].astype(F32)).astype(BF16)
                z_copy(unit, 2, i).start()

    def rs_second(unit, begin=0, count=Z):
        loop(count, lambda i: rs_step(unit, begin + i))

    FS, FR, FX, FT, FK = (R[k] for k in ("FS", "FR", "FX", "FT", "FK"))
    fz_sem, fx_sem = take(Z - 1), take()
    last_over = remote(FT.at[0], FT.at[1], peer)

    def zf_copy(d, i=0):
        return remote(FS.at[i], FR.at[d - 1], z_dev(d), fz_sem + d - 1)

    def zf_far(i=0):
        return remote(FS.at[i], FX, middle, fx_sem)

    def zf_first():
        def body(i):
            goal = target(1, i)
            d = lax.rem(goal + Z - z, Z)
            for side in range(2):
                FS[i, side] = mm(h2Q[:, lanes(B * (2 * goal + side), B)], dgdu[:, 0:HF], TN).astype(BF16)
            if not relays:
                pl.when(d != 0)(lambda: zf_copy(d, i).start())
                return
            far = outer & (goal + z == 3)
            pl.when(far)(lambda: zf_far(i).start())
            pl.when((d != 0) & jnp.logical_not(far | (inner & (d == 2))))(lambda: zf_copy(d, i).start())

        loop(Z, body)

    def zf_relay():
        if relays:

            @pl.when(inner)
            def _():
                zf_far().wait_recv()
                FS[3] = (FS[3].astype(F32) + FX[...].astype(F32)).astype(BF16)
                zf_copy(2, 3).start()

    def zf_second():
        for d in range(1, Z):
            if relays and d != 2:
                pl.when(z != (0 if d == 1 else Z - 1))(zf_copy(d).wait_recv)
            else:
                zf_copy(d).wait_recv()

        def total(side):
            value = FS[own_place(1), side].astype(F32)
            for d in range(1, Z):
                value = value + FR[d - 1, side].astype(F32)
            return value

        FT[0] = total(1 - y).astype(BF16)
        go(last_over)
        FK[...] = total(y)

    quad_copies = {}

    def rs_third(unit):
        for d in range(1, Z):
            if relays and d != 2:
                pl.when(z != (0 if d == 1 else Z - 1))(z_copy(unit, d).wait_recv)
            else:
                z_copy(unit, d).wait_recv()
        width = 256
        if unit == 1:
            last_over.wait_recv()
        for j in range(FC // width):
            cols = slice(width * j, width * (j + 1))
            if unit == 1 and width * j < HF:
                value = FK[:, cols] + FT[1, :, cols].astype(F32)
            else:
                value = YR[unit, own_place(unit), :, cols].astype(F32)
                for i in range(1, Z):
                    value = value + ZR[unit, i - 1, :, cols].astype(F32)
            if unit == 0:
                R["gd"][:, cols] = value
            else:
                QS[unit - 1, :, cols] = value.astype(BF16)
        if unit:
            QR[unit - 1, r] = QS[unit - 1, at(rows * r, rows), :]
            quad_copies[unit] = [
                go(remote(QS.at[unit - 1, at(rows * q, rows)], QR.at[unit - 1, r], dev)) for dev, q in quad
            ]

    def rs_last(unit):
        for copy in quad_copies[unit]:
            copy.wait_recv()
        R["parts"][unit - 1] = QR[unit - 1]

    rsS, rsR = R["rsS"], R["rsR"]

    def quad_sum(kind, prepare_block, partial, fill=None):
        copies = [
            remote(rsS.at[0], rsR.at[kind, 0], sib),
            remote(rsS.at[1], rsR.at[kind, 1], sib),
            remote(rsS.at[2], rsR.at[kind, 2], par),
        ]

        def blocks(role, store):
            def body(j):
                store(lanes(wide * j, wide), partial(at(T * role, T), wide * j))

            loop(D // wide, body)

        def to_dia(cols, value):
            rsS[1, :, cols] = value.astype(BF16)

        def to_par(cols, value):
            rsS[2, :, cols] = (value + rsR[kind, 1, :, cols].astype(F32)).astype(BF16)

        def to_sib(cols, value):
            rsS[0, :, cols] = value.astype(BF16)

        def keep(cols, value):
            acc[:, cols] = value

        prepare_block(r_dia)
        blocks(r_dia, to_dia)
        copies[1].start()
        prepare_block(r_par)
        copies[1].wait_recv()
        blocks(r_par, to_par)
        copies[2].start()
        if fill:
            fill(0)
        prepare_block(r_sib)
        blocks(r_sib, to_sib)
        copies[0].start()
        if fill:
            fill(1)
        prepare_block(r)
        blocks(r, keep)

        def finish():
            copies[0].wait_recv()
            copies[2].wait_recv()
            for copy in copies:
                copy.wait_send()

        return finish

    def summed(kind, at_i):
        return acc[at_i, :] + (rsR[kind, 0, at_i, :].astype(F32) + rsR[kind, 2, at_i, :].astype(F32))

    def nothing(role):
        return None

    zf_first()
    rs_first(1)
    rs_first(0, 0, Z // 2)
    ag_finish(6)
    ag_finish(7)
    h2_sum = quad_sum(
        0, functools.partial(ffn, 1), lambda at_r, j: mm(dgdu[at_r, :], WB[at(j, wide), :], NT),
        lambda i: (zf_relay() if i else None, rs_second(1, i, 1)),
    )
    rs_second(1, 2, 1)
    rs_first(2)
    h2_sum()

    TT, TR = R["TT"], R["TR"]
    daS, daR, dattS, dattR = (R[k] for k in ("daS", "daR", "dattS", "dattR"))
    TT[0] = jnp.zeros((8, D), F32)

    def norm_back(v, d_out, gain, row):
        inv = lax.rsqrt(jnp.mean(v * v, axis=-1, keepdims=True) + EPSILON)
        TT[0, row : row + 1, :] += jnp.sum(d_out * (v * inv), axis=0, keepdims=True)
        d = d_out * gain
        return inv * d - v * (inv * inv * inv * jnp.mean(d * v, axis=-1, keepdims=True))

    def mix_back(i):
        at_i = at(step * i, step)
        d = norm_back(x1[at_i, :], summed(0, at_i), GA[1:2, :], 1)
        d = d + dyQ[at(T * r + step * i, step), :].astype(F32)
        dx1[at_i, :] = d
        daS[at_i, :] = d.astype(BF16)

    loop(T // step, mix_back)
    sendD = [remote(daS.at[:, lanes(QC * q, QC)], daR.at[at(T * r, T)], dev) for dev, q in quad]
    sendT = [remote(dattS.at[:, lanes(QC * q, QC)], dattR.at[at(T * r, T)], dev) for dev, q in quad]

    def out_back(j):
        dattS[:, lanes(wide * j, wide)] = mm(daS[...], WO[at(wide * j, wide), :], NT).astype(BF16)

    loop(D // wide, out_back)
    for copy in sendT:
        go(copy)
    for copy in sendD:
        go(copy)
    dattR[at(T * r, T), :] = dattS[:, lanes(QC * r, QC)]
    daR[at(T * r, T), :] = daS[:, lanes(QC * r, QC)]
    rs_second(1, 3, 1)
    rs_first(0, Z // 2, Z // 2)
    zf_second()
    rs_relay(1)
    rs_second(0, 0, Z // 2)
    out_sum = quad_sum(1, nothing, lambda at_r, j: mm(hid[at_r, :], WC[:, lanes(j, wide)]))
    ag_drain(2)
    ag_drain(3)
    for copy in sendT:
        copy.wait_recv()

    def write_out(i):
        at_i = at(step * i, step)
        R["act"][at_i, :] = (x1[at_i, :] + summed(1, at_i)).astype(BF16)

    HG, BG = R["HG"], R["BG"]
    HG[...] = jnp.zeros(HG.shape, F32)
    BG[...] = jnp.zeros(BG.shape, F32)

    def fold(v):
        return jnp.sum(v.reshape(L // 8, 8, 128), axis=0)

    def prepare_back(raw, d, m, j, cosine, sine, factor):
        if factor != 1.0:
            d = d * factor
        d = d * cosine - swap(d) * sine
        inv = lax.rsqrt(per_head(raw * raw) / 64 + EPSILON)
        HG[m, j] += fold(d * (raw * inv))
        d = d * small[2 + m : 3 + m, :]
        return inv * d - raw * (inv * inv * inv * (per_head(d * raw) / 64))

    def attend_back(q):
        at_q = at(L * q, L)
        _, same = masks(q)
        cosine, sine = CT[at_q, :], ST[at_q, :]
        for j in range(QC // 128):
            tile = slice(128 * j, 128 * (j + 1))
            q2, k2, v2, d2 = qr[at_q, tile], kr[at_q, tile], vb[at_q, tile], dattR[at_q, tile]
            dq, dk, dv = [], [], []
            for h in range(2):
                p = PR[q, 2 * j + h]
                dp = mm(d2 * heads[h], v2, NT)
                ds = (p * (dp - jnp.sum(p * dp, axis=-1, keepdims=True))).astype(BF16)
                wide = ds.astype(F32)
                BG[0, 2 * j + h] += fold(jnp.where(same, 0.0, wide))
                BG[1, 2 * j + h] += fold(jnp.where(same, wide, 0.0))
                dv.append(mm(p.astype(BF16), d2, TN))
                dq.append(mm(ds, k2))
                dk.append(mm(ds, q2, TN))
            d_query = jnp.where(low, dq[0], dq[1])
            d_key = jnp.where(low, dk[0], dk[1])
            d_query = prepare_back(qraw[at_q, tile], d_query, 0, j, cosine, sine, 0.125)
            d_key = prepare_back(kraw[at_q, tile], d_key, 1, j, cosine, sine, 1.0)
            WC[at_q, tile] = d_query.astype(BF16)
            WC[at_q, QC + 128 * j : QC + 128 * (j + 1)] = d_key.astype(BF16)
            WC[at_q, 2 * QC + 128 * j : 2 * QC + 128 * (j + 1)] = jnp.where(low, dv[0], dv[1]).astype(BF16)

    def attend_and_step(i):
        for q in range(S):
            attend_back(S * i + q)
        rs_step(2, i)

    loop(4, attend_and_step)
    for copy in sendD + [near_rest, passed_rest]:
        copy.wait_recv()
    rs_first(3)
    rs_relay(2)
    out_sum()
    loop(T // step, write_out)
    in_sum = quad_sum(
        2, nothing, lambda at_r, j: mm(WC[at_r, 0 : 3 * QC], WA[at(j, wide), 0 : 3 * QC], NT),
        lambda i: rs_second(0, Z // 2 + i, 1),
    )
    rs_relay(0)
    for k in range(len(chunks)):
        if k not in (2, 3):
            ag_drain(k)
    rs_third(1)
    in_sum()

    def input_back(i):
        at_i = at(step * i, step)
        d = norm_back(tok[at_i, :].astype(F32), summed(2, at_i), GA[0:1, :], 0)
        R["ig"][at_i, :] = (dx1[at_i, :] + d).astype(BF16)

    loop(T // step, input_back)

    for m in range(2):
        value = HG[m, 0]
        for j in range(1, QC // 128):
            value = value + HG[m, j]
        TT[0, 2:3, 128 * m : 128 * (m + 1)] = jnp.sum(value, axis=0, keepdims=True)
    for m in range(2):
        line = jnp.zeros((1, 128), F32)
        for h in range(QC // 64):
            line = line + jnp.where(spot == QC // 64 * r + h, jnp.sum(BG[m, h]), 0.0)
        TT[0, 3 + m : 4 + m, 0:128] = line
    t1, t2, t3, t_finish = tile_sum(TT, TR)
    t1()
    rs_second(3, 0, 3)
    t2()
    rs_second(3, 3, 1)
    rs_relay(3)
    rs_third(2)
    rs_last(1)
    t3()
    rs_third(0)
    rs_third(3)
    rs_last(2)
    R["tot"][...] = t_finish()
    rs_last(3)
    for copy in sent:
        copy.wait_send()
    for d in range(1, Z):
        nearby(d, zf_copy(d).wait_send)
    if relays:
        pl.when(outer)(zf_far().wait_send)
    for unit in range(4):
        for i in range(Z):
            if unit != 1:
                y_copy(unit, i).wait_send()
            if i:
                nearby(i, z_copy(unit, i).wait_send)
        if relays:
            pl.when(outer)(x_copy(unit).wait_send)


LAST = ("act", "ig", "gq", "gk", "gv", "go", "gg", "gu", "gd", "ga", "gf", "ghq", "ghk", "gb")


def finishing(s, *refs):
    names = tuple(name + "_in" for name in OUTPUTS) + LAST
    R = dict(zip(names, refs, strict=True))
    D, rows, G, QC, FC, B, HD, H = (s[k] for k in ("D", "rows", "G", "QC", "FC", "B", "HD", "H"))
    HF = FC // 2
    for name in ("act", "ig", "gd"):
        R[name][...] = R[name + "_in"][...]
    parts = R["parts_in"]
    for q in range(4):
        for m, name in enumerate(("gq", "gk", "gv", "go")):
            R[name][:, QC * q : QC * (q + 1)] = parts[2, q, :, QC * m : QC * (m + 1)].astype(F32)
        for j in range(G):
            half, within = divmod(B * j, HF)
            target = slice(B * (4 * j + q), B * (4 * j + q) + B)
            R["gg"][:, target] = parts[half, q, :, within : within + B].astype(F32)
            R["gu"][:, target] = parts[half, q, :, HF + within : HF + within + B].astype(F32)
    tot = R["tot_in"]
    own = lax.axis_index("fsdp") * rows
    mine = pltpu.roll(tot[:, lanes(128 * lax.div(own, 128), 128)], lax.rem(128 - lax.rem(own, 128), 128), 1)
    R["ga"][...] = mine[0:1, 0:rows]
    R["gf"][...] = mine[1:2, 0:rows]
    both = tot[:, 0:256]
    both = both + pltpu.roll(both, 256 - HD, 1)
    R["ghq"][...] = both[2:3, 0:HD]
    R["ghk"][...] = both[2:3, 128 : 128 + HD]
    R["gb"][...] = tot[3:5, 0:H]


def layer(s, tokens, segment_ids, variate_ids, time_ids, w_query, w_key, w_value, w_out, w_gate, w_up, w_down,
          gain_attn, gain_ffn, gain_query, gain_key, variate_bias, cotangent):
    D, T, rows, B, FF, FC, HD, H = (s[k] for k in ("D", "T", "rows", "B", "FF", "FC", "HD", "H"))
    lines = [
        gain_attn[None], gain_ffn[None], jnp.tile(gain_query[None], (1, 2)), jnp.tile(gain_key[None], (1, 2)),
        variate_bias,
    ]
    small, line = jnp.zeros((8, 128), F32), 0
    for piece in lines:
        high, wide = piece.shape
        small = small + jnp.pad(piece.astype(F32), ((line, 8 - line - high), (0, 128 - wide)))
        line += high
    scratch = scratch_of(s)
    names = INPUTS + OUTPUTS + tuple(scratch)
    vmem, anywhere = pl.BlockSpec(memory_space=pltpu.VMEM), pl.BlockSpec(memory_space=pl.ANY)
    here = {"seg", "var", "tim", "small"}

    def shape(*dims, kind=F32):
        return jax.ShapeDtypeStruct(dims, kind)

    tokens_shape = shape(T, D, kind=BF16)
    outs = pl.pallas_call(
        functools.partial(fused, s, names),
        out_shape=[tokens_shape, tokens_shape, shape(B, D), shape(3, 4, rows, FC, kind=BF16), shape(8, D)],
        in_specs=[vmem if name in here else anywhere for name in INPUTS],
        out_specs=[vmem] * len(OUTPUTS),
        scratch_shapes=list(scratch.values()),
        compiler_params=pltpu.CompilerParams(
            collective_id=0, has_side_effects=True, vmem_limit_bytes=64 << 20
        ),
        name="fused_layer",
    )(
        tokens.reshape(T, D), cotangent.reshape(T, D), segment_ids, variate_ids, time_ids,
        w_query, w_key, w_value, w_out, w_gate, w_up, w_down, small,
    )
    last = pl.pallas_call(
        functools.partial(finishing, s),
        out_shape=[tokens_shape, tokens_shape] + [shape(rows, D)] * 4 + [shape(rows, FF)] * 2
        + [shape(B, D), shape(1, rows), shape(1, rows), shape(1, HD), shape(1, HD), shape(2, H)],
        in_specs=[vmem] * len(OUTPUTS),
        out_specs=[vmem] * len(LAST),
        name="finishing",
    )(*outs)
    flat = [value.reshape(-1) for value in last[9:13]]
    return (last[0].reshape(tokens.shape), last[1].reshape(tokens.shape), *last[2:9], *flat, last[13])


def local(tokens, segment_ids, variate_ids, time_ids, *rest):
    s = sizes_of(lax.axis_size("fsdp"), tokens, rest[0], rest[4], rest[9], rest[11])
    chosen = functools.partial(layer, s) if fits(s) else plain
    return chosen(tokens, segment_ids, variate_ids, time_ids, *rest)


def solution(mesh):
    placed = (
        P("fsdp", None, None),
        P("fsdp", None),
        P("fsdp", None),
        P("fsdp", None),
        P("fsdp", None),
        P("fsdp", None),
        P("fsdp", None),
        P("fsdp", None),
        P("fsdp", None),
        P("fsdp", None),
        P("fsdp", None),
        P("fsdp"),
        P("fsdp"),
        P(),
        P(),
        P(),
        P("fsdp", None, None),
    )
    return jax.shard_map(
        local,
        mesh=mesh,
        in_specs=placed,
        out_specs=(
            P("fsdp", None, None),
            P("fsdp", None, None),
            P("fsdp", None),
            P("fsdp", None),
            P("fsdp", None),
            P("fsdp", None),
            P("fsdp", None),
            P("fsdp", None),
            P("fsdp", None),
            P("fsdp"),
            P("fsdp"),
            P(),
            P(),
            P(),
        ),
        check_vma=False,
    )
```

```python
import functools
import math

import jax
import jax.numpy as jnp
from jax import lax
from jax.experimental import pallas as pl
from jax.experimental.pallas import tpu as pltpu
from jax.sharding import PartitionSpec as P

EPSILON = 1e-05


def normalize(values, scale_gain):
    return (
        values * lax.rsqrt(jnp.mean(values * values, axis=-1, keepdims=True) + EPSILON) * scale_gain
    )


def rotate(values, moments):
    halfway = values.shape[-1] // 2
    frequency = jnp.exp(-math.log(10000.0) * jnp.arange(halfway).astype(jnp.float32) / halfway)
    angles = moments.astype(jnp.float32)[:, None] * frequency[None, :]
    cosine = jnp.cos(angles)[:, None, :]
    sine_part = jnp.sin(angles)[:, None, :]
    former = values[..., :halfway]
    latter = values[..., halfway:]
    return jnp.concatenate(
        [former * cosine - latter * sine_part, former * sine_part + latter * cosine], axis=-1
    )


def prepare(raw_heads, head_gain, moments, factor):
    return rotate(normalize(raw_heads, head_gain), moments) * factor


def swiglu(gate_act, up_act):
    return jax.nn.silu(gate_act) * up_act


def attention_masks(segments, variates):
    length = segments.shape[0]
    diagonal = jnp.arange(length)[:, None] == jnp.arange(length)[None, :]
    allowed = (segments[:, None] == segments[None, :]) & ((segments[None, :] != 0) | diagonal)
    same_var = variates[:, None] == variates[None, :]
    return (allowed, same_var)


def scoring(q_rot, k_rot, bias_table, allowed, same_var):
    scores = jnp.einsum("qhe,khe->hqk", q_rot, k_rot, preferred_element_type=jnp.float32)
    scores = scores + jnp.where(
        same_var[None], bias_table[1][:, None, None], bias_table[0][:, None, None]
    )
    return jnp.where(allowed[None], scores, -1000000000.0)


def project(left, right):
    return jnp.dot(left, right, preferred_element_type=jnp.float32)


def across(left, right):
    return lax.dot_general(
        left, right, (((0,), (0,)), ((), ())), preferred_element_type=jnp.float32
    )


def against(left, weight):
    return lax.dot_general(
        left, weight, (((1,), (1,)), ((), ())), preferred_element_type=jnp.float32
    )


def forward(inputs_low, weights, side_params, segments, variates, moments):
    w_query, w_key, w_value, w_out, w_gate, w_up, w_down, gain_attn, gain_ffn = weights
    gain_query, gain_key, bias_table = side_params
    length, model_width = inputs_low.shape
    head_count = bias_table.shape[1]
    head_dim = gain_query.shape[0]
    inputs = inputs_low.astype(jnp.float32)
    normed = normalize(inputs, gain_attn.astype(jnp.float32)).astype(jnp.bfloat16)
    queries = project(normed, w_query).reshape(length, head_count, head_dim)
    key_raw = project(normed, w_key).reshape(length, head_count, head_dim)
    v_low = project(normed, w_value).reshape(length, head_count, head_dim).astype(jnp.bfloat16)
    q_rot = prepare(queries, gain_query, moments, head_dim ** (-0.5)).astype(jnp.bfloat16)
    k_rot = prepare(key_raw, gain_key, moments, 1.0).astype(jnp.bfloat16)
    allowed, same_var = attention_masks(segments, variates)
    scores = scoring(q_rot, k_rot, bias_table, allowed, same_var)
    maximum = jnp.max(scores, axis=-1, keepdims=True)
    exponent = jnp.exp(scores - maximum)
    row_total = jnp.sum(exponent, axis=-1, keepdims=True)
    log_total = maximum + jnp.log(row_total)
    softmax_probs = (exponent / row_total).astype(jnp.bfloat16)
    attended = jnp.einsum("hqk,khe->qhe", softmax_probs, v_low, preferred_element_type=jnp.float32)
    attended = attended.reshape(length, model_width).astype(jnp.bfloat16)
    mixed_state = inputs + project(attended, w_out)
    normed_ffn = normalize(mixed_state, gain_ffn.astype(jnp.float32)).astype(jnp.bfloat16)
    gate_act = project(normed_ffn, w_gate)
    up_act = project(normed_ffn, w_up)
    hidden = swiglu(gate_act, up_act).astype(jnp.bfloat16)
    result = mixed_state + project(hidden, w_down)
    kept_state = (
        inputs,
        normed,
        queries,
        key_raw,
        q_rot,
        k_rot,
        v_low,
        log_total,
        attended,
        mixed_state,
        normed_ffn,
        gate_act,
        up_act,
        hidden,
    )
    return (result, kept_state)


def backward(upstream, kept_state, weights, side_params, segments, variates, moments):
    (
        inputs,
        normed,
        queries,
        key_raw,
        q_rot,
        k_rot,
        v_low,
        log_total,
        attended,
        mixed_state,
        normed_ffn,
        gate_act,
        up_act,
        hidden,
    ) = kept_state
    w_query, w_key, w_value, w_out, w_gate, w_up, w_down, gain_attn, gain_ffn = weights
    gain_query, gain_key, bias_table = side_params
    length, head_count, head_dim = queries.shape
    grad_down = across(hidden, upstream)
    d_hidden = against(upstream, w_down)
    _, pullback = jax.vjp(swiglu, gate_act, up_act)
    d_gate, d_up = pullback(d_hidden)
    d_gate = d_gate.astype(jnp.bfloat16)
    d_up = d_up.astype(jnp.bfloat16)
    grad_gate = across(normed_ffn, d_gate)
    grad_up = across(normed_ffn, d_up)
    d_normed_ffn = against(d_gate, w_gate) + against(d_up, w_up)
    _, pullback = jax.vjp(normalize, mixed_state, gain_ffn.astype(jnp.float32))
    d_mixed, grad_gain_ffn = pullback(d_normed_ffn)
    d_mixed = d_mixed + upstream.astype(jnp.float32)
    d_branch = d_mixed.astype(jnp.bfloat16)
    grad_out = across(attended, d_branch)
    d_attended = against(d_branch, w_out).astype(jnp.bfloat16).reshape(length, head_count, head_dim)
    allowed, same_var = attention_masks(segments, variates)
    scores = scoring(q_rot, k_rot, bias_table, allowed, same_var)
    softmax_probs = jnp.exp(scores - log_total)
    d_probs = jnp.einsum("qhe,khe->hqk", d_attended, v_low, preferred_element_type=jnp.float32)
    d_values = jnp.einsum(
        "hqk,qhe->khe",
        softmax_probs.astype(jnp.bfloat16),
        d_attended,
        preferred_element_type=jnp.float32,
    )
    d_values = d_values.reshape(length, head_count * head_dim).astype(jnp.bfloat16)
    weighted = jnp.sum(softmax_probs * d_probs, axis=-1, keepdims=True)
    d_scores = (softmax_probs * (d_probs - weighted)).astype(jnp.bfloat16)
    d_float = d_scores.astype(jnp.float32)
    same_sum = jnp.sum(jnp.where(same_var[None], d_float, 0.0), axis=(1, 2))
    other_sum = jnp.sum(jnp.where(same_var[None], 0.0, d_float), axis=(1, 2))
    grad_bias = jnp.stack([other_sum, same_sum])
    d_qrot = jnp.einsum("hqk,khe->qhe", d_scores, k_rot, preferred_element_type=jnp.float32)
    d_krot = jnp.einsum("hqk,qhe->khe", d_scores, q_rot, preferred_element_type=jnp.float32)
    factor = head_dim ** (-0.5)
    _, pullback = jax.vjp(
        lambda raw_heads, head_gain: prepare(raw_heads, head_gain, moments, factor),
        queries,
        gain_query,
    )
    d_queries, grad_gain_query = pullback(d_qrot)
    _, pullback = jax.vjp(
        lambda raw_heads, head_gain: prepare(raw_heads, head_gain, moments, 1.0), key_raw, gain_key
    )
    d_keys, grad_gain_key = pullback(d_krot)
    d_queries = d_queries.reshape(length, head_count * head_dim).astype(jnp.bfloat16)
    d_keys = d_keys.reshape(length, head_count * head_dim).astype(jnp.bfloat16)
    grad_query = across(normed, d_queries)
    grad_key = across(normed, d_keys)
    grad_value = across(normed, d_values)
    d_normed = against(d_queries, w_query) + against(d_keys, w_key) + against(d_values, w_value)
    _, pullback = jax.vjp(normalize, inputs, gain_attn.astype(jnp.float32))
    d_inputs, grad_gain_attn = pullback(d_normed)
    row_grads = jnp.concatenate(
        [grad_query, grad_key, grad_value, grad_out, grad_gate, grad_up], axis=1
    )
    small = (grad_gain_query, grad_gain_key, grad_bias, grad_gain_attn, grad_gain_ffn)
    return (d_inputs + d_mixed, row_grads, grad_down, small)


def plain(
    tokens,
    segment_ids,
    variate_ids,
    time_ids,
    w_query,
    w_key,
    w_value,
    w_out,
    w_gate,
    w_up,
    w_down,
    gain_attn,
    gain_ffn,
    gain_query,
    gain_key,
    variate_bias,
    cotangent,
):
    devices = lax.axis_size("fsdp")
    owner = lax.axis_index("fsdp")
    width = w_query.shape[1]
    hidden_width = w_gate.shape[1]
    own_rows = w_query.shape[0]
    own_down = w_down.shape[0]
    side_params = (
        gain_query.astype(jnp.float32),
        gain_key.astype(jnp.float32),
        variate_bias.astype(jnp.float32),
    )
    rows_total = jnp.zeros((own_rows * devices, 4 * width + 2 * hidden_width), jnp.float32)
    down_total = jnp.zeros((own_down * devices, width), jnp.float32)
    side_totals = (
        jnp.zeros(gain_query.shape, jnp.float32),
        jnp.zeros(gain_key.shape, jnp.float32),
        jnp.zeros(variate_bias.shape, jnp.float32),
        jnp.zeros((own_rows * devices,), jnp.float32),
        jnp.zeros((own_rows * devices,), jnp.float32),
    )
    results = []
    input_grads = []
    for micro_index in range(tokens.shape[0]):
        segments = segment_ids[micro_index]
        variates = variate_ids[micro_index]
        moments = time_ids[micro_index]
        forward_weights = (
            lax.all_gather(w_query, "fsdp", axis=0, tiled=True),
            lax.all_gather(w_key, "fsdp", axis=0, tiled=True),
            lax.all_gather(w_value, "fsdp", axis=0, tiled=True),
            lax.all_gather(w_out, "fsdp", axis=0, tiled=True),
            lax.all_gather(w_gate, "fsdp", axis=0, tiled=True),
            lax.all_gather(w_up, "fsdp", axis=0, tiled=True),
            lax.all_gather(w_down, "fsdp", axis=0, tiled=True),
            lax.all_gather(gain_attn, "fsdp", axis=0, tiled=True),
            lax.all_gather(gain_ffn, "fsdp", axis=0, tiled=True),
        )
        result, kept_state = forward(
            tokens[micro_index], forward_weights, side_params, segments, variates, moments
        )
        results.append(result.astype(jnp.bfloat16))
        backward_weights = (
            lax.all_gather(w_query, "fsdp", axis=0, tiled=True),
            lax.all_gather(w_key, "fsdp", axis=0, tiled=True),
            lax.all_gather(w_value, "fsdp", axis=0, tiled=True),
            lax.all_gather(w_out, "fsdp", axis=0, tiled=True),
            lax.all_gather(w_gate, "fsdp", axis=0, tiled=True),
            lax.all_gather(w_up, "fsdp", axis=0, tiled=True),
            lax.all_gather(w_down, "fsdp", axis=0, tiled=True),
            lax.all_gather(gain_attn, "fsdp", axis=0, tiled=True),
            lax.all_gather(gain_ffn, "fsdp", axis=0, tiled=True),
        )
        d_inputs, row_grads, down_grads, small = backward(
            cotangent[micro_index],
            kept_state,
            backward_weights,
            side_params,
            segments,
            variates,
            moments,
        )
        input_grads.append(d_inputs.astype(jnp.bfloat16))
        rows_total = rows_total + row_grads
        down_total = down_total + down_grads
        side_totals = tuple((running + fresh for running, fresh in zip(side_totals, small)))
    owned_rows = lax.psum_scatter(rows_total, "fsdp", scatter_dimension=0, tiled=True)
    owned_down = lax.psum_scatter(down_total, "fsdp", scatter_dimension=0, tiled=True)
    shared = lax.psum(
        (side_totals[0], side_totals[1], side_totals[2], side_totals[3], side_totals[4]), "fsdp"
    )
    gain_attn_own = lax.dynamic_slice_in_dim(shared[3], owner * own_rows, own_rows, 0)
    gain_ffn_own = lax.dynamic_slice_in_dim(shared[4], owner * own_rows, own_rows, 0)
    grad_query = owned_rows[:, 0:width]
    grad_key = owned_rows[:, width : 2 * width]
    grad_value = owned_rows[:, 2 * width : 3 * width]
    grad_out = owned_rows[:, 3 * width : 4 * width]
    grad_gate = owned_rows[:, 4 * width : 4 * width + hidden_width]
    grad_up = owned_rows[:, 4 * width + hidden_width :]
    return (
        jnp.stack(results),
        jnp.stack(input_grads),
        grad_query,
        grad_key,
        grad_value,
        grad_out,
        grad_gate,
        grad_up,
        owned_down,
        gain_attn_own,
        gain_ffn_own,
        shared[0],
        shared[1],
        shared[2],
    )


F32 = jnp.float32
BF16 = jnp.bfloat16
MESH = pl.DeviceIdType.MESH
NT = (((1,), (1,)), ((), ()))
TN = (((0,), (0,)), ((), ()))


def mm(left, right, dims=(((1,), (0,)), ((), ()))):
    return lax.dot_general(left, right, dims, preferred_element_type=F32)


def at(start, size):
    return pl.ds(pl.multiple_of(start, size), size)


def lanes(start, size):
    return pl.ds(pl.multiple_of(start, 128), size)


def loop(count, body):
    lax.fori_loop(0, count, lambda i, carry: (body(i), carry)[1], 0)


def sizes_of(devices, tokens, w_query, w_gate, gain_query, bias):
    seqs, length, width = tokens.shape
    own_rows, hidden = w_query.shape[0], w_gate.shape[1]
    return dict(
        n=devices, S=seqs, L=length, D=width, FF=hidden, rows=own_rows, T=seqs * length,
        G=devices // 4, Z=devices // 8, QC=width // 4, FC=hidden // 4, B=4 * own_rows,
        HD=gain_query.shape[0], H=bias.shape[1],
    )


def fits(s):
    return (
        s["n"] % 8 == 0 and s["rows"] % 16 == 0 and s["L"] == 128 and s["HD"] == 64
        and s["H"] * s["HD"] == s["D"] and s["QC"] % 128 == 0 and s["FF"] == 4 * s["D"]
        and s["B"] == 128 and s["FC"] // 2 % s["B"] == 0 and s["FC"] == s["D"]
    )


def scratch_of(s):
    n, S, L, D, rows, T, G, Z, QC, FC, B = (
        s[k] for k in ("n", "S", "L", "D", "rows", "T", "G", "Z", "QC", "FC", "B")
    )
    Q = 4 * T
    vm = pltpu.VMEM
    return dict(
        WA=vm((D, 4 * QC), BF16), WB=vm((D, 2 * FC), BF16), WC=vm((FC, D), BF16), WO=vm((D, D), BF16),
        SA=vm((4, rows, 4 * QC), BF16), SB=vm((4, rows, 2 * FC), BF16),
        h1Q=vm((Q, D), BF16), dyQ=vm((Q, D), BF16), attQ=vm((Q, D), BF16), h2Q=vm((Q, D), BF16),
        qraw=vm((Q, QC), F32), kraw=vm((Q, QC), F32),
        qr=vm((Q, QC), BF16), kr=vm((Q, QC), BF16), vb=vm((Q, QC), BF16),
        PR=vm((4 * S, QC // 64, L, L), F32), CT=vm((Q, 128), F32), ST=vm((Q, 128), F32),
        x1=vm((T, D), F32), dx1=vm((T, D), F32), acc=vm((T, D), F32),
        hid=vm((Q, FC), BF16), dgdu=vm((Q, 2 * FC), BF16),
        rsS=vm((3, T, D), BF16), rsR=vm((3, 3, T, D), BF16),
        daS=vm((T, D), BF16), daR=vm((Q, QC), BF16), dattS=vm((T, D), BF16), dattR=vm((Q, QC), BF16),
        YS=vm((3, Z, B, FC), BF16), YR=vm((4, Z, B, FC), BF16), ZR=vm((4, Z - 1, B, FC), BF16), ZX=vm((4, B, FC), BF16),
        FS=vm((Z, 2, B, FC // 2), BF16), FR=vm((Z - 1, 2, B, FC // 2), BF16), FX=vm((2, B, FC // 2), BF16),
        FT=vm((2, B, FC // 2), BF16), FK=vm((B, FC // 2), F32),
        QS=vm((3, B, FC), BF16), QR=vm((3, 4, rows, FC), BF16),
        idq=vm((4 * S, 8, L), F32),
        SW=vm((4, rows, D), BF16), SG=vm((2, rows, s["FF"]), BF16), TK=vm((T, D), BF16),
        GQ=vm((4, 8, B), F32), GA=vm((8, D), F32), load=pltpu.SemaphoreType.DMA((9,)),
        TT=vm((3, 8, D), F32), TR=vm((4 + Z, 8, D), F32),
        HG=vm((4, QC // 128, 8, 128), F32), BG=vm((2, QC // 64, 8, 128), F32),
        send=pltpu.SemaphoreType.DMA((192,)), recv=pltpu.SemaphoreType.DMA((192,)),
    )


INPUTS = (
    "tok", "cot", "seg", "var", "tim", "wq", "wk", "wv", "wo", "wg", "wu", "wd", "small",
)
OUTPUTS = ("act", "ig", "gd", "parts", "tot")


def fused(s, names, *refs):
    R = dict(zip(names, refs, strict=True))
    n, S, L, D, rows, T, G, Z, QC, FC, B = (
        s[k] for k in ("n", "S", "L", "D", "rows", "T", "G", "Z", "QC", "FC", "B")
    )
    HF = FC // 2
    Q = 4 * T
    me = lax.axis_index("fsdp")
    r, c, xx, g = lax.rem(me, 4), lax.rem(me, 2), lax.rem(lax.div(me, 2), 2), lax.div(me, 4)
    y, z = lax.rem(g, 2), lax.div(g, 2)
    r_sib, r_par = r + 1 - 2 * c, r + 2 - 4 * xx
    r_dia = r_sib + 2 - 4 * xx
    sib, par, dia = me - r + r_sib, me - r + r_par, me - r + r_dia
    peer = me + 4 - 8 * y
    quad = ((sib, r_sib), (par, r_par), (dia, r_dia))

    def at_z(step):
        return lax.rem(z + step, Z)

    def z_dev(step):
        return at_z(step) * 8 + y * 4 + r

    def z_src(step):
        return lax.rem(z + Z - step, Z)

    relays = Z == 4
    inner, outer = lax.rem(z + 1, 4) >= 2, lax.rem(z + 1, 4) < 2

    def nearby(step, action):
        if relays and step != 2:
            pl.when(z != (Z - 1 if step == 1 else 0))(action)
        else:
            action()

    used = [0]
    sent = []

    def take(count=1):
        used[0] += count
        return used[0] - count

    def remote(src, dst, device, sem=None, arrival=None):
        sem = take() if sem is None else sem
        arrival = sem if arrival is None else arrival
        return pltpu.make_async_remote_copy(
            src_ref=src, dst_ref=dst, send_sem=R["send"].at[sem], recv_sem=R["recv"].at[arrival],
            device_id=(device,), device_id_type=MESH,
        )

    def go(copy):
        copy.start()
        sent.append(copy)
        return copy

    barrier = pltpu.get_barrier_semaphore()
    others = [sib, par, dia, peer] + [z_dev(d) for d in range(1, Z)]
    for device in others:
        pl.semaphore_signal(barrier, inc=1, device_id=(device,), device_id_type=MESH)

    SA, SB, SW, SG, WA, WB, WC, WO = (R[k] for k in ("SA", "SB", "SW", "SG", "WA", "WB", "WC", "WO"))
    dyQ, h1Q, h2Q, attQ, tok = R["dyQ"], R["h1Q"], R["h2Q"], R["attQ"], R["TK"]
    places = [("wq", SW.at[0]), ("wk", SW.at[1]), ("wv", SW.at[2]), ("wo", SW.at[3]), ("wd", WC.at[at(B * g, B)])]
    places += [("tok", tok), ("wg", SG.at[0]), ("wu", SG.at[1]), ("cot", dyQ.at[at(T * r, T)])]
    loads = {}
    for i, (name, place) in enumerate(places):
        loads[name] = pltpu.make_async_copy(R[name], place, R["load"].at[i])
        loads[name].start()
    own = at(B * g + rows * r, rows)
    idq, small, GQ, GA = R["idq"], R["small"], R["GQ"], R["GA"]
    for q in range(S):
        idq[S * r + q, 0:1, :] = R["seg"][q : q + 1, :].astype(F32)
        idq[S * r + q, 1:2, :] = R["var"][q : q + 1, :].astype(F32)
        idq[S * r + q, 2:3, :] = R["tim"][q : q + 1, :].astype(F32)
        idq[S * r + q, 3:8, :] = jnp.zeros((5, L), F32)
    GQ[r] = pltpu.roll(small[...], rows * r, 1)
    for m, name in enumerate(("wq", "wk", "wv", "wo")):
        loads[name].wait()
        for q in range(4):
            SA[q, :, QC * m : QC * (m + 1)] = SW[m, :, QC * q : QC * (q + 1)]
    WA[own, :] = SA[r]
    pl.semaphore_wait(barrier, len(others))

    def tile_sum(tile, got):
        first = [remote(tile.at[0], got.at[i], dev) for i, (dev, _) in enumerate(quad)]
        second = [remote(tile.at[1], got.at[4 + z], z_dev(d)) for d in range(1, Z)]
        third = remote(tile.at[2], got.at[3], peer)

        def round1():
            for copy in first:
                go(copy)

        def round2():
            for copy in first:
                copy.wait_recv()
            value = (tile[0] + got[0]) + (got[1] + got[2])
            tile[1] = value
            got[4 + z] = value
            for copy in second:
                go(copy)

        def round3():
            for copy in second:
                copy.wait_recv()
            value = got[4]
            for i in range(1, Z):
                value = value + got[4 + i]
            tile[2] = value
            go(third)

        def finish():
            third.wait_recv()
            return tile[2] + got[3]

        return round1, round2, round3, finish

    def quad_gather(block):
        to_sib, to_par = remote(block(r), block(r), sib), remote(block(r), block(r), par)
        passed = remote(block(r_par), block(r_par), sib)

        def start():
            go(to_par)
            go(to_sib)

        def forward():
            to_par.wait_recv()
            go(passed)

        def finish():
            to_sib.wait_recv()
            passed.wait_recv()

        return start, forward, finish

    chunks = [(WA, 0, 2 * QC), (WA, 2 * QC, 2 * QC), (WC, 0, D // 2), (WC, D // 2, D // 2)]
    chunks += [(WB, HF * k, HF) for k in range(4)] + [(GA, 0, B)]
    early, after = 7, {1: 4, 2: 5, 3: 6}

    def piece(k, group):
        ref, start, size = chunks[k]
        if ref is GA:
            return ref.at[:, lanes(B * group, B)]
        return ref.at[at(B * group, B), pl.ds(start, size)]

    a_sem, f_sem, o_sem = ([take(size) for _ in chunks] for size in (Z - 1, 1, Z))
    b_sem, e_sem = take(Z - 1), take()

    def across_y(other):
        return y + other * (1 - 2 * y)

    def along(k, d, other=0):
        block = piece(k, 2 * z + across_y(other))
        return remote(block, block, z_dev(d), (b_sem if other else a_sem[k]) + d - 1)

    def over(k, d):
        block = piece(k, 2 * z_src(d) + y)
        return remote(block, block, peer, o_sem[k] + d)

    def relay(k, other=0):
        block, end = piece(k, 2 * z_src(2) + across_y(other)), lax.div(z, 2)
        sems = (e_sem, b_sem + 2 * end) if other else (f_sem[k], a_sem[k] + 2 * end)
        return remote(block, block, 3 * end * 8 + y * 4 + r, *sems)

    def near(k, d, action):
        if k == 8:
            action()
        else:
            nearby(d, action)

    def both(k):
        return (0, 1) if k == early else (0,)

    def ag_start(k):
        for other in both(k):
            for d in range(1, Z):
                near(k, d, along(k, d, other).start)

    def ag_own(k):
        over(k, 0).start()

    def ag_forward(k):
        first = lax.div(3 - z, 3)
        for i in range(1, Z):
            d = i if not relays or i == 2 else 1 + 2 * first if i == 1 else 3 - 2 * first
            for other in both(k):
                along(k, d, other).wait_recv()
                if relays and i == 2 and k < 8:
                    pl.when(inner)(relay(k, other).start)
            if k != early:
                over(k, d).start()
        if k in after:
            ag_own(after[k])
        if 2 <= k <= 4:
            ag_start(k + 3)

    def ag_finish(k):
        for d in range(Z):
            if k != early:
                over(k, d).wait_recv()

    def ag_drain(k):
        for d in range(1 if k == early else Z):
            over(k, d).wait_send()
        for other in both(k):
            for d in range(1, Z):
                near(k, d, along(k, d, other).wait_send)
            if relays and k < 8:
                pl.when(inner)(relay(k, other).wait_send)

    sendG = [remote(GQ.at[r], GQ.at[r], dev) for dev, q in quad]
    sendA = [remote(SA.at[q], WA.at[own], dev) for dev, q in quad]
    sendB = [remote(SB.at[q], WB.at[own], dev) for dev, q in quad]
    mine = idq.at[pl.ds(S * r, S)]
    sendI = [remote(mine, mine, dev) for dev, q in quad]
    for copy in sendG + sendA + sendI:
        go(copy)
    loads["wd"].wait()
    ag_own(2)
    ag_own(3)
    ag_start(2)
    for copy in sendG:
        copy.wait_recv()
    GA[:, lanes(B * g, B)] = (GQ[0] + GQ[1]) + (GQ[2] + GQ[3])
    ag_start(8)
    ag_own(8)
    for copy in sendA:
        copy.wait_recv()
    ag_start(0)
    ag_own(0)
    ag_start(1)
    ag_own(1)
    for name in ("wg", "wu"):
        loads[name].wait()
    for q in range(4):
        for j in range(G):
            half, within = divmod(B * j, HF)
            source = slice(B * (4 * j + q), B * (4 * j + q) + B)
            SB[q, :, half * FC + within : half * FC + within + B] = SG[0, :, source]
            SB[q, :, half * FC + HF + within : half * FC + HF + within + B] = SG[1, :, source]
    WB[own, :] = SB[r]
    for copy in sendB:
        go(copy)
    for copy in sendI:
        copy.wait_recv()

    lane = lax.broadcasted_iota(jnp.int32, (L, 128), 1)
    sub = lax.broadcasted_iota(jnp.int32, (L, 128), 0)
    front = lax.rem(lane, 64) < 32
    low = lane < 64
    freq = jnp.exp(-math.log(10000.0) * lax.rem(lane, 32).astype(F32) / 32)
    CT, ST = R["CT"], R["ST"]

    def tables(q):
        times = jnp.broadcast_to(idq[q, 2:3, :], (L, L)).T
        angles = times * freq
        CT[at(L * q, L), :] = jnp.cos(angles)
        sine = jnp.sin(angles)
        ST[at(L * q, L), :] = jnp.where(front, -sine, sine)

    loop(2 * S, tables)
    ag_forward(8)
    loop(2 * S, lambda q: tables(2 * S + q))
    loads["tok"].wait()
    ag_finish(8)
    step = 64

    def norm_in(i):
        x = tok[at(step * i, step), :].astype(F32)
        inv = lax.rsqrt(jnp.mean(x * x, axis=-1, keepdims=True) + EPSILON)
        h1Q[at(T * r + step * i, step), :] = (x * inv * GA[0:1, :]).astype(BF16)

    loop(T // step, norm_in)

    def token_block(ref):
        return lambda role: ref.at[at(T * role, T)]

    h1_start, h1_forward, h1_finish = quad_gather(token_block(h1Q))
    dy_start, dy_forward, dy_finish = quad_gather(token_block(dyQ))

    def att_block(chip, role):
        return attQ.at[at(2 * T * chip, 2 * T), lanes(QC * role, QC)]

    def att_copy(chip, role, device):
        return remote(att_block(chip, role), att_block(chip, role), device)

    needed, passed = att_copy(1 - xx, r, par), att_copy(xx, r_par, sib)
    near_needed, near_rest = att_copy(xx, r, sib), att_copy(1 - xx, r, sib)
    rest, passed_rest = att_copy(xx, r, par), att_copy(1 - xx, r_par, sib)
    wo_start, wo_forward, wo_finish = quad_gather(lambda role: WO.at[:, lanes(QC * role, QC)])
    h2_start, h2_forward, h2_finish = quad_gather(token_block(h2Q))
    h1_start()
    for copy in sendB:
        copy.wait_recv()
    ag_own(early)
    ag_forward(0)
    ag_start(3)
    h1_forward()
    ag_forward(1)
    ag_start(4)
    loads["cot"].wait()
    dy_start()
    h1_finish()
    ag_finish(0)
    ag_finish(1)
    ag_forward(2)

    qraw, kraw, qr, kr, vb, PR = (R[k] for k in ("qraw", "kraw", "qr", "kr", "vb", "PR"))
    spot = lax.broadcasted_iota(jnp.int32, (1, 128), 1)
    bias = [
        [jnp.sum(jnp.where(spot == QC // 64 * r + h, small[4 + m : 5 + m, :], 0.0)) for h in range(QC // 64)]
        for m in range(2)
    ]

    def swap(v):
        return jnp.where(front, pltpu.roll(v, 96, 1), pltpu.roll(v, 32, 1))

    def per_head(v):
        first = jnp.sum(jnp.where(low, v, 0.0), axis=-1, keepdims=True)
        second = jnp.sum(jnp.where(low, 0.0, v), axis=-1, keepdims=True)
        return jnp.where(low, first, second)

    def project_heads(q):
        at_q = at(L * q, L)
        value = mm(h1Q[at_q, :], WA[:, 0 : 3 * QC])
        cosine, sine = CT[at_q, :], ST[at_q, :]
        for m, (raw, ready) in enumerate(((qraw, qr), (kraw, kr))):
            raw[at_q, :] = value[:, QC * m : QC * (m + 1)]
            for j in range(QC // 128):
                v = value[:, QC * m + 128 * j : QC * m + 128 * (j + 1)]
                inv = lax.rsqrt(per_head(v * v) / 64 + EPSILON)
                v = v * inv * small[2 + m : 3 + m, :]
                v = v * cosine + swap(v) * sine
                if m == 0:
                    v = v * 0.125
                ready[at_q, 128 * j : 128 * (j + 1)] = v.astype(BF16)
        vb[at_q, :] = value[:, 2 * QC : 3 * QC].astype(BF16)

    loop(4 * S, project_heads)
    WO[:, lanes(QC * r, QC)] = WA[:, 3 * QC : 4 * QC]
    wo_start()
    dy_forward()

    def masks(q):
        segment = jnp.broadcast_to(idq[q, 0:1, :], (L, L))
        variate = jnp.broadcast_to(idq[q, 1:2, :], (L, L))
        allowed = (segment == segment.T) & ((segment != 0.0) | (lane == sub))
        return allowed, variate == variate.T

    heads = [jnp.where(low, 1.0, 0.0).astype(BF16), jnp.where(low, 0.0, 1.0).astype(BF16)]

    def attend(q):
        at_q = at(L * q, L)
        allowed, same = masks(q)
        for j in range(QC // 128):
            tile = slice(128 * j, 128 * (j + 1))
            q2, k2, v2 = qr[at_q, tile], kr[at_q, tile], vb[at_q, tile]
            outs = []
            for h in range(2):
                head = 2 * j + h
                score = mm(q2 * heads[h], k2, NT) + jnp.where(same, bias[1][head], bias[0][head])
                score = jnp.where(allowed, score, -1000000000.0)
                e = jnp.exp(score - jnp.max(score, axis=-1, keepdims=True))
                p = e / jnp.sum(e, axis=-1, keepdims=True)
                PR[q, head] = p
                outs.append(mm(p.astype(BF16), v2))
            attQ[at_q, lanes(QC * r + 128 * j, 128)] = jnp.where(low, outs[0], outs[1]).astype(BF16)

    def attend_pair(q):
        attend(q)
        attend(q + 1)

    loop(S, lambda i: attend_pair(2 * S * (1 - xx) + 2 * i))
    go(needed)
    ag_forward(3)
    loop(S, lambda i: attend_pair(2 * S * xx + 2 * i))
    go(near_needed)
    go(near_rest)
    ZR, FR = R["ZR"], R["FR"]
    if relays:
        for k, end in ((0, 0), (2, 3)):

            @pl.when(z == end)
            def _():
                FR[k] = jnp.zeros((2, B, HF), BF16)
                for unit in range(4):
                    ZR[unit, k] = jnp.zeros((B, FC), BF16)

    needed.wait_recv()
    go(passed)
    wo_forward()
    over(early, 0).wait_recv()
    ag_forward(4)
    wo_finish()
    near_needed.wait_recv()
    passed.wait_recv()

    x1, dx1, acc = R["x1"], R["dx1"], R["acc"]

    wide = 256

    def mix_sum(j):
        cols = lanes(wide * j, wide)
        x1[:, cols] = tok[:, cols].astype(F32) + mm(attQ[at(T * r, T), :], WO[:, cols])

    loop(D // wide, mix_sum)

    def mix(i):
        x = x1[at(step * i, step), :]
        inv = lax.rsqrt(jnp.mean(x * x, axis=-1, keepdims=True) + EPSILON)
        h2Q[at(T * r + step * i, step), :] = (x * inv * GA[1:2, :]).astype(BF16)

    loop(T // step, mix)
    h2_start()
    go(rest)
    ag_forward(5)
    dy_finish()
    ag_forward(6)
    ag_finish(2)
    ag_finish(3)
    h2_forward()
    ag_finish(4)
    ag_finish(5)

    hid, dgdu = R["hid"], R["dgdu"]

    def ffn(half, role):
        at_r = at(T * role, T)

        def body(j):
            to_gate = lanes(half * FC + wide * j, wide)
            to_up = lanes(half * FC + HF + wide * j, wide)
            gate, up = mm(h2Q[at_r, :], WB[:, to_gate]), mm(h2Q[at_r, :], WB[:, to_up])
            sigma = 1.0 / (1.0 + jnp.exp(-gate))
            silu = gate * sigma
            hid[at_r, lanes(half * HF + wide * j, wide)] = (silu * up).astype(BF16)
            d_hidden = mm(dyQ[at_r, :], WC[at(half * HF + wide * j, wide), :], NT)
            d_gate = d_hidden * up * (sigma * (1.0 + gate * (1.0 - sigma)))
            dgdu[at_r, to_gate] = d_gate.astype(BF16)
            dgdu[at_r, to_up] = (d_hidden * silu).astype(BF16)

        loop(HF // wide, body)

    ffn(0, r)
    ag_forward(7)
    h2_finish()
    rest.wait_recv()
    go(passed_rest)
    ffn(0, r_sib)
    ffn(0, r_par)
    ffn(0, r_dia)

    YS, YR, ZR, ZX, QS, QR = (R[k] for k in ("YS", "YR", "ZR", "ZX", "QS", "QR"))
    y_sem, z_sem, x_sem = ([take(size) for _ in range(4)] for size in (Z, Z - 1, 1))

    def gradient(unit, group, store):
        at_g = lanes(B * group, B)
        if unit == 0:
            store(slice(0, FC), mm(hid[:, at_g], dyQ[...], TN))
        elif unit == 1:
            store(slice(HF, FC), mm(h2Q[:, at_g], dgdu[:, HF:FC], TN))
        elif unit == 2:
            store(slice(0, FC), mm(h2Q[:, at_g], dgdu[:, FC : 2 * FC], TN))
        else:
            store(slice(0, 3 * QC), mm(h1Q[:, at_g], WC[:, 0 : 3 * QC], TN))
            store(slice(3 * QC, 4 * QC), mm(attQ[:, at_g], R["daR"][...], TN))

    slots = {1: 0, 2: 1, 0: 2, 3: 0}

    def part(unit, ref):
        return ref.at[:, pl.ds(HF, HF)] if unit == 1 else ref

    def y_copy(unit, i):
        return remote(part(unit, YS.at[slots[unit], i]), part(unit, YR.at[unit, i]), peer, y_sem[unit] + i)

    def z_copy(unit, d, i=0):
        return remote(part(unit, YR.at[unit, i]), part(unit, ZR.at[unit, d - 1]), z_dev(d), z_sem[unit] + d - 1)

    middle = (1 + lax.div(z, 2)) * 8 + y * 4 + r

    def x_copy(unit, i=0):
        return remote(part(unit, YR.at[unit, i]), part(unit, ZX.at[unit]), middle, x_sem[unit])

    def target(unit, i):
        if not relays:
            return lax.rem(z + 1 + i, Z)
        even = 1 - lax.rem(z, 2)
        if unit == 0:
            return i + even * (1 - 2 * (i % 2 if isinstance(i, int) else lax.rem(i, 2)))
        o = (2 * i) % 3 + 3 * (i // 3) if isinstance(i, int) else lax.rem(2 * i, 3) + 3 * lax.div(i, 3)
        return o + even * (3 - 2 * o)

    def own_place(unit):
        if not relays:
            return Z - 1
        return 1 + 2 * lax.div(z, 2) if unit == 0 else 3 - lax.div(z * (3 - z), 2)

    def rs_first(unit, begin=0, count=Z):
        if unit == 3:
            for i in range(Z):
                y_copy(1, i).wait_send()

        def body(i):
            place = begin + i

            def store(cols, value):
                YS[slots[unit], place, :, cols] = value.astype(BF16)

            gradient(unit, 2 * target(unit, place) + 1 - y, store)
            y_copy(unit, place).start()

        loop(count, body)

    def rs_step(unit, i):
        goal = target(unit, i)
        d = lax.rem(goal + Z - z, Z)
        y_copy(unit, i).wait_recv()

        def store(cols, value):
            YR[unit, i, :, cols] = (value + YR[unit, i, :, cols].astype(F32)).astype(BF16)

        gradient(unit, 2 * goal + y, store)
        if not relays:
            pl.when(d != 0)(lambda: z_copy(unit, d, i).start())
            return
        far = outer & (goal + z == 3)
        pl.when(far)(lambda: x_copy(unit, i).start())
        pl.when((d != 0) & jnp.logical_not(far | (inner & (d == 2))))(lambda: z_copy(unit, d, i).start())

    def rs_relay(unit):
        i = 5 - 2 * z if unit == 0 else 3
        if relays:

            @pl.when(inner)
            def _():
                x_copy(unit).wait_recv()
                cols = slice(HF if unit == 1 else 0, FC)
                YR[unit, i, :, cols] = (YR[unit, i, :, cols].astype(F32) + ZX[unit, :, cols].astype(F32)).astype(BF16)
                z_copy(unit, 2, i).start()

    def rs_second(unit, begin=0, count=Z):
        loop(count, lambda i: rs_step(unit, begin + i))

    FS, FR, FX, FT, FK = (R[k] for k in ("FS", "FR", "FX", "FT", "FK"))
    fz_sem, fx_sem = take(Z - 1), take()
    last_over = remote(FT.at[0], FT.at[1], peer)

    def zf_copy(d, i=0):
        return remote(FS.at[i], FR.at[d - 1], z_dev(d), fz_sem + d - 1)

    def zf_far(i=0):
        return remote(FS.at[i], FX, middle, fx_sem)

    def zf_first():
        def body(i):
            goal = target(1, i)
            d = lax.rem(goal + Z - z, Z)
            for side in range(2):
                FS[i, side] = mm(h2Q[:, lanes(B * (2 * goal + side), B)], dgdu[:, 0:HF], TN).astype(BF16)
            if not relays:
                pl.when(d != 0)(lambda: zf_copy(d, i).start())
                return
            far = outer & (goal + z == 3)
            pl.when(far)(lambda: zf_far(i).start())
            pl.when((d != 0) & jnp.logical_not(far | (inner & (d == 2))))(lambda: zf_copy(d, i).start())

        loop(Z, body)

    def zf_relay():
        if relays:

            @pl.when(inner)
            def _():
                zf_far().wait_recv()
                FS[3] = (FS[3].astype(F32) + FX[...].astype(F32)).astype(BF16)
                zf_copy(2, 3).start()

    def zf_second():
        for d in range(1, Z):
            if relays and d != 2:
                pl.when(z != (0 if d == 1 else Z - 1))(zf_copy(d).wait_recv)
            else:
                zf_copy(d).wait_recv()

        def total(side):
            value = FS[own_place(1), side].astype(F32)
            for d in range(1, Z):
                value = value + FR[d - 1, side].astype(F32)
            return value

        FT[0] = total(1 - y).astype(BF16)
        go(last_over)
        FK[...] = total(y)

    quad_copies = {}

    def rs_third(unit):
        for d in range(1, Z):
            if relays and d != 2:
                pl.when(z != (0 if d == 1 else Z - 1))(z_copy(unit, d).wait_recv)
            else:
                z_copy(unit, d).wait_recv()
        width = 256
        if unit == 1:
            last_over.wait_recv()
        for j in range(FC // width):
            cols = slice(width * j, width * (j + 1))
            if unit == 1 and width * j < HF:
                value = FK[:, cols] + FT[1, :, cols].astype(F32)
            else:
                value = YR[unit, own_place(unit), :, cols].astype(F32)
                for i in range(1, Z):
                    value = value + ZR[unit, i - 1, :, cols].astype(F32)
            if unit == 0:
                R["gd"][:, cols] = value
            else:
                QS[unit - 1, :, cols] = value.astype(BF16)
        if unit:
            QR[unit - 1, r] = QS[unit - 1, at(rows * r, rows), :]
            quad_copies[unit] = [
                go(remote(QS.at[unit - 1, at(rows * q, rows)], QR.at[unit - 1, r], dev)) for dev, q in quad
            ]

    def rs_last(unit):
        for copy in quad_copies[unit]:
            copy.wait_recv()
        R["parts"][unit - 1] = QR[unit - 1]

    rsS, rsR = R["rsS"], R["rsR"]

    def quad_sum(kind, prepare_block, partial, fill=None):
        copies = [
            remote(rsS.at[0], rsR.at[kind, 0], sib),
            remote(rsS.at[1], rsR.at[kind, 1], sib),
            remote(rsS.at[2], rsR.at[kind, 2], par),
        ]

        def blocks(role, store):
            def body(j):
                store(lanes(wide * j, wide), partial(at(T * role, T), wide * j))

            loop(D // wide, body)

        def to_dia(cols, value):
            rsS[1, :, cols] = value.astype(BF16)

        def to_par(cols, value):
            rsS[2, :, cols] = (value + rsR[kind, 1, :, cols].astype(F32)).astype(BF16)

        def to_sib(cols, value):
            rsS[0, :, cols] = value.astype(BF16)

        def keep(cols, value):
            acc[:, cols] = value

        prepare_block(r_dia)
        blocks(r_dia, to_dia)
        copies[1].start()
        prepare_block(r_par)
        copies[1].wait_recv()
        blocks(r_par, to_par)
        copies[2].start()
        if fill:
            fill(0)
        prepare_block(r_sib)
        blocks(r_sib, to_sib)
        copies[0].start()
        if fill:
            fill(1)
        prepare_block(r)
        blocks(r, keep)

        def finish():
            copies[0].wait_recv()
            copies[2].wait_recv()
            for copy in copies:
                copy.wait_send()

        return finish

    def summed(kind, at_i):
        return acc[at_i, :] + (rsR[kind, 0, at_i, :].astype(F32) + rsR[kind, 2, at_i, :].astype(F32))

    def nothing(role):
        return None

    zf_first()
    rs_first(1)
    rs_first(0, 0, Z // 2)
    ag_finish(6)
    ag_finish(7)
    h2_sum = quad_sum(
        0, functools.partial(ffn, 1), lambda at_r, j: mm(dgdu[at_r, :], WB[at(j, wide), :], NT),
        lambda i: (zf_relay() if i else None, rs_second(1, i, 1)),
    )
    rs_second(1, 2, 1)
    rs_first(2)
    h2_sum()

    TT, TR = R["TT"], R["TR"]
    daS, daR, dattS, dattR = (R[k] for k in ("daS", "daR", "dattS", "dattR"))
    TT[0] = jnp.zeros((8, D), F32)

    def norm_back(v, d_out, gain, row):
        inv = lax.rsqrt(jnp.mean(v * v, axis=-1, keepdims=True) + EPSILON)
        TT[0, row : row + 1, :] += jnp.sum(d_out * (v * inv), axis=0, keepdims=True)
        d = d_out * gain
        return inv * d - v * (inv * inv * inv * jnp.mean(d * v, axis=-1, keepdims=True))

    def mix_back(i):
        at_i = at(step * i, step)
        d = norm_back(x1[at_i, :], summed(0, at_i), GA[1:2, :], 1)
        d = d + dyQ[at(T * r + step * i, step), :].astype(F32)
        dx1[at_i, :] = d
        daS[at_i, :] = d.astype(BF16)

    loop(T // step, mix_back)
    sendD = [remote(daS.at[:, lanes(QC * q, QC)], daR.at[at(T * r, T)], dev) for dev, q in quad]
    sendT = [remote(dattS.at[:, lanes(QC * q, QC)], dattR.at[at(T * r, T)], dev) for dev, q in quad]

    def out_back(j):
        dattS[:, lanes(wide * j, wide)] = mm(daS[...], WO[at(wide * j, wide), :], NT).astype(BF16)

    loop(D // wide, out_back)
    for copy in sendT:
        go(copy)
    for copy in sendD:
        go(copy)
    dattR[at(T * r, T), :] = dattS[:, lanes(QC * r, QC)]
    daR[at(T * r, T), :] = daS[:, lanes(QC * r, QC)]
    rs_second(1, 3, 1)
    rs_first(0, Z // 2, Z // 2)
    zf_second()
    rs_relay(1)
    rs_second(0, 0, Z // 2)
    out_sum = quad_sum(1, nothing, lambda at_r, j: mm(hid[at_r, :], WC[:, lanes(j, wide)]))
    ag_drain(2)
    ag_drain(3)
    for copy in sendT:
        copy.wait_recv()

    def write_out(i):
        at_i = at(step * i, step)
        R["act"][at_i, :] = (x1[at_i, :] + summed(1, at_i)).astype(BF16)

    HG, BG = R["HG"], R["BG"]
    HG[...] = jnp.zeros(HG.shape, F32)
    BG[...] = jnp.zeros(BG.shape, F32)

    def fold(v):
        return jnp.sum(v.reshape(L // 8, 8, 128), axis=0)

    def prepare_back(raw, d, m, j, cosine, sine, factor):
        if factor != 1.0:
            d = d * factor
        d = d * cosine - swap(d) * sine
        inv = lax.rsqrt(per_head(raw * raw) / 64 + EPSILON)
        HG[m, j] += fold(d * (raw * inv))
        d = d * small[2 + m : 3 + m, :]
        return inv * d - raw * (inv * inv * inv * (per_head(d * raw) / 64))

    def attend_back(q):
        at_q = at(L * q, L)
        _, same = masks(q)
        cosine, sine = CT[at_q, :], ST[at_q, :]
        for j in range(QC // 128):
            tile = slice(128 * j, 128 * (j + 1))
            q2, k2, v2, d2 = qr[at_q, tile], kr[at_q, tile], vb[at_q, tile], dattR[at_q, tile]
            dq, dk, dv = [], [], []
            for h in range(2):
                p = PR[q, 2 * j + h]
                dp = mm(d2 * heads[h], v2, NT)
                ds = (p * (dp - jnp.sum(p * dp, axis=-1, keepdims=True))).astype(BF16)
                wide = ds.astype(F32)
                BG[0, 2 * j + h] += fold(jnp.where(same, 0.0, wide))
                BG[1, 2 * j + h] += fold(jnp.where(same, wide, 0.0))
                dv.append(mm(p.astype(BF16), d2, TN))
                dq.append(mm(ds, k2))
                dk.append(mm(ds, q2, TN))
            d_query = jnp.where(low, dq[0], dq[1])
            d_key = jnp.where(low, dk[0], dk[1])
            d_query = prepare_back(qraw[at_q, tile], d_query, 0, j, cosine, sine, 0.125)
            d_key = prepare_back(kraw[at_q, tile], d_key, 1, j, cosine, sine, 1.0)
            WC[at_q, tile] = d_query.astype(BF16)
            WC[at_q, QC + 128 * j : QC + 128 * (j + 1)] = d_key.astype(BF16)
            WC[at_q, 2 * QC + 128 * j : 2 * QC + 128 * (j + 1)] = jnp.where(low, dv[0], dv[1]).astype(BF16)

    def attend_and_step(i):
        for q in range(S):
            attend_back(S * i + q)
        rs_step(2, i)

    loop(4, attend_and_step)
    for copy in sendD + [near_rest, passed_rest]:
        copy.wait_recv()
    rs_first(3)
    rs_relay(2)
    out_sum()
    loop(T // step, write_out)
    in_sum = quad_sum(
        2, nothing, lambda at_r, j: mm(WC[at_r, 0 : 3 * QC], WA[at(j, wide), 0 : 3 * QC], NT),
        lambda i: rs_second(0, Z // 2 + i, 1),
    )
    rs_relay(0)
    for k in range(len(chunks)):
        if k not in (2, 3):
            ag_drain(k)
    rs_third(1)
    in_sum()

    def input_back(i):
        at_i = at(step * i, step)
        d = norm_back(tok[at_i, :].astype(F32), summed(2, at_i), GA[0:1, :], 0)
        R["ig"][at_i, :] = (dx1[at_i, :] + d).astype(BF16)

    loop(T // step, input_back)

    for m in range(2):
        value = HG[m, 0]
        for j in range(1, QC // 128):
            value = value + HG[m, j]
        TT[0, 2:3, 128 * m : 128 * (m + 1)] = jnp.sum(value, axis=0, keepdims=True)
    for m in range(2):
        line = jnp.zeros((1, 128), F32)
        for h in range(QC // 64):
            line = line + jnp.where(spot == QC // 64 * r + h, jnp.sum(BG[m, h]), 0.0)
        TT[0, 3 + m : 4 + m, 0:128] = line
    t1, t2, t3, t_finish = tile_sum(TT, TR)
    t1()
    rs_second(3, 0, 3)
    t2()
    rs_second(3, 3, 1)
    rs_relay(3)
    rs_third(2)
    rs_last(1)
    t3()
    rs_third(0)
    rs_third(3)
    rs_last(2)
    R["tot"][...] = t_finish()
    rs_last(3)
    for copy in sent:
        copy.wait_send()
    for d in range(1, Z):
        nearby(d, zf_copy(d).wait_send)
    if relays:
        pl.when(outer)(zf_far().wait_send)
    for unit in range(4):
        for i in range(Z):
            if unit != 1:
                y_copy(unit, i).wait_send()
            if i:
                nearby(i, z_copy(unit, i).wait_send)
        if relays:
            pl.when(outer)(x_copy(unit).wait_send)


LAST = ("act", "ig", "gq", "gk", "gv", "go", "gg", "gu", "gd", "ga", "gf", "ghq", "ghk", "gb")


def finishing(s, *refs):
    names = tuple(name + "_in" for name in OUTPUTS) + LAST
    R = dict(zip(names, refs, strict=True))
    D, rows, G, QC, FC, B, HD, H = (s[k] for k in ("D", "rows", "G", "QC", "FC", "B", "HD", "H"))
    HF = FC // 2
    for name in ("act", "ig", "gd"):
        R[name][...] = R[name + "_in"][...]
    parts = R["parts_in"]
    for q in range(4):
        for m, name in enumerate(("gq", "gk", "gv", "go")):
            R[name][:, QC * q : QC * (q + 1)] = parts[2, q, :, QC * m : QC * (m + 1)].astype(F32)
        for j in range(G):
            half, within = divmod(B * j, HF)
            target = slice(B * (4 * j + q), B * (4 * j + q) + B)
            R["gg"][:, target] = parts[half, q, :, within : within + B].astype(F32)
            R["gu"][:, target] = parts[half, q, :, HF + within : HF + within + B].astype(F32)
    tot = R["tot_in"]
    own = lax.axis_index("fsdp") * rows
    mine = pltpu.roll(tot[:, lanes(128 * lax.div(own, 128), 128)], lax.rem(128 - lax.rem(own, 128), 128), 1)
    R["ga"][...] = mine[0:1, 0:rows]
    R["gf"][...] = mine[1:2, 0:rows]
    both = tot[:, 0:256]
    both = both + pltpu.roll(both, 256 - HD, 1)
    R["ghq"][...] = both[2:3, 0:HD]
    R["ghk"][...] = both[2:3, 128 : 128 + HD]
    R["gb"][...] = tot[3:5, 0:H]


def layer(s, tokens, segment_ids, variate_ids, time_ids, w_query, w_key, w_value, w_out, w_gate, w_up, w_down,
          gain_attn, gain_ffn, gain_query, gain_key, variate_bias, cotangent):
    D, T, rows, B, FF, FC, HD, H = (s[k] for k in ("D", "T", "rows", "B", "FF", "FC", "HD", "H"))
    lines = [
        gain_attn[None], gain_ffn[None], jnp.tile(gain_query[None], (1, 2)), jnp.tile(gain_key[None], (1, 2)),
        variate_bias,
    ]
    small, line = jnp.zeros((8, 128), F32), 0
    for piece in lines:
        high, wide = piece.shape
        small = small + jnp.pad(piece.astype(F32), ((line, 8 - line - high), (0, 128 - wide)))
        line += high
    scratch = scratch_of(s)
    names = INPUTS + OUTPUTS + tuple(scratch)
    vmem, anywhere = pl.BlockSpec(memory_space=pltpu.VMEM), pl.BlockSpec(memory_space=pl.ANY)
    here = {"seg", "var", "tim", "small"}

    def shape(*dims, kind=F32):
        return jax.ShapeDtypeStruct(dims, kind)

    tokens_shape = shape(T, D, kind=BF16)
    outs = pl.pallas_call(
        functools.partial(fused, s, names),
        out_shape=[tokens_shape, tokens_shape, shape(B, D), shape(3, 4, rows, FC, kind=BF16), shape(8, D)],
        in_specs=[vmem if name in here else anywhere for name in INPUTS],
        out_specs=[vmem] * len(OUTPUTS),
        scratch_shapes=list(scratch.values()),
        compiler_params=pltpu.CompilerParams(
            collective_id=0, has_side_effects=True, vmem_limit_bytes=64 << 20
        ),
        name="fused_layer",
    )(
        tokens.reshape(T, D), cotangent.reshape(T, D), segment_ids, variate_ids, time_ids,
        w_query, w_key, w_value, w_out, w_gate, w_up, w_down, small,
    )
    last = pl.pallas_call(
        functools.partial(finishing, s),
        out_shape=[tokens_shape, tokens_shape] + [shape(rows, D)] * 4 + [shape(rows, FF)] * 2
        + [shape(B, D), shape(1, rows), shape(1, rows), shape(1, HD), shape(1, HD), shape(2, H)],
        in_specs=[vmem] * len(OUTPUTS),
        out_specs=[vmem] * len(LAST),
        name="finishing",
    )(*outs)
    flat = [value.reshape(-1) for value in last[9:13]]
    return (last[0].reshape(tokens.shape), last[1].reshape(tokens.shape), *last[2:9], *flat, last[13])


def local(tokens, segment_ids, variate_ids, time_ids, *rest):
    s = sizes_of(lax.axis_size("fsdp"), tokens, rest[0], rest[4], rest[9], rest[11])
    chosen = functools.partial(layer, s) if fits(s) else plain
    return chosen(tokens, segment_ids, variate_ids, time_ids, *rest)


def solution(mesh):
    placed = (
        P("fsdp", None, None),
        P("fsdp", None),
        P("fsdp", None),
        P("fsdp", None),
        P("fsdp", None),
        P("fsdp", None),
        P("fsdp", None),
        P("fsdp", None),
        P("fsdp", None),
        P("fsdp", None),
        P("fsdp", None),
        P("fsdp"),
        P("fsdp"),
        P(),
        P(),
        P(),
        P("fsdp", None, None),
    )
    return jax.shard_map(
        local,
        mesh=mesh,
        in_specs=placed,
        out_specs=(
            P("fsdp", None, None),
            P("fsdp", None, None),
            P("fsdp", None),
            P("fsdp", None),
            P("fsdp", None),
            P("fsdp", None),
            P("fsdp", None),
            P("fsdp", None),
            P("fsdp", None),
            P("fsdp"),
            P("fsdp"),
            P(),
            P(),
            P(),
        ),
        check_vma=False,
    )
```

```python
import functools
import math

import jax
import jax.numpy as jnp
from jax import lax
from jax.experimental import pallas as pl
from jax.experimental.pallas import tpu as pltpu
from jax.sharding import PartitionSpec as P

EPSILON = 1e-05


def normalize(values, scale_gain):
    return (
        values * lax.rsqrt(jnp.mean(values * values, axis=-1, keepdims=True) + EPSILON) * scale_gain
    )


def rotate(values, moments):
    halfway = values.shape[-1] // 2
    frequency = jnp.exp(-math.log(10000.0) * jnp.arange(halfway).astype(jnp.float32) / halfway)
    angles = moments.astype(jnp.float32)[:, None] * frequency[None, :]
    cosine = jnp.cos(angles)[:, None, :]
    sine_part = jnp.sin(angles)[:, None, :]
    former = values[..., :halfway]
    latter = values[..., halfway:]
    return jnp.concatenate(
        [former * cosine - latter * sine_part, former * sine_part + latter * cosine], axis=-1
    )


def prepare(raw_heads, head_gain, moments, factor):
    return rotate(normalize(raw_heads, head_gain), moments) * factor


def swiglu(gate_act, up_act):
    return jax.nn.silu(gate_act) * up_act


def attention_masks(segments, variates):
    length = segments.shape[0]
    diagonal = jnp.arange(length)[:, None] == jnp.arange(length)[None, :]
    allowed = (segments[:, None] == segments[None, :]) & ((segments[None, :] != 0) | diagonal)
    same_var = variates[:, None] == variates[None, :]
    return (allowed, same_var)


def scoring(q_rot, k_rot, bias_table, allowed, same_var):
    scores = jnp.einsum("qhe,khe->hqk", q_rot, k_rot, preferred_element_type=jnp.float32)
    scores = scores + jnp.where(
        same_var[None], bias_table[1][:, None, None], bias_table[0][:, None, None]
    )
    return jnp.where(allowed[None], scores, -1000000000.0)


def project(left, right):
    return jnp.dot(left, right, preferred_element_type=jnp.float32)


def across(left, right):
    return lax.dot_general(
        left, right, (((0,), (0,)), ((), ())), preferred_element_type=jnp.float32
    )


def against(left, weight):
    return lax.dot_general(
        left, weight, (((1,), (1,)), ((), ())), preferred_element_type=jnp.float32
    )


def forward(inputs_low, weights, side_params, segments, variates, moments):
    w_query, w_key, w_value, w_out, w_gate, w_up, w_down, gain_attn, gain_ffn = weights
    gain_query, gain_key, bias_table = side_params
    length, model_width = inputs_low.shape
    head_count = bias_table.shape[1]
    head_dim = gain_query.shape[0]
    inputs = inputs_low.astype(jnp.float32)
    normed = normalize(inputs, gain_attn.astype(jnp.float32)).astype(jnp.bfloat16)
    queries = project(normed, w_query).reshape(length, head_count, head_dim)
    key_raw = project(normed, w_key).reshape(length, head_count, head_dim)
    v_low = project(normed, w_value).reshape(length, head_count, head_dim).astype(jnp.bfloat16)
    q_rot = prepare(queries, gain_query, moments, head_dim ** (-0.5)).astype(jnp.bfloat16)
    k_rot = prepare(key_raw, gain_key, moments, 1.0).astype(jnp.bfloat16)
    allowed, same_var = attention_masks(segments, variates)
    scores = scoring(q_rot, k_rot, bias_table, allowed, same_var)
    maximum = jnp.max(scores, axis=-1, keepdims=True)
    exponent = jnp.exp(scores - maximum)
    row_total = jnp.sum(exponent, axis=-1, keepdims=True)
    log_total = maximum + jnp.log(row_total)
    softmax_probs = (exponent / row_total).astype(jnp.bfloat16)
    attended = jnp.einsum("hqk,khe->qhe", softmax_probs, v_low, preferred_element_type=jnp.float32)
    attended = attended.reshape(length, model_width).astype(jnp.bfloat16)
    mixed_state = inputs + project(attended, w_out)
    normed_ffn = normalize(mixed_state, gain_ffn.astype(jnp.float32)).astype(jnp.bfloat16)
    gate_act = project(normed_ffn, w_gate)
    up_act = project(normed_ffn, w_up)
    hidden = swiglu(gate_act, up_act).astype(jnp.bfloat16)
    result = mixed_state + project(hidden, w_down)
    kept_state = (
        inputs,
        normed,
        queries,
        key_raw,
        q_rot,
        k_rot,
        v_low,
        log_total,
        attended,
        mixed_state,
        normed_ffn,
        gate_act,
        up_act,
        hidden,
    )
    return (result, kept_state)


def backward(upstream, kept_state, weights, side_params, segments, variates, moments):
    (
        inputs,
        normed,
        queries,
        key_raw,
        q_rot,
        k_rot,
        v_low,
        log_total,
        attended,
        mixed_state,
        normed_ffn,
        gate_act,
        up_act,
        hidden,
    ) = kept_state
    w_query, w_key, w_value, w_out, w_gate, w_up, w_down, gain_attn, gain_ffn = weights
    gain_query, gain_key, bias_table = side_params
    length, head_count, head_dim = queries.shape
    grad_down = across(hidden, upstream)
    d_hidden = against(upstream, w_down)
    _, pullback = jax.vjp(swiglu, gate_act, up_act)
    d_gate, d_up = pullback(d_hidden)
    d_gate = d_gate.astype(jnp.bfloat16)
    d_up = d_up.astype(jnp.bfloat16)
    grad_gate = across(normed_ffn, d_gate)
    grad_up = across(normed_ffn, d_up)
    d_normed_ffn = against(d_gate, w_gate) + against(d_up, w_up)
    _, pullback = jax.vjp(normalize, mixed_state, gain_ffn.astype(jnp.float32))
    d_mixed, grad_gain_ffn = pullback(d_normed_ffn)
    d_mixed = d_mixed + upstream.astype(jnp.float32)
    d_branch = d_mixed.astype(jnp.bfloat16)
    grad_out = across(attended, d_branch)
    d_attended = against(d_branch, w_out).astype(jnp.bfloat16).reshape(length, head_count, head_dim)
    allowed, same_var = attention_masks(segments, variates)
    scores = scoring(q_rot, k_rot, bias_table, allowed, same_var)
    softmax_probs = jnp.exp(scores - log_total)
    d_probs = jnp.einsum("qhe,khe->hqk", d_attended, v_low, preferred_element_type=jnp.float32)
    d_values = jnp.einsum(
        "hqk,qhe->khe",
        softmax_probs.astype(jnp.bfloat16),
        d_attended,
        preferred_element_type=jnp.float32,
    )
    d_values = d_values.reshape(length, head_count * head_dim).astype(jnp.bfloat16)
    weighted = jnp.sum(softmax_probs * d_probs, axis=-1, keepdims=True)
    d_scores = (softmax_probs * (d_probs - weighted)).astype(jnp.bfloat16)
    d_float = d_scores.astype(jnp.float32)
    same_sum = jnp.sum(jnp.where(same_var[None], d_float, 0.0), axis=(1, 2))
    other_sum = jnp.sum(jnp.where(same_var[None], 0.0, d_float), axis=(1, 2))
    grad_bias = jnp.stack([other_sum, same_sum])
    d_qrot = jnp.einsum("hqk,khe->qhe", d_scores, k_rot, preferred_element_type=jnp.float32)
    d_krot = jnp.einsum("hqk,qhe->khe", d_scores, q_rot, preferred_element_type=jnp.float32)
    factor = head_dim ** (-0.5)
    _, pullback = jax.vjp(
        lambda raw_heads, head_gain: prepare(raw_heads, head_gain, moments, factor),
        queries,
        gain_query,
    )
    d_queries, grad_gain_query = pullback(d_qrot)
    _, pullback = jax.vjp(
        lambda raw_heads, head_gain: prepare(raw_heads, head_gain, moments, 1.0), key_raw, gain_key
    )
    d_keys, grad_gain_key = pullback(d_krot)
    d_queries = d_queries.reshape(length, head_count * head_dim).astype(jnp.bfloat16)
    d_keys = d_keys.reshape(length, head_count * head_dim).astype(jnp.bfloat16)
    grad_query = across(normed, d_queries)
    grad_key = across(normed, d_keys)
    grad_value = across(normed, d_values)
    d_normed = against(d_queries, w_query) + against(d_keys, w_key) + against(d_values, w_value)
    _, pullback = jax.vjp(normalize, inputs, gain_attn.astype(jnp.float32))
    d_inputs, grad_gain_attn = pullback(d_normed)
    row_grads = jnp.concatenate(
        [grad_query, grad_key, grad_value, grad_out, grad_gate, grad_up], axis=1
    )
    small = (grad_gain_query, grad_gain_key, grad_bias, grad_gain_attn, grad_gain_ffn)
    return (d_inputs + d_mixed, row_grads, grad_down, small)


def plain(
    tokens,
    segment_ids,
    variate_ids,
    time_ids,
    w_query,
    w_key,
    w_value,
    w_out,
    w_gate,
    w_up,
    w_down,
    gain_attn,
    gain_ffn,
    gain_query,
    gain_key,
    variate_bias,
    cotangent,
):
    devices = lax.axis_size("fsdp")
    owner = lax.axis_index("fsdp")
    width = w_query.shape[1]
    hidden_width = w_gate.shape[1]
    own_rows = w_query.shape[0]
    own_down = w_down.shape[0]
    side_params = (
        gain_query.astype(jnp.float32),
        gain_key.astype(jnp.float32),
        variate_bias.astype(jnp.float32),
    )
    rows_total = jnp.zeros((own_rows * devices, 4 * width + 2 * hidden_width), jnp.float32)
    down_total = jnp.zeros((own_down * devices, width), jnp.float32)
    side_totals = (
        jnp.zeros(gain_query.shape, jnp.float32),
        jnp.zeros(gain_key.shape, jnp.float32),
        jnp.zeros(variate_bias.shape, jnp.float32),
        jnp.zeros((own_rows * devices,), jnp.float32),
        jnp.zeros((own_rows * devices,), jnp.float32),
    )
    results = []
    input_grads = []
    for micro_index in range(tokens.shape[0]):
        segments = segment_ids[micro_index]
        variates = variate_ids[micro_index]
        moments = time_ids[micro_index]
        forward_weights = (
            lax.all_gather(w_query, "fsdp", axis=0, tiled=True),
            lax.all_gather(w_key, "fsdp", axis=0, tiled=True),
            lax.all_gather(w_value, "fsdp", axis=0, tiled=True),
            lax.all_gather(w_out, "fsdp", axis=0, tiled=True),
            lax.all_gather(w_gate, "fsdp", axis=0, tiled=True),
            lax.all_gather(w_up, "fsdp", axis=0, tiled=True),
            lax.all_gather(w_down, "fsdp", axis=0, tiled=True),
            lax.all_gather(gain_attn, "fsdp", axis=0, tiled=True),
            lax.all_gather(gain_ffn, "fsdp", axis=0, tiled=True),
        )
        result, kept_state = forward(
            tokens[micro_index], forward_weights, side_params, segments, variates, moments
        )
        results.append(result.astype(jnp.bfloat16))
        backward_weights = (
            lax.all_gather(w_query, "fsdp", axis=0, tiled=True),
            lax.all_gather(w_key, "fsdp", axis=0, tiled=True),
            lax.all_gather(w_value, "fsdp", axis=0, tiled=True),
            lax.all_gather(w_out, "fsdp", axis=0, tiled=True),
            lax.all_gather(w_gate, "fsdp", axis=0, tiled=True),
            lax.all_gather(w_up, "fsdp", axis=0, tiled=True),
            lax.all_gather(w_down, "fsdp", axis=0, tiled=True),
            lax.all_gather(gain_attn, "fsdp", axis=0, tiled=True),
            lax.all_gather(gain_ffn, "fsdp", axis=0, tiled=True),
        )
        d_inputs, row_grads, down_grads, small = backward(
            cotangent[micro_index],
            kept_state,
            backward_weights,
            side_params,
            segments,
            variates,
            moments,
        )
        input_grads.append(d_inputs.astype(jnp.bfloat16))
        rows_total = rows_total + row_grads
        down_total = down_total + down_grads
        side_totals = tuple((running + fresh for running, fresh in zip(side_totals, small)))
    owned_rows = lax.psum_scatter(rows_total, "fsdp", scatter_dimension=0, tiled=True)
    owned_down = lax.psum_scatter(down_total, "fsdp", scatter_dimension=0, tiled=True)
    shared = lax.psum(
        (side_totals[0], side_totals[1], side_totals[2], side_totals[3], side_totals[4]), "fsdp"
    )
    gain_attn_own = lax.dynamic_slice_in_dim(shared[3], owner * own_rows, own_rows, 0)
    gain_ffn_own = lax.dynamic_slice_in_dim(shared[4], owner * own_rows, own_rows, 0)
    grad_query = owned_rows[:, 0:width]
    grad_key = owned_rows[:, width : 2 * width]
    grad_value = owned_rows[:, 2 * width : 3 * width]
    grad_out = owned_rows[:, 3 * width : 4 * width]
    grad_gate = owned_rows[:, 4 * width : 4 * width + hidden_width]
    grad_up = owned_rows[:, 4 * width + hidden_width :]
    return (
        jnp.stack(results),
        jnp.stack(input_grads),
        grad_query,
        grad_key,
        grad_value,
        grad_out,
        grad_gate,
        grad_up,
        owned_down,
        gain_attn_own,
        gain_ffn_own,
        shared[0],
        shared[1],
        shared[2],
    )


F32 = jnp.float32
BF16 = jnp.bfloat16
MESH = pl.DeviceIdType.MESH
NT = (((1,), (1,)), ((), ()))
TN = (((0,), (0,)), ((), ()))


def mm(left, right, dims=(((1,), (0,)), ((), ()))):
    return lax.dot_general(left, right, dims, preferred_element_type=F32)


def at(start, size):
    return pl.ds(pl.multiple_of(start, size), size)


def lanes(start, size):
    return pl.ds(pl.multiple_of(start, 128), size)


def loop(count, body):
    lax.fori_loop(0, count, lambda i, carry: (body(i), carry)[1], 0)


def sizes_of(devices, tokens, w_query, w_gate, gain_query, bias):
    seqs, length, width = tokens.shape
    own_rows, hidden = w_query.shape[0], w_gate.shape[1]
    return dict(
        n=devices, S=seqs, L=length, D=width, FF=hidden, rows=own_rows, T=seqs * length,
        G=devices // 4, Z=devices // 8, QC=width // 4, FC=hidden // 4, B=4 * own_rows,
        HD=gain_query.shape[0], H=bias.shape[1],
    )


def fits(s):
    return (
        s["n"] % 8 == 0 and s["rows"] % 16 == 0 and s["L"] == 128 and s["HD"] == 64
        and s["H"] * s["HD"] == s["D"] and s["QC"] % 128 == 0 and s["FF"] == 4 * s["D"]
        and s["B"] == 128 and s["FC"] // 2 % s["B"] == 0 and s["FC"] == s["D"]
    )


def scratch_of(s):
    n, S, L, D, rows, T, G, Z, QC, FC, B = (
        s[k] for k in ("n", "S", "L", "D", "rows", "T", "G", "Z", "QC", "FC", "B")
    )
    Q = 4 * T
    vm = pltpu.VMEM
    return dict(
        WA=vm((D, 4 * QC), BF16), WB=vm((D, 2 * FC), BF16), WC=vm((FC, D), BF16), WO=vm((D, D), BF16),
        SA=vm((4, rows, 4 * QC), BF16), SB=vm((4, rows, 2 * FC), BF16),
        h1Q=vm((Q, D), BF16), dyQ=vm((Q, D), BF16), attQ=vm((Q, D), BF16), h2Q=vm((Q, D), BF16),
        qraw=vm((Q, QC), F32), kraw=vm((Q, QC), F32),
        qr=vm((Q, QC), BF16), kr=vm((Q, QC), BF16), vb=vm((Q, QC), BF16),
        PR=vm((4 * S, QC // 64, L, L), F32), CT=vm((Q, 128), F32), ST=vm((Q, 128), F32),
        x1=vm((T, D), F32), dx1=vm((T, D), F32), acc=vm((T, D), F32),
        hid=vm((Q, FC), BF16), dgdu=vm((Q, 2 * FC), BF16),
        rsS=vm((3, T, D), BF16), rsR=vm((3, 3, T, D), BF16),
        daS=vm((T, D), BF16), daR=vm((Q, QC), BF16), dattS=vm((T, D), BF16), dattR=vm((Q, QC), BF16),
        YS=vm((3, Z, B, FC), BF16), YR=vm((4, Z, B, FC), BF16), ZR=vm((4, Z - 1, B, FC), BF16), ZX=vm((4, B, FC), BF16),
        FS=vm((Z, 2, B, FC // 2), BF16), FR=vm((Z - 1, 2, B, FC // 2), BF16), FX=vm((2, B, FC // 2), BF16),
        FT=vm((2, B, FC // 2), BF16), FK=vm((B, FC // 2), F32),
        QS=vm((3, B, FC), BF16), QR=vm((3, 4, rows, FC), BF16),
        idq=vm((4 * S, 8, L), F32),
        SW=vm((4, rows, D), BF16), SG=vm((2, rows, s["FF"]), BF16), TK=vm((T, D), BF16),
        GQ=vm((4, 8, B), F32), GA=vm((8, D), F32), load=pltpu.SemaphoreType.DMA((9,)),
        TT=vm((3, 8, D), F32), TR=vm((4 + Z, 8, D), F32),
        HG=vm((4, QC // 128, 8, 128), F32), BG=vm((2, QC // 64, 8, 128), F32),
        send=pltpu.SemaphoreType.DMA((192,)), recv=pltpu.SemaphoreType.DMA((192,)),
    )


INPUTS = (
    "tok", "cot", "seg", "var", "tim", "wq", "wk", "wv", "wo", "wg", "wu", "wd", "small",
)
OUTPUTS = ("act", "ig", "gd", "parts", "tot")


def fused(s, names, *refs):
    R = dict(zip(names, refs, strict=True))
    n, S, L, D, rows, T, G, Z, QC, FC, B = (
        s[k] for k in ("n", "S", "L", "D", "rows", "T", "G", "Z", "QC", "FC", "B")
    )
    HF = FC // 2
    Q = 4 * T
    me = lax.axis_index("fsdp")
    r, c, xx, g = lax.rem(me, 4), lax.rem(me, 2), lax.rem(lax.div(me, 2), 2), lax.div(me, 4)
    y, z = lax.rem(g, 2), lax.div(g, 2)
    r_sib, r_par = r + 1 - 2 * c, r + 2 - 4 * xx
    r_dia = r_sib + 2 - 4 * xx
    sib, par, dia = me - r + r_sib, me - r + r_par, me - r + r_dia
    peer = me + 4 - 8 * y
    quad = ((sib, r_sib), (par, r_par), (dia, r_dia))

    def at_z(step):
        return lax.rem(z + step, Z)

    def z_dev(step):
        return at_z(step) * 8 + y * 4 + r

    def z_src(step):
        return lax.rem(z + Z - step, Z)

    relays = Z == 4
    inner, outer = lax.rem(z + 1, 4) >= 2, lax.rem(z + 1, 4) < 2

    def nearby(step, action):
        if relays and step != 2:
            pl.when(z != (Z - 1 if step == 1 else 0))(action)
        else:
            action()

    used = [0]
    sent = []

    def take(count=1):
        used[0] += count
        return used[0] - count

    def remote(src, dst, device, sem=None, arrival=None):
        sem = take() if sem is None else sem
        arrival = sem if arrival is None else arrival
        return pltpu.make_async_remote_copy(
            src_ref=src, dst_ref=dst, send_sem=R["send"].at[sem], recv_sem=R["recv"].at[arrival],
            device_id=(device,), device_id_type=MESH,
        )

    def go(copy):
        copy.start()
        sent.append(copy)
        return copy

    barrier = pltpu.get_barrier_semaphore()
    others = [sib, par, dia, peer] + [z_dev(d) for d in range(1, Z)]
    for device in others:
        pl.semaphore_signal(barrier, inc=1, device_id=(device,), device_id_type=MESH)

    SA, SB, SW, SG, WA, WB, WC, WO = (R[k] for k in ("SA", "SB", "SW", "SG", "WA", "WB", "WC", "WO"))
    dyQ, h1Q, h2Q, attQ, tok = R["dyQ"], R["h1Q"], R["h2Q"], R["attQ"], R["TK"]
    places = [("wq", SW.at[0]), ("wk", SW.at[1]), ("wv", SW.at[2]), ("wo", SW.at[3]), ("wd", WC.at[at(B * g, B)])]
    places += [("tok", tok), ("wg", SG.at[0]), ("wu", SG.at[1]), ("cot", dyQ.at[at(T * r, T)])]
    loads = {}
    for i, (name, place) in enumerate(places):
        loads[name] = pltpu.make_async_copy(R[name], place, R["load"].at[i])
        loads[name].start()
    own = at(B * g + rows * r, rows)
    idq, small, GQ, GA = R["idq"], R["small"], R["GQ"], R["GA"]
    for q in range(S):
        idq[S * r + q, 0:1, :] = R["seg"][q : q + 1, :].astype(F32)
        idq[S * r + q, 1:2, :] = R["var"][q : q + 1, :].astype(F32)
        idq[S * r + q, 2:3, :] = R["tim"][q : q + 1, :].astype(F32)
        idq[S * r + q, 3:8, :] = jnp.zeros((5, L), F32)
    GQ[r] = pltpu.roll(small[...], rows * r, 1)
    for m, name in enumerate(("wq", "wk", "wv", "wo")):
        loads[name].wait()
        for q in range(4):
            SA[q, :, QC * m : QC * (m + 1)] = SW[m, :, QC * q : QC * (q + 1)]
    WA[own, :] = SA[r]
    pl.semaphore_wait(barrier, len(others))

    def tile_sum(tile, got):
        first = [remote(tile.at[0], got.at[i], dev) for i, (dev, _) in enumerate(quad)]
        second = [remote(tile.at[1], got.at[4 + z], z_dev(d)) for d in range(1, Z)]
        third = remote(tile.at[2], got.at[3], peer)

        def round1():
            for copy in first:
                go(copy)

        def round2():
            for copy in first:
                copy.wait_recv()
            value = (tile[0] + got[0]) + (got[1] + got[2])
            tile[1] = value
            got[4 + z] = value
            for copy in second:
                go(copy)

        def round3():
            for copy in second:
                copy.wait_recv()
            value = got[4]
            for i in range(1, Z):
                value = value + got[4 + i]
            tile[2] = value
            go(third)

        def finish():
            third.wait_recv()
            return tile[2] + got[3]

        return round1, round2, round3, finish

    def quad_gather(block):
        to_sib, to_par = remote(block(r), block(r), sib), remote(block(r), block(r), par)
        passed = remote(block(r_par), block(r_par), sib)

        def start():
            go(to_par)
            go(to_sib)

        def forward():
            to_par.wait_recv()
            go(passed)

        def finish():
            to_sib.wait_recv()
            passed.wait_recv()

        return start, forward, finish

    chunks = [(WA, 0, 2 * QC), (WA, 2 * QC, 2 * QC), (WC, 0, D // 2), (WC, D // 2, D // 2)]
    chunks += [(WB, HF * k, HF) for k in range(4)] + [(GA, 0, B)]
    early, after = 7, {1: 4, 2: 5, 3: 6}

    def piece(k, group):
        ref, start, size = chunks[k]
        if ref is GA:
            return ref.at[:, lanes(B * group, B)]
        return ref.at[at(B * group, B), pl.ds(start, size)]

    a_sem, f_sem, o_sem = ([take(size) for _ in chunks] for size in (Z - 1, 1, Z))
    b_sem, e_sem = take(Z - 1), take()

    def across_y(other):
        return y + other * (1 - 2 * y)

    def along(k, d, other=0):
        block = piece(k, 2 * z + across_y(other))
        return remote(block, block, z_dev(d), (b_sem if other else a_sem[k]) + d - 1)

    def over(k, d):
        block = piece(k, 2 * z_src(d) + y)
        return remote(block, block, peer, o_sem[k] + d)

    def relay(k, other=0):
        block, end = piece(k, 2 * z_src(2) + across_y(other)), lax.div(z, 2)
        sems = (e_sem, b_sem + 2 * end) if other else (f_sem[k], a_sem[k] + 2 * end)
        return remote(block, block, 3 * end * 8 + y * 4 + r, *sems)

    def near(k, d, action):
        if k == 8:
            action()
        else:
            nearby(d, action)

    def both(k):
        return (0, 1) if k == early else (0,)

    def ag_start(k):
        for other in both(k):
            for d in range(1, Z):
                near(k, d, along(k, d, other).start)

    def ag_own(k):
        over(k, 0).start()

    def ag_forward(k):
        first = lax.div(3 - z, 3)
        for i in range(1, Z):
            d = i if not relays or i == 2 else 1 + 2 * first if i == 1 else 3 - 2 * first
            for other in both(k):
                along(k, d, other).wait_recv()
                if relays and i == 2 and k < 8:
                    pl.when(inner)(relay(k, other).start)
            if k != early:
                over(k, d).start()
        if k in after:
            ag_own(after[k])
        if 2 <= k <= 4:
            ag_start(k + 3)

    def ag_finish(k):
        for d in range(Z):
            if k != early:
                over(k, d).wait_recv()

    def ag_drain(k):
        for d in range(1 if k == early else Z):
            over(k, d).wait_send()
        for other in both(k):
            for d in range(1, Z):
                near(k, d, along(k, d, other).wait_send)
            if relays and k < 8:
                pl.when(inner)(relay(k, other).wait_send)

    sendG = [remote(GQ.at[r], GQ.at[r], dev) for dev, q in quad]
    sendA = [remote(SA.at[q], WA.at[own], dev) for dev, q in quad]
    sendB = [remote(SB.at[q], WB.at[own], dev) for dev, q in quad]
    mine = idq.at[pl.ds(S * r, S)]
    sendI = [remote(mine, mine, dev) for dev, q in quad]
    for copy in sendG + sendA + sendI:
        go(copy)
    loads["wd"].wait()
    ag_own(2)
    ag_own(3)
    ag_start(2)
    for copy in sendG:
        copy.wait_recv()
    GA[:, lanes(B * g, B)] = (GQ[0] + GQ[1]) + (GQ[2] + GQ[3])
    ag_start(8)
    ag_own(8)
    for copy in sendA:
        copy.wait_recv()
    ag_start(0)
    ag_own(0)
    ag_start(1)
    ag_own(1)
    for name in ("wg", "wu"):
        loads[name].wait()
    for q in range(4):
        for j in range(G):
            half, within = divmod(B * j, HF)
            source = slice(B * (4 * j + q), B * (4 * j + q) + B)
            SB[q, :, half * FC + within : half * FC + within + B] = SG[0, :, source]
            SB[q, :, half * FC + HF + within : half * FC + HF + within + B] = SG[1, :, source]
    WB[own, :] = SB[r]
    for copy in sendB:
        go(copy)
    for copy in sendI:
        copy.wait_recv()

    lane = lax.broadcasted_iota(jnp.int32, (L, 128), 1)
    sub = lax.broadcasted_iota(jnp.int32, (L, 128), 0)
    front = lax.rem(lane, 64) < 32
    low = lane < 64
    freq = jnp.exp(-math.log(10000.0) * lax.rem(lane, 32).astype(F32) / 32)
    CT, ST = R["CT"], R["ST"]

    def tables(q):
        times = jnp.broadcast_to(idq[q, 2:3, :], (L, L)).T
        angles = times * freq
        CT[at(L * q, L), :] = jnp.cos(angles)
        sine = jnp.sin(angles)
        ST[at(L * q, L), :] = jnp.where(front, -sine, sine)

    loop(2 * S, tables)
    ag_forward(8)
    loop(2 * S, lambda q: tables(2 * S + q))
    loads["tok"].wait()
    ag_finish(8)
    step = 64

    def norm_in(i):
        x = tok[at(step * i, step), :].astype(F32)
        inv = lax.rsqrt(jnp.mean(x * x, axis=-1, keepdims=True) + EPSILON)
        h1Q[at(T * r + step * i, step), :] = (x * inv * GA[0:1, :]).astype(BF16)

    loop(T // step, norm_in)

    def token_block(ref):
        return lambda role: ref.at[at(T * role, T)]

    h1_start, h1_forward, h1_finish = quad_gather(token_block(h1Q))
    dy_start, dy_forward, dy_finish = quad_gather(token_block(dyQ))

    def att_block(chip, role):
        return attQ.at[at(2 * T * chip, 2 * T), lanes(QC * role, QC)]

    def att_copy(chip, role, device):
        return remote(att_block(chip, role), att_block(chip, role), device)

    needed, passed = att_copy(1 - xx, r, par), att_copy(xx, r_par, sib)
    near_needed, near_rest = att_copy(xx, r, sib), att_copy(1 - xx, r, sib)
    rest, passed_rest = att_copy(xx, r, par), att_copy(1 - xx, r_par, sib)
    wo_start, wo_forward, wo_finish = quad_gather(lambda role: WO.at[:, lanes(QC * role, QC)])
    h2_start, h2_forward, h2_finish = quad_gather(token_block(h2Q))
    h1_start()
    for copy in sendB:
        copy.wait_recv()
    ag_own(early)
    ag_forward(0)
    ag_start(3)
    h1_forward()
    ag_forward(1)
    ag_start(4)
    loads["cot"].wait()
    dy_start()
    h1_finish()
    ag_finish(0)
    ag_finish(1)
    ag_forward(2)

    qraw, kraw, qr, kr, vb, PR = (R[k] for k in ("qraw", "kraw", "qr", "kr", "vb", "PR"))
    spot = lax.broadcasted_iota(jnp.int32, (1, 128), 1)
    bias = [
        [jnp.sum(jnp.where(spot == QC // 64 * r + h, small[4 + m : 5 + m, :], 0.0)) for h in range(QC // 64)]
        for m in range(2)
    ]

    def swap(v):
        return jnp.where(front, pltpu.roll(v, 96, 1), pltpu.roll(v, 32, 1))

    def per_head(v):
        first = jnp.sum(jnp.where(low, v, 0.0), axis=-1, keepdims=True)
        second = jnp.sum(jnp.where(low, 0.0, v), axis=-1, keepdims=True)
        return jnp.where(low, first, second)

    def project_heads(q):
        at_q = at(L * q, L)
        value = mm(h1Q[at_q, :], WA[:, 0 : 3 * QC])
        cosine, sine = CT[at_q, :], ST[at_q, :]
        for m, (raw, ready) in enumerate(((qraw, qr), (kraw, kr))):
            raw[at_q, :] = value[:, QC * m : QC * (m + 1)]
            for j in range(QC // 128):
                v = value[:, QC * m + 128 * j : QC * m + 128 * (j + 1)]
                inv = lax.rsqrt(per_head(v * v) / 64 + EPSILON)
                v = v * inv * small[2 + m : 3 + m, :]
                v = v * cosine + swap(v) * sine
                if m == 0:
                    v = v * 0.125
                ready[at_q, 128 * j : 128 * (j + 1)] = v.astype(BF16)
        vb[at_q, :] = value[:, 2 * QC : 3 * QC].astype(BF16)

    loop(4 * S, project_heads)
    WO[:, lanes(QC * r, QC)] = WA[:, 3 * QC : 4 * QC]
    wo_start()
    dy_forward()

    def masks(q):
        segment = jnp.broadcast_to(idq[q, 0:1, :], (L, L))
        variate = jnp.broadcast_to(idq[q, 1:2, :], (L, L))
        allowed = (segment == segment.T) & ((segment != 0.0) | (lane == sub))
        return allowed, variate == variate.T

    heads = [jnp.where(low, 1.0, 0.0).astype(BF16), jnp.where(low, 0.0, 1.0).astype(BF16)]

    def attend(q):
        at_q = at(L * q, L)
        allowed, same = masks(q)
        for j in range(QC // 128):
            tile = slice(128 * j, 128 * (j + 1))
            q2, k2, v2 = qr[at_q, tile], kr[at_q, tile], vb[at_q, tile]
            outs = []
            for h in range(2):
                head = 2 * j + h
                score = mm(q2 * heads[h], k2, NT) + jnp.where(same, bias[1][head], bias[0][head])
                score = jnp.where(allowed, score, -1000000000.0)
                e = jnp.exp(score - jnp.max(score, axis=-1, keepdims=True))
                p = e / jnp.sum(e, axis=-1, keepdims=True)
                PR[q, head] = p
                outs.append(mm(p.astype(BF16), v2))
            attQ[at_q, lanes(QC * r + 128 * j, 128)] = jnp.where(low, outs[0], outs[1]).astype(BF16)

    def attend_pair(q):
        attend(q)
        attend(q + 1)

    loop(S, lambda i: attend_pair(2 * S * (1 - xx) + 2 * i))
    go(needed)
    ag_forward(3)
    loop(S, lambda i: attend_pair(2 * S * xx + 2 * i))
    go(near_needed)
    go(near_rest)
    ZR, FR = R["ZR"], R["FR"]
    if relays:
        for k, end in ((0, 0), (2, 3)):

            @pl.when(z == end)
            def _():
                FR[k] = jnp.zeros((2, B, HF), BF16)
                for unit in range(4):
                    ZR[unit, k] = jnp.zeros((B, FC), BF16)

    needed.wait_recv()
    go(passed)
    wo_forward()
    over(early, 0).wait_recv()
    ag_forward(4)
    wo_finish()
    near_needed.wait_recv()
    passed.wait_recv()

    x1, dx1, acc = R["x1"], R["dx1"], R["acc"]

    wide = 256

    def mix_sum(j):
        cols = lanes(wide * j, wide)
        x1[:, cols] = tok[:, cols].astype(F32) + mm(attQ[at(T * r, T), :], WO[:, cols])

    loop(D // wide, mix_sum)

    def mix(i):
        x = x1[at(step * i, step), :]
        inv = lax.rsqrt(jnp.mean(x * x, axis=-1, keepdims=True) + EPSILON)
        h2Q[at(T * r + step * i, step), :] = (x * inv * GA[1:2, :]).astype(BF16)

    loop(T // step, mix)
    h2_start()
    go(rest)
    ag_forward(5)
    dy_finish()
    ag_forward(6)
    ag_finish(2)
    ag_finish(3)
    h2_forward()
    ag_finish(4)
    ag_finish(5)

    hid, dgdu = R["hid"], R["dgdu"]

    def ffn(half, role):
        at_r = at(T * role, T)

        def body(j):
            to_gate = lanes(half * FC + wide * j, wide)
            to_up = lanes(half * FC + HF + wide * j, wide)
            gate, up = mm(h2Q[at_r, :], WB[:, to_gate]), mm(h2Q[at_r, :], WB[:, to_up])
            sigma = 1.0 / (1.0 + jnp.exp(-gate))
            silu = gate * sigma
            hid[at_r, lanes(half * HF + wide * j, wide)] = (silu * up).astype(BF16)
            d_hidden = mm(dyQ[at_r, :], WC[at(half * HF + wide * j, wide), :], NT)
            d_gate = d_hidden * up * (sigma * (1.0 + gate * (1.0 - sigma)))
            dgdu[at_r, to_gate] = d_gate.astype(BF16)
            dgdu[at_r, to_up] = (d_hidden * silu).astype(BF16)

        loop(HF // wide, body)

    ffn(0, r)
    ag_forward(7)
    h2_finish()
    rest.wait_recv()
    go(passed_rest)
    ffn(0, r_sib)
    ffn(0, r_par)
    ffn(0, r_dia)

    YS, YR, ZR, ZX, QS, QR = (R[k] for k in ("YS", "YR", "ZR", "ZX", "QS", "QR"))
    y_sem, z_sem, x_sem = ([take(size) for _ in range(4)] for size in (Z, Z - 1, 1))

    def gradient(unit, group, store):
        at_g = lanes(B * group, B)
        if unit == 0:
            store(slice(0, FC), mm(hid[:, at_g], dyQ[...], TN))
        elif unit == 1:
            store(slice(HF, FC), mm(h2Q[:, at_g], dgdu[:, HF:FC], TN))
        elif unit == 2:
            store(slice(0, FC), mm(h2Q[:, at_g], dgdu[:, FC : 2 * FC], TN))
        else:
            store(slice(0, 3 * QC), mm(h1Q[:, at_g], WC[:, 0 : 3 * QC], TN))
            store(slice(3 * QC, 4 * QC), mm(attQ[:, at_g], R["daR"][...], TN))

    slots = {1: 0, 2: 1, 0: 2, 3: 0}

    def part(unit, ref):
        return ref.at[:, pl.ds(HF, HF)] if unit == 1 else ref

    def y_copy(unit, i):
        return remote(part(unit, YS.at[slots[unit], i]), part(unit, YR.at[unit, i]), peer, y_sem[unit] + i)

    def z_copy(unit, d, i=0):
        return remote(part(unit, YR.at[unit, i]), part(unit, ZR.at[unit, d - 1]), z_dev(d), z_sem[unit] + d - 1)

    middle = (1 + lax.div(z, 2)) * 8 + y * 4 + r

    def x_copy(unit, i=0):
        return remote(part(unit, YR.at[unit, i]), part(unit, ZX.at[unit]), middle, x_sem[unit])

    def target(unit, i):
        if not relays:
            return lax.rem(z + 1 + i, Z)
        even = 1 - lax.rem(z, 2)
        if unit == 0:
            return i + even * (1 - 2 * (i % 2 if isinstance(i, int) else lax.rem(i, 2)))
        o = (2 * i) % 3 + 3 * (i // 3) if isinstance(i, int) else lax.rem(2 * i, 3) + 3 * lax.div(i, 3)
        return o + even * (3 - 2 * o)

    def own_place(unit):
        if not relays:
            return Z - 1
        return 1 + 2 * lax.div(z, 2) if unit == 0 else 3 - lax.div(z * (3 - z), 2)

    def rs_first(unit, begin=0, count=Z):
        if unit == 3:
            for i in range(Z):
                y_copy(1, i).wait_send()

        def body(i):
            place = begin + i

            def store(cols, value):
                YS[slots[unit], place, :, cols] = value.astype(BF16)

            gradient(unit, 2 * target(unit, place) + 1 - y, store)
            y_copy(unit, place).start()

        loop(count, body)

    def rs_step(unit, i):
        goal = target(unit, i)
        d = lax.rem(goal + Z - z, Z)
        y_copy(unit, i).wait_recv()

        def store(cols, value):
            YR[unit, i, :, cols] = (value + YR[unit, i, :, cols].astype(F32)).astype(BF16)

        gradient(unit, 2 * goal + y, store)
        if not relays:
            pl.when(d != 0)(lambda: z_copy(unit, d, i).start())
            return
        far = outer & (goal + z == 3)
        pl.when(far)(lambda: x_copy(unit, i).start())
        pl.when((d != 0) & jnp.logical_not(far | (inner & (d == 2))))(lambda: z_copy(unit, d, i).start())

    def rs_relay(unit):
        i = 5 - 2 * z if unit == 0 else 3
        if relays:

            @pl.when(inner)
            def _():
                x_copy(unit).wait_recv()
                cols = slice(HF if unit == 1 else 0, FC)
                YR[unit, i, :, cols] = (YR[unit, i, :, cols].astype(F32) + ZX[unit, :, cols].astype(F32)).astype(BF16)
                z_copy(unit, 2, i).start()

    def rs_second(unit, begin=0, count=Z):
        loop(count, lambda i: rs_step(unit, begin + i))

    FS, FR, FX, FT, FK = (R[k] for k in ("FS", "FR", "FX", "FT", "FK"))
    fz_sem, fx_sem = take(Z - 1), take()
    last_over = remote(FT.at[0], FT.at[1], peer)

    def zf_copy(d, i=0):
        return remote(FS.at[i], FR.at[d - 1], z_dev(d), fz_sem + d - 1)

    def zf_far(i=0):
        return remote(FS.at[i], FX, middle, fx_sem)

    def zf_first():
        def body(i):
            goal = target(1, i)
            d = lax.rem(goal + Z - z, Z)
            for side in range(2):
                FS[i, side] = mm(h2Q[:, lanes(B * (2 * goal + side), B)], dgdu[:, 0:HF], TN).astype(BF16)
            if not relays:
                pl.when(d != 0)(lambda: zf_copy(d, i).start())
                return
            far = outer & (goal + z == 3)
            pl.when(far)(lambda: zf_far(i).start())
            pl.when((d != 0) & jnp.logical_not(far | (inner & (d == 2))))(lambda: zf_copy(d, i).start())

        loop(Z, body)

    def zf_relay():
        if relays:

            @pl.when(inner)
            def _():
                zf_far().wait_recv()
                FS[3] = (FS[3].astype(F32) + FX[...].astype(F32)).astype(BF16)
                zf_copy(2, 3).start()

    def zf_second():
        for d in range(1, Z):
            if relays and d != 2:
                pl.when(z != (0 if d == 1 else Z - 1))(zf_copy(d).wait_recv)
            else:
                zf_copy(d).wait_recv()

        def total(side):
            value = FS[own_place(1), side].astype(F32)
            for d in range(1, Z):
                value = value + FR[d - 1, side].astype(F32)
            return value

        FT[0] = total(1 - y).astype(BF16)
        go(last_over)
        FK[...] = total(y)

    quad_copies = {}

    def rs_third(unit):
        for d in range(1, Z):
            if relays and d != 2:
                pl.when(z != (0 if d == 1 else Z - 1))(z_copy(unit, d).wait_recv)
            else:
                z_copy(unit, d).wait_recv()
        width = 256
        if unit == 1:
            last_over.wait_recv()
        for j in range(FC // width):
            cols = slice(width * j, width * (j + 1))
            if unit == 1 and width * j < HF:
                value = FK[:, cols] + FT[1, :, cols].astype(F32)
            else:
                value = YR[unit, own_place(unit), :, cols].astype(F32)
                for i in range(1, Z):
                    value = value + ZR[unit, i - 1, :, cols].astype(F32)
            if unit == 0:
                R["gd"][:, cols] = value
            else:
                QS[unit - 1, :, cols] = value.astype(BF16)
        if unit:
            QR[unit - 1, r] = QS[unit - 1, at(rows * r, rows), :]
            quad_copies[unit] = [
                go(remote(QS.at[unit - 1, at(rows * q, rows)], QR.at[unit - 1, r], dev)) for dev, q in quad
            ]

    def rs_last(unit):
        for copy in quad_copies[unit]:
            copy.wait_recv()
        R["parts"][unit - 1] = QR[unit - 1]

    rsS, rsR = R["rsS"], R["rsR"]

    def quad_sum(kind, prepare_block, partial, fill=None):
        copies = [
            remote(rsS.at[0], rsR.at[kind, 0], sib),
            remote(rsS.at[1], rsR.at[kind, 1], sib),
            remote(rsS.at[2], rsR.at[kind, 2], par),
        ]

        def blocks(role, store):
            def body(j):
                store(lanes(wide * j, wide), partial(at(T * role, T), wide * j))

            loop(D // wide, body)

        def to_dia(cols, value):
            rsS[1, :, cols] = value.astype(BF16)

        def to_par(cols, value):
            rsS[2, :, cols] = (value + rsR[kind, 1, :, cols].astype(F32)).astype(BF16)

        def to_sib(cols, value):
            rsS[0, :, cols] = value.astype(BF16)

        def keep(cols, value):
            acc[:, cols] = value

        prepare_block(r_dia)
        blocks(r_dia, to_dia)
        copies[1].start()
        prepare_block(r_par)
        copies[1].wait_recv()
        blocks(r_par, to_par)
        copies[2].start()
        if fill:
            fill(0)
        prepare_block(r_sib)
        blocks(r_sib, to_sib)
        copies[0].start()
        if fill:
            fill(1)
        prepare_block(r)
        blocks(r, keep)

        def finish():
            copies[0].wait_recv()
            copies[2].wait_recv()
            for copy in copies:
                copy.wait_send()

        return finish

    def summed(kind, at_i):
        return acc[at_i, :] + (rsR[kind, 0, at_i, :].astype(F32) + rsR[kind, 2, at_i, :].astype(F32))

    def nothing(role):
        return None

    zf_first()
    rs_first(1)
    rs_first(0, 0, Z // 2)
    ag_finish(6)
    ag_finish(7)
    h2_sum = quad_sum(
        0, functools.partial(ffn, 1), lambda at_r, j: mm(dgdu[at_r, :], WB[at(j, wide), :], NT),
        lambda i: (zf_relay() if i else None, rs_second(1, i, 1)),
    )
    rs_second(1, 2, 1)
    rs_first(2)
    h2_sum()

    TT, TR = R["TT"], R["TR"]
    daS, daR, dattS, dattR = (R[k] for k in ("daS", "daR", "dattS", "dattR"))
    TT[0] = jnp.zeros((8, D), F32)

    def norm_back(v, d_out, gain, row):
        inv = lax.rsqrt(jnp.mean(v * v, axis=-1, keepdims=True) + EPSILON)
        TT[0, row : row + 1, :] += jnp.sum(d_out * (v * inv), axis=0, keepdims=True)
        d = d_out * gain
        return inv * d - v * (inv * inv * inv * jnp.mean(d * v, axis=-1, keepdims=True))

    def mix_back(i):
        at_i = at(step * i, step)
        d = norm_back(x1[at_i, :], summed(0, at_i), GA[1:2, :], 1)
        d = d + dyQ[at(T * r + step * i, step), :].astype(F32)
        dx1[at_i, :] = d
        daS[at_i, :] = d.astype(BF16)

    loop(T // step, mix_back)
    sendD = [remote(daS.at[:, lanes(QC * q, QC)], daR.at[at(T * r, T)], dev) for dev, q in quad]
    sendT = [remote(dattS.at[:, lanes(QC * q, QC)], dattR.at[at(T * r, T)], dev) for dev, q in quad]

    def out_back(j):
        dattS[:, lanes(wide * j, wide)] = mm(daS[...], WO[at(wide * j, wide), :], NT).astype(BF16)

    loop(D // wide, out_back)
    for copy in sendT:
        go(copy)
    for copy in sendD:
        go(copy)
    dattR[at(T * r, T), :] = dattS[:, lanes(QC * r, QC)]
    daR[at(T * r, T), :] = daS[:, lanes(QC * r, QC)]
    rs_second(1, 3, 1)
    rs_first(0, Z // 2, Z // 2)
    zf_second()
    rs_relay(1)
    out_sum = quad_sum(1, nothing, lambda at_r, j: mm(hid[at_r, :], WC[:, lanes(j, wide)]))
    ag_drain(2)
    ag_drain(3)
    for copy in sendT:
        copy.wait_recv()

    def write_out(i):
        at_i = at(step * i, step)
        R["act"][at_i, :] = (x1[at_i, :] + summed(1, at_i)).astype(BF16)

    HG, BG = R["HG"], R["BG"]
    HG[...] = jnp.zeros(HG.shape, F32)
    BG[...] = jnp.zeros(BG.shape, F32)

    def fold(v):
        return jnp.sum(v.reshape(L // 8, 8, 128), axis=0)

    def prepare_back(raw, d, m, j, cosine, sine, factor):
        if factor != 1.0:
            d = d * factor
        d = d * cosine - swap(d) * sine
        inv = lax.rsqrt(per_head(raw * raw) / 64 + EPSILON)
        HG[m, j] += fold(d * (raw * inv))
        d = d * small[2 + m : 3 + m, :]
        return inv * d - raw * (inv * inv * inv * (per_head(d * raw) / 64))

    def attend_back(q):
        at_q = at(L * q, L)
        _, same = masks(q)
        cosine, sine = CT[at_q, :], ST[at_q, :]
        for j in range(QC // 128):
            tile = slice(128 * j, 128 * (j + 1))
            q2, k2, v2, d2 = qr[at_q, tile], kr[at_q, tile], vb[at_q, tile], dattR[at_q, tile]
            dq, dk, dv = [], [], []
            for h in range(2):
                p = PR[q, 2 * j + h]
                dp = mm(d2 * heads[h], v2, NT)
                ds = (p * (dp - jnp.sum(p * dp, axis=-1, keepdims=True))).astype(BF16)
                wide = ds.astype(F32)
                BG[0, 2 * j + h] += fold(jnp.where(same, 0.0, wide))
                BG[1, 2 * j + h] += fold(jnp.where(same, wide, 0.0))
                dv.append(mm(p.astype(BF16), d2, TN))
                dq.append(mm(ds, k2))
                dk.append(mm(ds, q2, TN))
            d_query = jnp.where(low, dq[0], dq[1])
            d_key = jnp.where(low, dk[0], dk[1])
            d_query = prepare_back(qraw[at_q, tile], d_query, 0, j, cosine, sine, 0.125)
            d_key = prepare_back(kraw[at_q, tile], d_key, 1, j, cosine, sine, 1.0)
            WC[at_q, tile] = d_query.astype(BF16)
            WC[at_q, QC + 128 * j : QC + 128 * (j + 1)] = d_key.astype(BF16)
            WC[at_q, 2 * QC + 128 * j : 2 * QC + 128 * (j + 1)] = jnp.where(low, dv[0], dv[1]).astype(BF16)

    def attend_and_step(i):
        for q in range(S):
            attend_back(S * i + q)
        rs_step(2, i)

    rs_second(0, 0, Z // 2)
    loop(4, attend_and_step)
    for copy in sendD + [near_rest, passed_rest]:
        copy.wait_recv()
    rs_first(3)
    rs_relay(2)
    out_sum()
    loop(T // step, write_out)
    in_sum = quad_sum(
        2, nothing, lambda at_r, j: mm(WC[at_r, 0 : 3 * QC], WA[at(j, wide), 0 : 3 * QC], NT),
        lambda i: rs_second(0, Z // 2 + i, 1),
    )
    rs_relay(0)
    for k in range(len(chunks)):
        if k not in (2, 3):
            ag_drain(k)
    rs_third(1)
    in_sum()

    def input_back(i):
        at_i = at(step * i, step)
        d = norm_back(tok[at_i, :].astype(F32), summed(2, at_i), GA[0:1, :], 0)
        R["ig"][at_i, :] = (dx1[at_i, :] + d).astype(BF16)

    loop(T // step, input_back)

    for m in range(2):
        value = HG[m, 0]
        for j in range(1, QC // 128):
            value = value + HG[m, j]
        TT[0, 2:3, 128 * m : 128 * (m + 1)] = jnp.sum(value, axis=0, keepdims=True)
    for m in range(2):
        line = jnp.zeros((1, 128), F32)
        for h in range(QC // 64):
            line = line + jnp.where(spot == QC // 64 * r + h, jnp.sum(BG[m, h]), 0.0)
        TT[0, 3 + m : 4 + m, 0:128] = line
    t1, t2, t3, t_finish = tile_sum(TT, TR)
    t1()
    rs_second(3, 0, 2)
    t2()
    rs_second(3, 2, 1)
    rs_second(3, 3, 1)
    rs_relay(3)
    rs_third(2)
    rs_last(1)
    t3()
    rs_third(0)
    rs_third(3)
    rs_last(2)
    R["tot"][...] = t_finish()
    rs_last(3)
    for copy in sent:
        copy.wait_send()
    for d in range(1, Z):
        nearby(d, zf_copy(d).wait_send)
    if relays:
        pl.when(outer)(zf_far().wait_send)
    for unit in range(4):
        for i in range(Z):
            if unit != 1:
                y_copy(unit, i).wait_send()
            if i:
                nearby(i, z_copy(unit, i).wait_send)
        if relays:
            pl.when(outer)(x_copy(unit).wait_send)


LAST = ("act", "ig", "gq", "gk", "gv", "go", "gg", "gu", "gd", "ga", "gf", "ghq", "ghk", "gb")


def finishing(s, *refs):
    names = tuple(name + "_in" for name in OUTPUTS) + LAST
    R = dict(zip(names, refs, strict=True))
    D, rows, G, QC, FC, B, HD, H = (s[k] for k in ("D", "rows", "G", "QC", "FC", "B", "HD", "H"))
    HF = FC // 2
    for name in ("act", "ig", "gd"):
        R[name][...] = R[name + "_in"][...]
    parts = R["parts_in"]
    for q in range(4):
        for m, name in enumerate(("gq", "gk", "gv", "go")):
            R[name][:, QC * q : QC * (q + 1)] = parts[2, q, :, QC * m : QC * (m + 1)].astype(F32)
        for j in range(G):
            half, within = divmod(B * j, HF)
            target = slice(B * (4 * j + q), B * (4 * j + q) + B)
            R["gg"][:, target] = parts[half, q, :, within : within + B].astype(F32)
            R["gu"][:, target] = parts[half, q, :, HF + within : HF + within + B].astype(F32)
    tot = R["tot_in"]
    own = lax.axis_index("fsdp") * rows
    mine = pltpu.roll(tot[:, lanes(128 * lax.div(own, 128), 128)], lax.rem(128 - lax.rem(own, 128), 128), 1)
    R["ga"][...] = mine[0:1, 0:rows]
    R["gf"][...] = mine[1:2, 0:rows]
    both = tot[:, 0:256]
    both = both + pltpu.roll(both, 256 - HD, 1)
    R["ghq"][...] = both[2:3, 0:HD]
    R["ghk"][...] = both[2:3, 128 : 128 + HD]
    R["gb"][...] = tot[3:5, 0:H]


def layer(s, tokens, segment_ids, variate_ids, time_ids, w_query, w_key, w_value, w_out, w_gate, w_up, w_down,
          gain_attn, gain_ffn, gain_query, gain_key, variate_bias, cotangent):
    D, T, rows, B, FF, FC, HD, H = (s[k] for k in ("D", "T", "rows", "B", "FF", "FC", "HD", "H"))
    lines = [
        gain_attn[None], gain_ffn[None], jnp.tile(gain_query[None], (1, 2)), jnp.tile(gain_key[None], (1, 2)),
        variate_bias,
    ]
    small, line = jnp.zeros((8, 128), F32), 0
    for piece in lines:
        high, wide = piece.shape
        small = small + jnp.pad(piece.astype(F32), ((line, 8 - line - high), (0, 128 - wide)))
        line += high
    scratch = scratch_of(s)
    names = INPUTS + OUTPUTS + tuple(scratch)
    vmem, anywhere = pl.BlockSpec(memory_space=pltpu.VMEM), pl.BlockSpec(memory_space=pl.ANY)
    here = {"seg", "var", "tim", "small"}

    def shape(*dims, kind=F32):
        return jax.ShapeDtypeStruct(dims, kind)

    tokens_shape = shape(T, D, kind=BF16)
    outs = pl.pallas_call(
        functools.partial(fused, s, names),
        out_shape=[tokens_shape, tokens_shape, shape(B, D), shape(3, 4, rows, FC, kind=BF16), shape(8, D)],
        in_specs=[vmem if name in here else anywhere for name in INPUTS],
        out_specs=[vmem] * len(OUTPUTS),
        scratch_shapes=list(scratch.values()),
        compiler_params=pltpu.CompilerParams(
            collective_id=0, has_side_effects=True, vmem_limit_bytes=64 << 20
        ),
        name="fused_layer",
    )(
        tokens.reshape(T, D), cotangent.reshape(T, D), segment_ids, variate_ids, time_ids,
        w_query, w_key, w_value, w_out, w_gate, w_up, w_down, small,
    )
    last = pl.pallas_call(
        functools.partial(finishing, s),
        out_shape=[tokens_shape, tokens_shape] + [shape(rows, D)] * 4 + [shape(rows, FF)] * 2
        + [shape(B, D), shape(1, rows), shape(1, rows), shape(1, HD), shape(1, HD), shape(2, H)],
        in_specs=[vmem] * len(OUTPUTS),
        out_specs=[vmem] * len(LAST),
        name="finishing",
    )(*outs)
    flat = [value.reshape(-1) for value in last[9:13]]
    return (last[0].reshape(tokens.shape), last[1].reshape(tokens.shape), *last[2:9], *flat, last[13])


def local(tokens, segment_ids, variate_ids, time_ids, *rest):
    s = sizes_of(lax.axis_size("fsdp"), tokens, rest[0], rest[4], rest[9], rest[11])
    chosen = functools.partial(layer, s) if fits(s) else plain
    return chosen(tokens, segment_ids, variate_ids, time_ids, *rest)


def solution(mesh):
    placed = (
        P("fsdp", None, None),
        P("fsdp", None),
        P("fsdp", None),
        P("fsdp", None),
        P("fsdp", None),
        P("fsdp", None),
        P("fsdp", None),
        P("fsdp", None),
        P("fsdp", None),
        P("fsdp", None),
        P("fsdp", None),
        P("fsdp"),
        P("fsdp"),
        P(),
        P(),
        P(),
        P("fsdp", None, None),
    )
    return jax.shard_map(
        local,
        mesh=mesh,
        in_specs=placed,
        out_specs=(
            P("fsdp", None, None),
            P("fsdp", None, None),
            P("fsdp", None),
            P("fsdp", None),
            P("fsdp", None),
            P("fsdp", None),
            P("fsdp", None),
            P("fsdp", None),
            P("fsdp", None),
            P("fsdp"),
            P("fsdp"),
            P(),
            P(),
            P(),
        ),
        check_vma=False,
    )
```
